128 devices in a mesh: row: 16 (over x_hi, y, core), vec: 8 (over z, x_lo).
Axes of the slice: x: 4 (x_hi: 2, x_lo: 2; x = x_hi * 2 + x_lo), y: 4, z: 4, core: 2. Of those that a mesh axis runs over, the one named last changes fastest.
Arguments:
- eigvecs: float32 [32768, 8192], P('row', 'vec'), may hold values from -6 to 6
- wy_v: float32 [2, 256, 256, 128], P(None, ('row', 'vec')), as said below
- wy_t: float32 [2, 256, 128, 128], P(None, ('row', 'vec')), as said below
Outputs:
- back_vectors: float32 [32768, 8192], P('row', 'vec')
The draws below stay inside these ranges and needn't reach their ends.
Inputs may be any that keep to these rules, and one draw needn't show every extreme that they name: Each block wy_v[g, k] is unit lower trapezoidal: ones on its diagonal, zeros above it. wy_t[g, k] is upper triangular and makes I - wy_v[g, k] wy_t[g, k] wy_v[g, k]^T the product, in order, of the 128 reflectors I - tau_i v_i v_i^T of its columns v_i, with tau_i = 2 / (v_i^T v_i).
All inputs are finite; a program needn't handle non-finite values.
Results may differ from the reference program's by a relative error of at most 0.0003.
Values sent between devices are 32-bit elements; how exact they have to be, the bound alone decides.
No kernel may reach another device: no remote copies, remote signals or barrier semaphores. Data moves between devices by JAX's collectives and lax.ppermute only.
A program may use at most 128 MiB of HBM per device.

```python
import math
import jax
import jax.numpy as jnp
from jax import lax

BW = 128
GROUPS = 2
NBLK = 256
ROWS = 32768
COLS = 8192


def reflector_block(key):
    entries = jax.random.normal(key, (GROUPS, NBLK, 2 * BW, BW), jnp.float32) / math.sqrt(BW)
    row_ids = lax.broadcasted_iota(jnp.int32, (2 * BW, BW), 0)
    col_ids = lax.broadcasted_iota(jnp.int32, (2 * BW, BW), 1)
    return jnp.where(row_ids > col_ids, entries, jnp.where(row_ids == col_ids, 1.0, 0.0))


def triangular_factor(reflector):
    edge_offsets = jnp.dot(reflector.T, reflector, precision=lax.Precision.HIGHEST)
    scale_factors = 2.0 / jnp.diagonal(edge_offsets)
    slot_positions = jnp.arange(BW)

    def build_column(slot_position, reflector_factor):
        masked_values = jnp.where(slot_positions < slot_position, edge_offsets[:, slot_position], 0.0)
        column_entries = -scale_factors[slot_position] * jnp.dot(reflector_factor, masked_values, precision=lax.Precision.HIGHEST)
        column_entries = jnp.where(slot_positions == slot_position, scale_factors[slot_position], column_entries)
        return reflector_factor.at[:, slot_position].set(column_entries)
    return lax.fori_loop(0, BW, build_column, jnp.zeros((BW, BW), jnp.float32))


def draw_wy_v(key, part):
    return reflector_block(key)


def draw_wy_t(key, part):
    reflector = reflector_block(key)
    stacked = reflector.reshape(GROUPS * NBLK, 2 * BW, BW)
    return jax.vmap(triangular_factor)(stacked).reshape(GROUPS, NBLK, BW, BW)


def block_levels(stream_key, extent, shards, low, top_value):
    loudness, own = 1.0, jax.random.fold_in(stream_key, 6)
    for position, blocks in shards:
        heights = jnp.exp(jax.random.uniform(jax.random.fold_in(own, position), (blocks,), jnp.float32, low / len(shards), top_value / len(shards)))
        loudness = loudness * jnp.repeat(heights, extent[position] // blocks).reshape([-1 if axis == position else 1 for axis in range(len(extent))])
    return loudness


def centred(rng, shape, deviation, most, pieces=(), kind=jnp.bfloat16):
    result = jax.random.normal(rng, shape, jnp.float32) * deviation
    if len(pieces) > 0:
        result = block_levels(rng, shape, pieces, -0.22, 0.18) * result
    return jnp.clip(result, min=-most, max=most).astype(kind)


def setup_inputs(seed: int = 0) -> dict:
    keys = jax.random.split(jax.random.key(seed), 4)
    eigvecs = centred(keys[0], (ROWS, COLS), 1.0, 6.0, ((0, 16), (1, 8)), jnp.float32)
    wy_v = draw_wy_v(jax.random.fold_in(keys[3], 71), 0)
    wy_t = draw_wy_t(jax.random.fold_in(keys[3], 71), 0)
    return dict(eigvecs=eigvecs, wy_v=wy_v, wy_t=wy_t)


def apply_group(padded, reflectors, factors, band_width):
    def apply_one(block_index, working):
        start = (block_index * band_width).astype(jnp.int32)
        window_rows = lax.dynamic_slice_in_dim(working, start, 2 * band_width, 0)
        projected = lax.dot_general(reflectors[block_index], window_rows, (((0,), (0,)), ((), ())), precision=lax.Precision.HIGHEST, preferred_element_type=jnp.float32)
        weights = jnp.dot(factors[block_index], projected, precision=lax.Precision.HIGHEST, preferred_element_type=jnp.float32)
        correction = jnp.dot(reflectors[block_index], weights, precision=lax.Precision.HIGHEST, preferred_element_type=jnp.float32)
        return lax.dynamic_update_slice_in_dim(working, window_rows - correction, start, 0)
    return lax.fori_loop(0, reflectors.shape[0], apply_one, padded)


def reference(eigvecs, wy_v, wy_t):
    current = eigvecs
    for group_index in range(GROUPS):
        padded = jnp.concatenate([jnp.zeros((BW, eigvecs.shape[1]), jnp.float32), current], axis=0)
        padded = apply_group(padded, wy_v[group_index], wy_t[group_index], BW)
        current = padded[BW:]
    return current
```

```python
import jax
import jax.numpy as jnp
from jax import lax
from jax.experimental import pallas as pl
from jax.experimental.pallas import tpu as pltpu
from jax.sharding import PartitionSpec as P

F32 = jnp.float32
BF16 = jnp.bfloat16
Z_SIZE = 4
Y_SIZE = 4
HIGHEST = lax.Precision.HIGHEST


def dot(a, b, precision=None):
    return jnp.dot(a, b, precision=precision, preferred_element_type=F32)


def split(value):
    high = value.astype(BF16)
    return high, (value - high.astype(F32)).astype(BF16)


def dot3(a, b):
    a_high, a_low = split(a)
    b_high, b_low = split(b)
    return dot(a_high, b_high) + (dot(a_low, b_high) + dot(a_high, b_low))


def along_z(value, by):
    pairs = [(v, ((v // 2 + by) % Z_SIZE) * 2 + v % 2) for v in range(2 * Z_SIZE)]
    return lax.ppermute(value, "vec", pairs)


def across_x(value):
    return lax.ppermute(value, "vec", [(v, v ^ 1) for v in range(2 * Z_SIZE)])


def across_core(value):
    return lax.ppermute(value, "row", [(i, i ^ 1) for i in range(lax.axis_size("row"))])


def along_y(value, by):
    def target(i):
        high, y, core = i // (2 * Y_SIZE), (i // 2) % Y_SIZE, i % 2
        return (high * Y_SIZE + (y + by) % Y_SIZE) * 2 + core

    return lax.ppermute(value, "row", [(i, target(i)) for i in range(lax.axis_size("row"))])


def from_next_row(value):
    return lax.ppermute(value, "row", [(i + 1, i) for i in range(lax.axis_size("row") - 1)])


def gather_groups(packed):
    first, second = {(0, 0): packed[0]}, {(0, 0): packed[1]}
    first[0, 1] = across_x(first[0, 0])
    first[3, 0] = along_z(first[0, 0], 1)
    first[1, 0] = along_z(first[0, 0], -1)
    first[3, 1] = across_x(first[3, 0])
    first[2, 0] = along_z(first[3, 0], 1)
    first[1, 1] = along_z(first[0, 1], -1)
    own, _ = lax.optimization_barrier((second[0, 0], first[3, 1]))
    first[2, 1] = across_x(first[2, 0])
    second[3, 0] = along_z(own, 1)
    second[1, 0] = along_z(own, -1)
    own, _ = lax.optimization_barrier((own, first[2, 1]))
    second[0, 1] = across_x(own)
    second[2, 0] = along_z(second[3, 0], 1)
    second[3, 1] = along_z(second[0, 1], 1)
    second[1, 1] = along_z(second[0, 1], -1)
    second[2, 1] = across_x(second[2, 0])
    keys = [(dz, dx) for dz in range(Z_SIZE) for dx in range(2)]
    return [first[key] for key in keys], [second[key] for key in keys]


def place_of(index):
    vec = lax.axis_index("vec")
    z, x = vec // 2, vec % 2
    dz, dx = index // 2, index % 2
    return lax.rem(z + dz, Z_SIZE) * 2 + lax.rem(x + dx, 2)


def pick_kernel(*refs):
    pieces, out, sem = refs[:-2], refs[-2], refs[-1]
    for index, piece in enumerate(pieces):

        @pl.when(place_of(index) == 0)
        def _():
            copy = pltpu.make_async_copy(piece, out, sem)
            copy.start()
            copy.wait()


def pick_first(pieces):
    return pl.pallas_call(
        pick_kernel,
        out_shape=jax.ShapeDtypeStruct(pieces[0].shape, F32),
        in_specs=[pl.BlockSpec(memory_space=pl.ANY)] * len(pieces),
        out_specs=pl.BlockSpec(memory_space=pl.ANY),
        scratch_shapes=[pltpu.SemaphoreType.DMA],
    )(*pieces)


def build_reflection(packed):
    width = packed.shape[1]
    rows = lax.broadcasted_iota(jnp.int32, (width, width), 0)
    cols = lax.broadcasted_iota(jnp.int32, (width, width), 1)
    top = packed[:width]
    unit = jnp.where(rows == cols, 1.0, jnp.where(rows > cols, top, 0.0))
    factor = jnp.where(rows <= cols, top, 0.0)
    vectors = jnp.concatenate([unit, packed[width:]], axis=0)
    weighted = dot(vectors, factor, HIGHEST)
    update = lax.dot_general(
        weighted, vectors, (((1,), (1,)), ((), ())), precision=HIGHEST, preferred_element_type=F32
    )
    rows = lax.broadcasted_iota(jnp.int32, update.shape, 0)
    cols = lax.broadcasted_iota(jnp.int32, update.shape, 1)
    high, low = split(jnp.where(rows == cols, 1.0, 0.0) - update)
    return jnp.concatenate([high, low], axis=0)


def sweep(pieces, extra, block_count, prologue, data, tail, unit_in, width, unit_cols):
    piece_count = len(pieces)
    data_cols = data.shape[1]
    total_cols = data_cols + unit_cols
    out_blocks = block_count - 1
    last_data = data.shape[0] // width - 1
    has_tail = tail is not None

    def kernel(*refs):
        ins = list(refs[: piece_count + 1])
        at = piece_count + 1
        data_ref = refs[at]
        other_ref = refs[at + 1]
        out, unit_out, state_out, blocks, reflections, sems = refs[at + 2 :]
        body(
            piece_count, block_count, prologue, width, has_tail,
            ins[:piece_count], ins[piece_count], data_ref, other_ref,
            out, unit_out, state_out, blocks, reflections, sems,
        )

    if has_tail:
        other = tail
        other_spec = pl.BlockSpec((width, data_cols), lambda k: (jnp.clip(k - last_data - 1, 0, 1), 0))
    else:
        other = unit_in
        other_spec = pl.BlockSpec((width, unit_in.shape[1]), lambda k: (k, 0))
    any_spec = pl.BlockSpec(memory_space=pl.ANY)
    flops = 2 * block_count * (2 * width) ** 2 * (total_cols * 3 + 2 * width * 6)
    return pl.pallas_call(
        kernel,
        grid=(block_count,),
        out_shape=(
            jax.ShapeDtypeStruct((out_blocks * width, data_cols), F32),
            jax.ShapeDtypeStruct((out_blocks * width, unit_cols), F32),
            jax.ShapeDtypeStruct((width, total_cols), F32),
        ),
        in_specs=[any_spec] * (piece_count + 1)
        + [pl.BlockSpec((width, data_cols), lambda k: (jnp.minimum(k, last_data), 0)), other_spec],
        out_specs=(
            pl.BlockSpec((width, data_cols), lambda k: (jnp.maximum(k - 1, 0), 0)),
            pl.BlockSpec((width, unit_cols), lambda k: (jnp.maximum(k - 1, 0), 0)),
            pl.BlockSpec((width, total_cols), lambda k: (0, 0)),
        ),
        scratch_shapes=[
            pltpu.VMEM((block_count, 2 * width, width), F32),
            pltpu.VMEM((2, 4 * width, 2 * width), BF16),
            pltpu.SemaphoreType.DMA((piece_count + 1,)),
        ],
        compiler_params=pltpu.CompilerParams(vmem_limit_bytes=40 * 2**20),
        cost_estimate=pl.CostEstimate(flops=flops, bytes_accessed=2 * 4 * data.size, transcendentals=0),
    )(*pieces, extra, data, other)


def body(
    piece_count, block_count, prologue, width, has_tail,
    pieces, extra, data, other, out, unit_out, state, blocks, reflections, sems,
):
    step = pl.program_id(0)
    is_first = lax.axis_index("row") == 0
    data_cols = data.shape[1]
    total_cols = state.shape[1]
    main_blocks = 2 * piece_count

    @pl.when(step == 0)
    def _():
        copies = []
        for index, piece in enumerate(pieces):
            place = place_of(index)
            copies.append(pltpu.make_async_copy(piece, blocks.at[pl.ds(2 * place, 2)], sems.at[index]))
        left = block_count - main_blocks
        copies.append(
            pltpu.make_async_copy(
                extra.at[pl.ds(0, left)], blocks.at[pl.ds(main_blocks, left)], sems.at[piece_count]
            )
        )
        for copy in copies:
            copy.start()
        for copy in copies:
            copy.wait()
        state[...] = jnp.zeros_like(state)
        reflections[0] = build_reflection(blocks[0])

    @pl.when(step == prologue)
    def _():
        @pl.when(jnp.logical_not(is_first))
        def _():
            state[:, :data_cols] = jnp.zeros((width, data_cols), F32)

        rows = lax.broadcasted_iota(jnp.int32, (width, width), 0)
        cols = lax.broadcasted_iota(jnp.int32, (width, width), 1)
        if total_cols - width > data_cols:
            state[:, data_cols : total_cols - width] = jnp.zeros((width, total_cols - width - data_cols), F32)
        state[:, total_cols - width :] = jnp.where(rows == cols, 1.0, 0.0)

    current = lax.rem(step, 2)
    reflection = reflections[current]
    upcoming = build_reflection(blocks[jnp.minimum(step + 1, block_count - 1)])
    for start in range(0, total_cols, 2 * width):
        size = min(2 * width, total_cols - start)
        if start < data_cols:
            lower = data[:, start : start + size]
            if has_tail:
                lower = jnp.where(step >= main_blocks, other[:, start : start + size], lower)
        elif has_tail:
            lower = jnp.zeros((width, size), F32)
        else:
            lower = jnp.concatenate([other[...], jnp.zeros((width, size - other.shape[1]), F32)], axis=1)
            lower = jnp.where(step >= prologue, lower, 0.0)
        high, low = split(jnp.concatenate([state[:, start : start + size], lower], axis=0))
        both = dot(reflection, high)
        cross = dot(reflection[: 2 * width], low)
        result = both[: 2 * width] + (both[2 * width :] + cross)
        if start < data_cols:
            out[:, start : start + size] = result[:width]
        else:
            unit_out[:, start - data_cols : start - data_cols + size] = result[:width]
        state[:, start : start + size] = result[width:]
    reflections[1 - current] = upcoming


def correct_kernel(rows_ref, response_ref, incoming_ref, out_ref, high_ref, low_ref):
    @pl.when(pl.program_id(0) == 0)
    def _():
        high, low = split(incoming_ref[...])
        high_ref[...] = high
        low_ref[...] = low

    high, low = split(response_ref[...])
    out_ref[...] = rows_ref[...] + (
        dot(high, high_ref[...]) + (dot(low, high_ref[...]) + dot(high, low_ref[...]))
    )


def correct(rows, response, incoming, tile=256):
    count, cols = rows.shape
    depth = response.shape[1]
    return pl.pallas_call(
        correct_kernel,
        grid=(count // tile,),
        out_shape=jax.ShapeDtypeStruct(rows.shape, F32),
        in_specs=[
            pl.BlockSpec((tile, cols), lambda k: (k, 0)),
            pl.BlockSpec((tile, depth), lambda k: (k, 0)),
            pl.BlockSpec((depth, cols), lambda k: (0, 0)),
        ],
        out_specs=pl.BlockSpec((tile, cols), lambda k: (k, 0)),
        scratch_shapes=[pltpu.VMEM((depth, cols), BF16), pltpu.VMEM((depth, cols), BF16)],
        compiler_params=pltpu.CompilerParams(vmem_limit_bytes=40 * 2**20),
    )(rows, response, incoming)


def incoming_state(transition, offset):
    row = lax.axis_index("row")
    core, y = row % 2, (row // 2) % Y_SIZE
    half = offset.shape[1] // 2
    quarter = half // Y_SIZE
    own_half = lax.dynamic_slice_in_dim(offset, core * half, half, 1)
    sent_half = lax.dynamic_slice_in_dim(offset, (1 - core) * half, half, 1)
    received = across_core(jnp.concatenate([transition, sent_half], axis=1))
    depth = transition.shape[1]
    own = jnp.concatenate([transition, own_half], axis=1)
    lower = jnp.where(core == 0, own, received)
    upper = jnp.where(core == 0, received, own)
    chip = dot(upper[:, :depth], lower, HIGHEST)
    chip_transition = chip[:, :depth]
    chip_offset = chip[:, depth:] + upper[:, depth:]

    def with_quarter(index):
        return jnp.concatenate(
            [chip_transition, lax.dynamic_slice_in_dim(chip_offset, index * quarter, quarter, 1)], axis=1
        )

    relative = [with_quarter(y)] + [along_y(with_quarter((y + d) % Y_SIZE), d) for d in range(1, Y_SIZE)]
    stacked = jnp.stack(relative)
    chips = [lax.dynamic_index_in_dim(stacked, (y - at) % Y_SIZE, 0, False) for at in range(Y_SIZE)]
    states = [chips[0][:, depth:]]
    for at in range(1, Y_SIZE):
        states.append(dot(chips[at][:, :depth], states[-1], HIGHEST) + chips[at][:, depth:])
    size = lax.axis_size("row")
    entering = lax.ppermute(states[-1], "row", [(i, i + size // 2) for i in range(size // 2)])
    result = [entering]
    for at in range(Y_SIZE - 1):
        result.append(dot(chips[at][:, :depth], result[-1], HIGHEST) + chips[at][:, depth:])
    result = jnp.stack(result)
    back = [lax.dynamic_index_in_dim(result, (y + d) % Y_SIZE, 0, False) for d in range(Y_SIZE)]
    arrived = jnp.stack([back[0]] + [along_y(back[d], d) for d in range(1, Y_SIZE)])
    into_chip = jnp.concatenate(
        [lax.dynamic_index_in_dim(arrived, (y - at) % Y_SIZE, 0, False) for at in range(Y_SIZE)], axis=1
    )
    into_second = dot(lower[:, :depth], into_chip, HIGHEST) + lower[:, depth:]
    kept = jnp.where(core == 0, into_chip, into_second)
    given = jnp.where(core == 0, into_second, into_chip)
    other = across_core(given)
    return jnp.where(
        core == 0, jnp.concatenate([kept, other], axis=1), jnp.concatenate([other, kept], axis=1)
    )


def local(eigvecs, wy_v, wy_t):
    width = wy_t.shape[-1]
    rows_dev, cols_dev = eigvecs.shape
    own_blocks = rows_dev // width
    below = lax.broadcasted_iota(jnp.int32, (width, width), 0) > lax.broadcasted_iota(
        jnp.int32, (width, width), 1
    )
    packed = jnp.concatenate(
        [jnp.where(below, wy_v[:, :, :width], wy_t), wy_v[:, :, width:]], axis=2
    )
    tail = from_next_row(eigvecs[: 2 * width])
    first, second = gather_groups(packed)
    first_extra = from_next_row(pick_first(first))
    second_extra = from_next_row(pick_first(second))
    middle, middle_unit, first_state = sweep(
        first, first_extra, own_blocks + 2, 2, eigvecs, tail, None, width, width
    )
    rows, response, second_state = sweep(
        second, second_extra, own_blocks + 1, 1, middle, None, middle_unit, width, 2 * width
    )
    unit = first_state[:, cols_dev:]
    transition = jnp.concatenate(
        [jnp.concatenate([unit, jnp.zeros_like(unit)], axis=1), second_state[:, cols_dev:]], axis=0
    )
    offset = jnp.concatenate([first_state[:, :cols_dev], second_state[:, :cols_dev]], axis=0)
    incoming = incoming_state(transition, offset)
    return correct(rows, response, incoming)


def solution(mesh):
    placed = (
        P("row", "vec"),
        P(None, ("row", "vec"), None, None),
        P(None, ("row", "vec"), None, None),
    )
    return jax.shard_map(
        local, mesh=mesh, in_specs=placed, out_specs=P("row", "vec"), check_vma=False
    )
```

```python
import functools

import jax
import jax.numpy as jnp
from jax import lax
from jax.experimental import pallas as pl
from jax.experimental.pallas import tpu as pltpu
from jax.sharding import PartitionSpec as P

F32 = jnp.float32
BF16 = jnp.bfloat16
Z_SIZE = 4
Y_SIZE = 4
HIGHEST = lax.Precision.HIGHEST
VMEM_BYTES = 56 * 2**20


def dot(a, b, precision=None):
    return jnp.dot(a, b, precision=precision, preferred_element_type=F32)


def dot_transposed(a, b):
    return lax.dot_general(a, b, (((1,), (1,)), ((), ())), preferred_element_type=F32)


def split(value):
    high = value.astype(BF16)
    return high, (value - high.astype(F32)).astype(BF16)


def along_z(value, by):
    pairs = [(v, ((v // 2 + by) % Z_SIZE) * 2 + v % 2) for v in range(2 * Z_SIZE)]
    return lax.ppermute(value, "vec", pairs)


def across_x(value):
    return lax.ppermute(value, "vec", [(v, v ^ 1) for v in range(2 * Z_SIZE)])


def across_core(value):
    return lax.ppermute(value, "row", [(i, i ^ 1) for i in range(lax.axis_size("row"))])


def along_y(value, by):
    def target(i):
        high, y, core = i // (2 * Y_SIZE), (i // 2) % Y_SIZE, i % 2
        return (high * Y_SIZE + (y + by) % Y_SIZE) * 2 + core

    return lax.ppermute(value, "row", [(i, target(i)) for i in range(lax.axis_size("row"))])


def from_next_row(value):
    return lax.ppermute(value, "row", [(i + 1, i) for i in range(lax.axis_size("row") - 1)])


def together(*values):
    return lax.optimization_barrier(values)


def place_of(index):
    vec = lax.axis_index("vec")
    z, x = vec // 2, vec % 2
    dz, dx = index // 2, index % 2
    return lax.rem(z + dz, Z_SIZE) * 2 + lax.rem(x + dx, 2)


def pick_kernel(keys, *refs):
    pieces, out, sems = refs[:-2], refs[-2], refs[-1]
    for (dz, dx), piece in zip(keys, pieces):

        @pl.when(place_of(2 * dz + dx) == 0)
        def _():
            copies = [
                pltpu.make_async_copy(piece.at[0], out.at[pl.ds(0, 2)], sems.at[0]),
                pltpu.make_async_copy(piece.at[1, pl.ds(0, 1)], out.at[pl.ds(2, 1)], sems.at[1]),
            ]
            for copy in copies:
                copy.start()
            for copy in copies:
                copy.wait()


def pick_first(pieces):
    keys = list(pieces)
    return pl.pallas_call(
        functools.partial(pick_kernel, keys),
        out_shape=jax.ShapeDtypeStruct((3,) + pieces[keys[0]].shape[2:], F32),
        in_specs=[pl.BlockSpec(memory_space=pl.ANY)] * len(keys),
        out_specs=pl.BlockSpec(memory_space=pltpu.VMEM),
        scratch_shapes=[pltpu.SemaphoreType.DMA((2,))],
        compiler_params=pltpu.CompilerParams(vmem_limit_bytes=VMEM_BYTES),
    )(*[pieces[key] for key in keys])


def build_reflection(packed):
    width = packed.shape[1]
    rows = lax.broadcasted_iota(jnp.int32, (width, width), 0)
    cols = lax.broadcasted_iota(jnp.int32, (width, width), 1)
    top = packed[:width]
    unit = jnp.where(rows == cols, 1.0, jnp.where(rows > cols, top, 0.0))
    factor = jnp.where(rows <= cols, top, 0.0)
    vectors = jnp.concatenate([unit, packed[width:]], axis=0)
    high, low = split(vectors)
    factor_high, factor_low = split(factor)
    both = dot(jnp.concatenate([high, low], axis=0), factor_high)
    weighted_high, weighted_low = split(
        both[: 2 * width] + (both[2 * width :] + dot(high, factor_low))
    )
    both = dot_transposed(jnp.concatenate([weighted_high, weighted_low], axis=0), high)
    update = both[: 2 * width] + (both[2 * width :] + dot_transposed(weighted_high, low))
    rows = lax.broadcasted_iota(jnp.int32, update.shape, 0)
    cols = lax.broadcasted_iota(jnp.int32, update.shape, 1)
    return split(jnp.where(rows == cols, 1.0, 0.0) - update)


def build_kernel(parts, has_input, *refs):
    count = max(part[0] for part in parts) + 1
    pieces = refs[:count]
    outs = refs[count + (2 if has_input else 0) :][:2]
    staged, sems = refs[-2], refs[-1]
    depth = staged.shape[2]
    copies = []
    at = 0
    for index, (source, blocks, group, place) in enumerate(parts):
        size = len(blocks)
        for block in blocks:
            high, low = build_reflection(pieces[source][block])
            staged[at, :depth] = high
            staged[at, depth:] = low
            at += 1
        first = place(lax.axis_index("vec"))
        copy = pltpu.make_async_copy(
            staged.at[pl.ds(at - size, size)], outs[group].at[pl.ds(first, size)], sems.at[index]
        )
        copy.start()
        copies.append(copy)
    for copy in copies:
        copy.wait()


def build(buffers, shapes, pieces, parts):
    depth = pieces[0].shape[-2]
    blocks = sum(len(part[1]) for part in parts)
    has_input = buffers is not None
    any_spec = pl.BlockSpec(memory_space=pl.ANY)
    return pl.pallas_call(
        functools.partial(build_kernel, parts, has_input),
        out_shape=tuple(jax.ShapeDtypeStruct(shape, BF16) for shape in shapes),
        in_specs=[pl.BlockSpec(memory_space=pltpu.VMEM)] * len(pieces) + ([any_spec] * 2 if has_input else []),
        out_specs=(any_spec, any_spec),
        scratch_shapes=[pltpu.VMEM((blocks, 2 * depth, depth), BF16), pltpu.SemaphoreType.DMA((len(parts),))],
        input_output_aliases={len(pieces): 0, len(pieces) + 1: 1} if has_input else {},
        compiler_params=pltpu.CompilerParams(vmem_limit_bytes=VMEM_BYTES),
        cost_estimate=pl.CostEstimate(
            flops=blocks * 300_000_000, bytes_accessed=blocks * depth * depth * 6, transcendentals=0
        ),
    )(*pieces, *(buffers if has_input else ()))


def parts_of(keys):
    return [
        (source, [(group, block) for block in range(2)], group, lambda vec, key=key: 2 * place_of(2 * key[0] + key[1]))
        for source, key in enumerate(keys)
        for group in range(2)
    ]


def apply(reflection, upper, lower):
    depth = reflection.shape[1]
    high, low = split(jnp.concatenate([upper, lower], axis=0))
    both = dot(reflection, high)
    result = both[:depth] + (both[depth:] + dot(reflection[:depth], low))
    return result[: depth // 2], result[depth // 2 :]


def chunks(total, size=256):
    return [(start, min(size, total - start)) for start in range(0, total, size)]


def sweep_kernel(width, unit, other_half, *refs):
    if unit:
        first_hbm, second_hbm, out, state_out, first, second, first_state, second_state, between, result, sems = refs
        data = None
    else:
        (first_hbm, second_hbm, data_hbm, tail_hbm, out, state_out) = refs[:6]
        first, second, data, first_state, second_state, between, result, sems = refs[6:]
    first_cols, second_cols = first_state.shape[1], second_state.shape[1]
    first_count, second_count = first.shape[0], second.shape[0]
    granules = first_count // 2

    def copies_of(m):
        result = [pltpu.make_async_copy(first_hbm.at[pl.ds(2 * m, 2)], first.at[pl.ds(2 * m, 2)], sems.at[0, m])]
        if not unit:
            core = lax.rem(lax.axis_index("row"), 2)
            half = (1 - core) if other_half else core
            cols = pl.ds(pl.multiple_of(half * first_cols, first_cols), first_cols)
            if isinstance(m, int) and m == granules - 1:
                source = tail_hbm.at[:, cols]
            else:
                source = data_hbm.at[pl.ds(m * 2 * width, 2 * width), cols]
            result.append(pltpu.make_async_copy(source, data.at[m], sems.at[1, m]))
        return result

    def second_copy(m):
        size = 1 if isinstance(m, int) and 2 * m + 1 >= second_count else 2
        return pltpu.make_async_copy(second_hbm.at[pl.ds(2 * m, size)], second.at[pl.ds(2 * m, size)], sems.at[2, m])

    def out_copy(block):
        return pltpu.make_async_copy(
            result.at[pl.ds(block * width, width)], out.at[pl.ds(block * width, width)], sems.at[3, block]
        )

    for m in range(granules):
        for copy in copies_of(m):
            copy.start()
        second_copy(m).start()
    for m in range(2):
        for copy in copies_of(m):
            copy.wait()
    second_copy(0).wait()

    def first_step(m, odd):
        reflection = first[2 * m + odd]
        for start, size in chunks(first_cols):
            if unit:
                lower = jnp.zeros((width, size), F32)
            else:
                lower = data[m, odd * width : (odd + 1) * width, start : start + size]
            top, bottom = apply(reflection, first_state[:, start : start + size], lower)
            between[:, start : start + size] = top
            first_state[:, start : start + size] = bottom

    def second_step(index, keep):
        reflection = second[index]
        for start, size in chunks(second_cols):
            top, bottom = apply(
                reflection, second_state[:, start : start + size], between[:, start : start + size]
            )
            if keep:
                row = (index - 1) * width
                if not isinstance(row, int):
                    row = pl.multiple_of(row, width)
                result[pl.ds(row, width), start : start + size] = top
            second_state[:, start : start + size] = bottom

    def both_steps(m, odd):
        index = 2 * m + odd - 2
        second_step(index, True)
        first_step(m, odd)
        out_copy(index - 1).start()

    if unit:
        rows = lax.broadcasted_iota(jnp.int32, (width, width), 0)
        cols = lax.broadcasted_iota(jnp.int32, (width, width), 1)
        eye = jnp.where(rows == cols, 1.0, 0.0)
        first_state[...] = eye
        second_state[...] = jnp.concatenate([jnp.zeros((width, width), F32), eye], axis=1)
        between[...] = jnp.zeros_like(between)
    else:
        first_state[...] = jnp.zeros_like(first_state)
        second_state[...] = jnp.zeros_like(second_state)

        @pl.when(lax.axis_index("row") == 0)
        def _():
            first_step(0, 0)
            first_step(0, 1)
            second_step(0, False)

    first_step(1, 0)
    both_steps(1, 1)

    @pl.loop(2, granules - 1)
    def _(m):
        for copy in copies_of(m):
            copy.wait()
        second_copy(m - 1).wait()
        both_steps(m, 0)
        both_steps(m, 1)

    last = granules - 1
    for copy in copies_of(last):
        copy.wait()
    second_copy(last - 1).wait()
    both_steps(last, 0)
    both_steps(last, 1)
    second_copy(last).wait()
    second_step(second_count - 1, True)
    out_copy(second_count - 2).start()
    if unit:
        zeros = jnp.zeros((width, width), F32)
        state_out[:width] = jnp.concatenate([first_state[...], zeros], axis=1)
    else:
        state_out[:width] = first_state[...]
    state_out[width:] = second_state[...]
    for block in range(second_count - 1):
        out_copy(block).wait()


def sweep(buffers, data=None, tail=None, other_half=False, unit=False):
    first, second = buffers
    depth = first.shape[2]
    width = depth // 2
    blocks = second.shape[0] - 1
    granules = first.shape[0] // 2
    first_cols = width if unit else data.shape[1] // 2
    second_cols = 2 * width if unit else first_cols
    any_spec = pl.BlockSpec(memory_space=pl.ANY)
    rows = blocks * width
    scratch = [pltpu.VMEM(first.shape, BF16), pltpu.VMEM(second.shape, BF16)]
    if not unit:
        scratch.append(pltpu.VMEM((granules, 2 * width, first_cols), F32))
    scratch += [
        pltpu.VMEM((width, first_cols), F32),
        pltpu.VMEM((width, second_cols), F32),
        pltpu.VMEM((width, second_cols), F32),
        pltpu.VMEM((rows, second_cols), F32),
        pltpu.SemaphoreType.DMA((4, blocks)),
    ]
    ins = (first, second) if unit else (first, second, data, tail)
    return pl.pallas_call(
        functools.partial(sweep_kernel, width, unit, other_half),
        out_shape=(
            jax.ShapeDtypeStruct((rows, second_cols), F32),
            jax.ShapeDtypeStruct((depth, second_cols), F32),
        ),
        in_specs=[any_spec] * len(ins),
        out_specs=(any_spec, pl.BlockSpec(memory_space=pltpu.VMEM)),
        scratch_shapes=scratch,
        compiler_params=pltpu.CompilerParams(vmem_limit_bytes=VMEM_BYTES),
        cost_estimate=pl.CostEstimate(
            flops=6 * blocks * depth * depth * (first_cols + second_cols),
            bytes_accessed=30 * 2**20,
            transcendentals=0,
        ),
    )(*ins)


def correct_kernel(other_ref, own_ref, response_ref, incoming_ref, out_ref, high_ref, low_ref):
    @pl.when(pl.program_id(0) == 0)
    def _():
        high, low = split(incoming_ref[...])
        high_ref[...] = high
        low_ref[...] = low

    core = lax.rem(lax.axis_index("row"), 2)
    half = own_ref.shape[1]
    high, low = split(response_ref[...])
    both = jnp.concatenate([high, low], axis=0)
    tile = high.shape[0]
    for at in range(2):
        cols = slice(at * half, (at + 1) * half)
        sums = dot(both, high_ref[:, cols])
        update = sums[:tile] + (sums[tile:] + dot(high, low_ref[:, cols]))
        out_ref[:, cols] = jnp.where(core == at, own_ref[...], other_ref[...]) + update


def correct(other, own, response, incoming, tile=256):
    count, half = own.shape
    depth = response.shape[1]
    cols = 2 * half
    tiled = pl.BlockSpec((tile, half), lambda k: (k, 0))
    return pl.pallas_call(
        correct_kernel,
        grid=(count // tile,),
        out_shape=jax.ShapeDtypeStruct((count, cols), F32),
        in_specs=[
            tiled,
            tiled,
            pl.BlockSpec((tile, depth), lambda k: (k, 0)),
            pl.BlockSpec((depth, cols), lambda k: (0, 0)),
        ],
        out_specs=pl.BlockSpec((tile, cols), lambda k: (k, 0)),
        scratch_shapes=[pltpu.VMEM((depth, cols), BF16), pltpu.VMEM((depth, cols), BF16)],
        compiler_params=pltpu.CompilerParams(vmem_limit_bytes=VMEM_BYTES),
    )(other, own, response, incoming)


def local(eigvecs, wy_v, wy_t):
    width = wy_t.shape[-1]
    rows_dev, cols_dev = eigvecs.shape
    own_blocks = rows_dev // width
    row = lax.axis_index("row")
    core, y = row % 2, (row // 2) % Y_SIZE
    below = lax.broadcasted_iota(jnp.int32, (width, width), 0) > lax.broadcasted_iota(
        jnp.int32, (width, width), 1
    )
    packed = jnp.concatenate(
        [jnp.where(below, wy_v[:, :, :width], wy_t), wy_v[:, :, width:]], axis=2
    )
    tail = from_next_row(eigvecs[: 2 * width])
    depth = 2 * width
    shapes = ((own_blocks + 2, 2 * depth, depth), (own_blocks + 1, 2 * depth, depth))

    own = packed
    p01, p30, p10 = across_x(own), along_z(own, 1), along_z(own, -1)
    buffers = build(None, shapes, [own], parts_of([(0, 0)]))
    p01, p30, p10, *buffers = together(p01, p30, p10, *buffers)
    p31, p20, p11 = across_x(p30), along_z(p30, 1), along_z(p01, -1)
    buffers = build(buffers, shapes, [p01, p30, p10], parts_of([(0, 1), (3, 0), (1, 0)]))
    p31, p20, p11, tail, *buffers = together(p31, p20, p11, tail, *buffers)
    last = [across_x(p20[0]), along_z(p31[1, :1], 1), along_z(p11[1, 1:], -1)]
    known = {(0, 0): own, (0, 1): p01, (3, 0): p30, (1, 0): p10, (3, 1): p31, (2, 0): p20, (1, 1): p11}
    picked = pick_first(known)
    vecs, rows = lax.axis_size("vec"), lax.axis_size("row")
    late = 5
    extras = [
        lax.ppermute(
            picked,
            ("row", "vec"),
            [((i + 1) * vecs + v, i * vecs + v) for i in range(rows - 1) for v in range(vecs) if v != late],
        ),
        lax.ppermute(
            picked, ("row", "vec"), [((i + 1) * vecs + late - 1, i * vecs + late) for i in range(rows - 1)]
        ),
    ]
    buffers = build(buffers, shapes, [p31, p20, p11], parts_of([(3, 1), (2, 0), (1, 1)]))
    *arrived, _, _ = together(*last, *extras, *buffers)
    extra = jnp.where(lax.axis_index("vec") == late, arrived[4], arrived[3])
    opposite = 2 * 2 + 1
    buffers = build(
        buffers,
        shapes,
        [arrived[0], arrived[1], arrived[2], extra],
        [
            (0, [0, 1], 0, lambda vec: 2 * place_of(opposite)),
            (1, [0], 1, lambda vec: 2 * place_of(opposite)),
            (2, [0], 1, lambda vec: 2 * place_of(opposite) + 1),
            (3, [0, 1], 0, lambda vec: own_blocks),
            (3, [2], 1, lambda vec: own_blocks),
        ],
    )

    response, transition = sweep(buffers, unit=True)
    received_transition = across_core(transition)
    other_rows, other_offset = sweep(buffers, eigvecs, tail, other_half=True)
    received_offset = across_core(other_offset)
    lower_transition = jnp.where(core == 0, transition, received_transition)
    upper_transition = jnp.where(core == 0, received_transition, transition)
    chip_transition = dot(upper_transition, lower_transition, HIGHEST)
    part = lax.dynamic_slice_in_dim(chip_transition, core * width, width, 0)
    parts = jnp.stack([part] + [along_y(part, d) for d in range(1, Y_SIZE)])
    own_rows, own_offset = sweep(buffers, eigvecs, tail, other_half=False)
    other_parts = across_core(parts)
    lower_offset = jnp.where(core == 0, own_offset, received_offset)
    upper_offset = jnp.where(core == 0, received_offset, own_offset)
    chip_offset = dot(upper_transition, lower_offset, HIGHEST) + upper_offset
    quarter = chip_offset.shape[1] // Y_SIZE

    def quarter_of(index):
        return lax.dynamic_slice_in_dim(chip_offset, index * quarter, quarter, 1)

    offsets = jnp.stack(
        [quarter_of(y)] + [along_y(quarter_of((y + d) % Y_SIZE), d) for d in range(1, Y_SIZE)]
    )

    def at_chip(stacked, index):
        return lax.dynamic_index_in_dim(stacked, (y - index) % Y_SIZE, 0, False)

    transitions = jnp.where(
        core == 0,
        jnp.concatenate([parts, other_parts], axis=1),
        jnp.concatenate([other_parts, parts], axis=1),
    )
    steps = [(at_chip(transitions, at), at_chip(offsets, at)) for at in range(Y_SIZE)]
    state = steps[0][1]
    for at in range(1, Y_SIZE):
        state = dot(steps[at][0], state, HIGHEST) + steps[at][1]
    size = lax.axis_size("row")
    entering = lax.ppermute(state, "row", [(i, i + size // 2) for i in range(size // 2)])
    result = [entering]
    for at in range(Y_SIZE - 1):
        result.append(dot(steps[at][0], result[-1], HIGHEST) + steps[at][1])
    result = jnp.stack(result)
    back = [lax.dynamic_index_in_dim(result, (y + d) % Y_SIZE, 0, False) for d in range(Y_SIZE)]
    arrived = jnp.stack([back[0]] + [along_y(back[d], d) for d in range(1, Y_SIZE)])
    into_chip = jnp.concatenate([at_chip(arrived, at) for at in range(Y_SIZE)], axis=1)
    into_second = dot(lower_transition, into_chip, HIGHEST) + lower_offset
    kept = jnp.where(core == 0, into_chip, into_second)
    given = jnp.where(core == 0, into_second, into_chip)
    taken = across_core(given)
    incoming = jnp.where(
        core == 0, jnp.concatenate([kept, taken], axis=1), jnp.concatenate([taken, kept], axis=1)
    )
    return correct(other_rows, own_rows, response, incoming)


def solution(mesh):
    placed = (
        P("row", "vec"),
        P(None, ("row", "vec"), None, None),
        P(None, ("row", "vec"), None, None),
    )
    return jax.shard_map(
        local, mesh=mesh, in_specs=placed, out_specs=P("row", "vec"), check_vma=False
    )
```

```python
import functools

import jax
import jax.numpy as jnp
from jax import lax
from jax.experimental import pallas as pl
from jax.experimental.pallas import tpu as pltpu
from jax.sharding import PartitionSpec as P

F32 = jnp.float32
BF16 = jnp.bfloat16
Z_SIZE = 4
Y_SIZE = 4
HIGHEST = lax.Precision.HIGHEST
VMEM_BYTES = 56 * 2**20


def dot(a, b, precision=None):
    return jnp.dot(a, b, precision=precision, preferred_element_type=F32)


def dot_transposed(a, b):
    return lax.dot_general(a, b, (((1,), (1,)), ((), ())), preferred_element_type=F32)


def split(value):
    high = value.astype(BF16)
    return high, (value - high.astype(F32)).astype(BF16)


def along_z(value, by):
    pairs = [(v, ((v // 2 + by) % Z_SIZE) * 2 + v % 2) for v in range(2 * Z_SIZE)]
    return lax.ppermute(value, "vec", pairs)


def across_x(value):
    return lax.ppermute(value, "vec", [(v, v ^ 1) for v in range(2 * Z_SIZE)])


def across_core(value):
    return lax.ppermute(value, "row", [(i, i ^ 1) for i in range(lax.axis_size("row"))])


def along_y(value, by):
    def target(i):
        high, y, core = i // (2 * Y_SIZE), (i // 2) % Y_SIZE, i % 2
        return (high * Y_SIZE + (y + by) % Y_SIZE) * 2 + core

    return lax.ppermute(value, "row", [(i, target(i)) for i in range(lax.axis_size("row"))])


def from_next_row(value):
    return lax.ppermute(value, "row", [(i + 1, i) for i in range(lax.axis_size("row") - 1)])


def together(*values):
    return lax.optimization_barrier(values)


def place_of(index):
    vec = lax.axis_index("vec")
    z, x = vec // 2, vec % 2
    dz, dx = index // 2, index % 2
    return lax.rem(z + dz, Z_SIZE) * 2 + lax.rem(x + dx, 2)


def pick_kernel(keys, *refs):
    pieces, out, sems = refs[:-2], refs[-2], refs[-1]
    for (dz, dx), piece in zip(keys, pieces):

        @pl.when(place_of(2 * dz + dx) == 0)
        def _():
            copies = [
                pltpu.make_async_copy(piece.at[0], out.at[pl.ds(0, 2)], sems.at[0]),
                pltpu.make_async_copy(piece.at[1, pl.ds(0, 1)], out.at[pl.ds(2, 1)], sems.at[1]),
            ]
            for copy in copies:
                copy.start()
            for copy in copies:
                copy.wait()


def pick_first(pieces):
    keys = list(pieces)
    return pl.pallas_call(
        functools.partial(pick_kernel, keys),
        out_shape=jax.ShapeDtypeStruct((3,) + pieces[keys[0]].shape[2:], F32),
        in_specs=[pl.BlockSpec(memory_space=pl.ANY)] * len(keys),
        out_specs=pl.BlockSpec(memory_space=pltpu.VMEM),
        scratch_shapes=[pltpu.SemaphoreType.DMA((2,))],
        compiler_params=pltpu.CompilerParams(vmem_limit_bytes=VMEM_BYTES),
    )(*[pieces[key] for key in keys])


def build_reflection(packed):
    width = packed.shape[1]
    rows = lax.broadcasted_iota(jnp.int32, (width, width), 0)
    cols = lax.broadcasted_iota(jnp.int32, (width, width), 1)
    top = packed[:width]
    unit = jnp.where(rows == cols, 1.0, jnp.where(rows > cols, top, 0.0))
    factor = jnp.where(rows <= cols, top, 0.0)
    vectors = jnp.concatenate([unit, packed[width:]], axis=0)
    high, low = split(vectors)
    factor_high, factor_low = split(factor)
    both = dot(jnp.concatenate([high, low], axis=0), factor_high)
    weighted_high, weighted_low = split(
        both[: 2 * width] + (both[2 * width :] + dot(high, factor_low))
    )
    both = dot_transposed(jnp.concatenate([weighted_high, weighted_low], axis=0), high)
    update = both[: 2 * width] + (both[2 * width :] + dot_transposed(weighted_high, low))
    rows = lax.broadcasted_iota(jnp.int32, update.shape, 0)
    cols = lax.broadcasted_iota(jnp.int32, update.shape, 1)
    return split(jnp.where(rows == cols, 1.0, 0.0) - update)


def build_kernel(parts, has_input, *refs):
    pieces = refs[: len(refs) - (6 if has_input else 4)]
    outs = refs[-4:-2]
    staged, sems = refs[-2], refs[-1]
    depth = staged.shape[2]
    copies = []
    at = 0
    for index, (source, blocks, group, place) in enumerate(parts):
        size = len(blocks)
        for block in blocks:
            if isinstance(source, tuple):
                usual, late, late_vec = source
                packed = jnp.where(lax.axis_index("vec") == late_vec, pieces[late][block], pieces[usual][block])
            else:
                packed = pieces[source][block]
            high, low = build_reflection(packed)
            staged[at, :depth] = high
            staged[at, depth:] = low
            at += 1
        first = place(lax.axis_index("vec"))
        copy = pltpu.make_async_copy(
            staged.at[pl.ds(at - size, size)], outs[group].at[pl.ds(first, size)], sems.at[index]
        )
        copy.start()
        copies.append(copy)
    for copy in copies:
        copy.wait()


def build(buffers, shapes, pieces, parts):
    depth = pieces[0].shape[-2]
    blocks = sum(len(part[1]) for part in parts)
    has_input = buffers is not None
    any_spec = pl.BlockSpec(memory_space=pl.ANY)
    return pl.pallas_call(
        functools.partial(build_kernel, parts, has_input),
        out_shape=tuple(jax.ShapeDtypeStruct(shape, BF16) for shape in shapes),
        in_specs=[pl.BlockSpec(memory_space=pltpu.VMEM)] * len(pieces) + ([any_spec] * 2 if has_input else []),
        out_specs=(any_spec, any_spec),
        scratch_shapes=[pltpu.VMEM((blocks, 2 * depth, depth), BF16), pltpu.SemaphoreType.DMA((len(parts),))],
        input_output_aliases={len(pieces): 0, len(pieces) + 1: 1} if has_input else {},
        compiler_params=pltpu.CompilerParams(vmem_limit_bytes=VMEM_BYTES),
        cost_estimate=pl.CostEstimate(
            flops=blocks * 300_000_000, bytes_accessed=blocks * depth * depth * 6, transcendentals=0
        ),
    )(*pieces, *(buffers if has_input else ()))


def parts_of(keys):
    return [
        (source, [(group, block) for block in range(2)], group, lambda vec, key=key: 2 * place_of(2 * key[0] + key[1]))
        for source, key in enumerate(keys)
        for group in range(2)
    ]


def apply(reflection, upper, lower):
    depth = reflection.shape[1]
    high, low = split(jnp.concatenate([upper, lower], axis=0))
    both = dot(reflection, high)
    result = both[:depth] + (both[depth:] + dot(reflection[:depth], low))
    return result[: depth // 2], result[depth // 2 :]


def chunks(total, size=256):
    return [(start, min(size, total - start)) for start in range(0, total, size)]


def sweep_kernel(width, unit, *refs):
    if unit:
        first_hbm, second_hbm, out, state_out, first, second, first_state, second_state, between, result, sems = refs
        data = None
    else:
        (first_hbm, second_hbm, data_hbm, tail_hbm, out, state_out) = refs[:6]
        first, second, data, first_state, second_state, between, result, sems = refs[6:]
    first_cols, second_cols = first_state.shape[1], second_state.shape[1]
    first_count, second_count = first.shape[0], second.shape[0]
    granules = first_count // 2

    def copies_of(m):
        result = [pltpu.make_async_copy(first_hbm.at[pl.ds(2 * m, 2)], first.at[pl.ds(2 * m, 2)], sems.at[0, m])]
        if not unit:
            if isinstance(m, int) and m == granules - 1:
                source = tail_hbm
            else:
                source = data_hbm.at[pl.ds(m * 2 * width, 2 * width)]
            result.append(pltpu.make_async_copy(source, data.at[m], sems.at[1, m]))
        return result

    def second_copy(m):
        size = 1 if isinstance(m, int) and 2 * m + 1 >= second_count else 2
        return pltpu.make_async_copy(second_hbm.at[pl.ds(2 * m, size)], second.at[pl.ds(2 * m, size)], sems.at[2, m])

    def out_copy(block):
        return pltpu.make_async_copy(
            result.at[pl.ds(block * width, width)], out.at[pl.ds(block * width, width)], sems.at[3, block]
        )

    for m in range(granules):
        for copy in copies_of(m):
            copy.start()
        second_copy(m).start()
    for m in range(2):
        for copy in copies_of(m):
            copy.wait()
    second_copy(0).wait()

    def first_step(m, odd):
        reflection = first[2 * m + odd]
        for start, size in chunks(first_cols):
            if unit:
                lower = jnp.zeros((width, size), F32)
            else:
                lower = data[m, odd * width : (odd + 1) * width, start : start + size]
            top, bottom = apply(reflection, first_state[:, start : start + size], lower)
            between[:, start : start + size] = top
            first_state[:, start : start + size] = bottom

    def second_step(index, keep):
        reflection = second[index]
        for start, size in chunks(second_cols):
            top, bottom = apply(
                reflection, second_state[:, start : start + size], between[:, start : start + size]
            )
            if keep:
                row = (index - 1) * width
                if not isinstance(row, int):
                    row = pl.multiple_of(row, width)
                result[pl.ds(row, width), start : start + size] = top
            second_state[:, start : start + size] = bottom

    def both_steps(m, odd):
        index = 2 * m + odd - 2
        second_step(index, True)
        first_step(m, odd)
        out_copy(index - 1).start()

    if unit:
        rows = lax.broadcasted_iota(jnp.int32, (width, width), 0)
        cols = lax.broadcasted_iota(jnp.int32, (width, width), 1)
        eye = jnp.where(rows == cols, 1.0, 0.0)
        first_state[...] = eye
        second_state[...] = jnp.concatenate([jnp.zeros((width, width), F32), eye], axis=1)
        between[...] = jnp.zeros_like(between)
    else:
        first_state[...] = jnp.zeros_like(first_state)
        second_state[...] = jnp.zeros_like(second_state)

        @pl.when(lax.axis_index("row") == 0)
        def _():
            first_step(0, 0)
            first_step(0, 1)
            second_step(0, False)

    first_step(1, 0)
    both_steps(1, 1)

    @pl.loop(2, granules - 1)
    def _(m):
        for copy in copies_of(m):
            copy.wait()
        second_copy(m - 1).wait()
        both_steps(m, 0)
        both_steps(m, 1)

    last = granules - 1
    for copy in copies_of(last):
        copy.wait()
    second_copy(last - 1).wait()
    both_steps(last, 0)
    both_steps(last, 1)
    second_copy(last).wait()
    second_step(second_count - 1, True)
    out_copy(second_count - 2).start()
    if unit:
        zeros = jnp.zeros((width, width), F32)
        state_out[:width] = jnp.concatenate([first_state[...], zeros], axis=1)
    else:
        state_out[:width] = first_state[...]
    state_out[width:] = second_state[...]
    for block in range(second_count - 1):
        out_copy(block).wait()


def sweep(buffers, data=None, tail=None, unit=False):
    first, second = buffers
    depth = first.shape[2]
    width = depth // 2
    blocks = second.shape[0] - 1
    granules = first.shape[0] // 2
    first_cols = width if unit else data.shape[1]
    second_cols = 2 * width if unit else first_cols
    any_spec = pl.BlockSpec(memory_space=pl.ANY)
    rows = blocks * width
    scratch = [pltpu.VMEM(first.shape, BF16), pltpu.VMEM(second.shape, BF16)]
    if not unit:
        scratch.append(pltpu.VMEM((granules, 2 * width, first_cols), F32))
    scratch += [
        pltpu.VMEM((width, first_cols), F32),
        pltpu.VMEM((width, second_cols), F32),
        pltpu.VMEM((width, second_cols), F32),
        pltpu.VMEM((rows, second_cols), F32),
        pltpu.SemaphoreType.DMA((4, blocks)),
    ]
    ins = (first, second) if unit else (first, second, data, tail)
    return pl.pallas_call(
        functools.partial(sweep_kernel, width, unit),
        out_shape=(
            jax.ShapeDtypeStruct((rows, second_cols), F32),
            jax.ShapeDtypeStruct((depth, second_cols), F32),
        ),
        in_specs=[any_spec] * len(ins),
        out_specs=(any_spec, pl.BlockSpec(memory_space=pltpu.VMEM)),
        scratch_shapes=scratch,
        compiler_params=pltpu.CompilerParams(vmem_limit_bytes=VMEM_BYTES),
        cost_estimate=pl.CostEstimate(
            flops=6 * blocks * depth * depth * (first_cols + second_cols),
            bytes_accessed=30 * 2**20,
            transcendentals=0,
        ),
    )(*ins)


def correct_kernel(tile, rows_hbm, response_hbm, incoming, out_hbm, rows, response, sems):
    count = rows.shape[0] // tile

    def span(index):
        return pl.ds(index * tile, tile)

    arrivals = [
        (
            pltpu.make_async_copy(response_hbm.at[span(k)], response.at[span(k)], sems.at[0, k]),
            pltpu.make_async_copy(rows_hbm.at[span(k)], rows.at[span(k)], sems.at[1, k]),
        )
        for k in range(count)
    ]
    for pair in arrivals:
        for copy in pair:
            copy.start()
    incoming_high, incoming_low = split(incoming[...])
    departures = []
    for k in range(count):
        for copy in arrivals[k]:
            copy.wait()
        high, low = split(response[k * tile : (k + 1) * tile])
        both = jnp.concatenate([high, low], axis=0)
        for start, size in chunks(rows.shape[1], 512):
            at = (slice(k * tile, (k + 1) * tile), slice(start, start + size))
            sums = dot(both, incoming_high[:, at[1]])
            rows[at] = rows[at] + (sums[:tile] + (sums[tile:] + dot(high, incoming_low[:, at[1]])))
        copy = pltpu.make_async_copy(rows.at[span(k)], out_hbm.at[span(k)], sems.at[2, k])
        copy.start()
        departures.append(copy)
    for copy in departures:
        copy.wait()


def correct(rows, response, incoming, tile=256):
    any_spec = pl.BlockSpec(memory_space=pl.ANY)
    return pl.pallas_call(
        functools.partial(correct_kernel, tile),
        out_shape=jax.ShapeDtypeStruct(rows.shape, F32),
        in_specs=[any_spec, any_spec, pl.BlockSpec(memory_space=pltpu.VMEM)],
        out_specs=any_spec,
        scratch_shapes=[
            pltpu.VMEM(rows.shape, F32),
            pltpu.VMEM(response.shape, F32),
            pltpu.SemaphoreType.DMA((3, rows.shape[0] // tile)),
        ],
        compiler_params=pltpu.CompilerParams(vmem_limit_bytes=VMEM_BYTES),
    )(rows, response, incoming)


def local(eigvecs, wy_v, wy_t):
    width = wy_t.shape[-1]
    rows_dev, cols_dev = eigvecs.shape
    own_blocks = rows_dev // width
    row = lax.axis_index("row")
    core, y = row % 2, (row // 2) % Y_SIZE
    below = lax.broadcasted_iota(jnp.int32, (width, width), 0) > lax.broadcasted_iota(
        jnp.int32, (width, width), 1
    )
    packed = jnp.concatenate(
        [jnp.where(below, wy_v[:, :, :width], wy_t), wy_v[:, :, width:]], axis=2
    )
    tail = from_next_row(eigvecs[: 2 * width])
    depth = 2 * width
    shapes = ((own_blocks + 2, 2 * depth, depth), (own_blocks + 1, 2 * depth, depth))

    own = packed
    p01, p30, p10 = across_x(own), along_z(own, 1), along_z(own, -1)
    buffers = build(None, shapes, [own], parts_of([(0, 0)]))
    p01, p30, p10, *buffers = together(p01, p30, p10, *buffers)
    p31, p20, p11 = across_x(p30), along_z(p30, 1), along_z(p01, -1)
    buffers = build(buffers, shapes, [p01, p30, p10], parts_of([(0, 1), (3, 0), (1, 0)]))
    p31, p20, p11, *buffers = together(p31, p20, p11, *buffers)
    last = [across_x(p20[0]), along_z(p31[1, :1], 1), along_z(p11[1, 1:], -1)]
    known = {(0, 0): own, (0, 1): p01, (3, 0): p30, (1, 0): p10, (3, 1): p31, (2, 0): p20, (1, 1): p11}
    picked = pick_first(known)
    vecs, rows = lax.axis_size("vec"), lax.axis_size("row")
    late = 5
    extras = [
        lax.ppermute(
            picked,
            ("row", "vec"),
            [((i + 1) * vecs + v, i * vecs + v) for i in range(rows - 1) for v in range(vecs) if v != late],
        ),
        lax.ppermute(
            picked, ("row", "vec"), [((i + 1) * vecs + late - 1, i * vecs + late) for i in range(rows - 1)]
        ),
    ]
    buffers = build(buffers, shapes, [p31, p20, p11], parts_of([(3, 1), (2, 0), (1, 1)]))
    *arrived, _, _ = together(*last, *extras, *buffers)
    opposite = 2 * 2 + 1
    buffers = build(
        buffers,
        shapes,
        arrived,
        [
            (0, [0, 1], 0, lambda vec: 2 * place_of(opposite)),
            (1, [0], 1, lambda vec: 2 * place_of(opposite)),
            (2, [0], 1, lambda vec: 2 * place_of(opposite) + 1),
            ((3, 4, late), [0, 1], 0, lambda vec: own_blocks),
            ((3, 4, late), [2], 1, lambda vec: own_blocks),
        ],
    )

    response, transition = sweep(buffers, unit=True)
    received_transition = across_core(transition)
    lower_transition = jnp.where(core == 0, transition, received_transition)
    upper_transition = jnp.where(core == 0, received_transition, transition)
    chip_transition = dot(upper_transition, lower_transition, HIGHEST)
    chip_transition, *buffers = together(chip_transition, *buffers)
    transitions = [chip_transition] + [along_y(chip_transition, d) for d in range(1, Y_SIZE)]
    swept, offset = sweep(buffers, eigvecs, tail)
    offset, *transitions = together(offset, *transitions)
    half = cols_dev // 2
    own_offset = lax.dynamic_slice_in_dim(offset, core * half, half, 1)
    received_offset = across_core(lax.dynamic_slice_in_dim(offset, (1 - core) * half, half, 1))
    lower_offset = jnp.where(core == 0, own_offset, received_offset)
    upper_offset = jnp.where(core == 0, received_offset, own_offset)
    chip_offset = dot(upper_transition, lower_offset, HIGHEST) + upper_offset
    quarter = half // Y_SIZE

    def quarter_of(index):
        return lax.dynamic_slice_in_dim(chip_offset, index * quarter, quarter, 1)

    offsets = jnp.stack(
        [quarter_of(y)] + [along_y(quarter_of((y + d) % Y_SIZE), d) for d in range(1, Y_SIZE)]
    )
    transitions = jnp.stack(transitions)

    def at_chip(stacked, index):
        return lax.dynamic_index_in_dim(stacked, (y - index) % Y_SIZE, 0, False)

    steps = [(at_chip(transitions, at), at_chip(offsets, at)) for at in range(Y_SIZE)]
    state = steps[0][1]
    for at in range(1, Y_SIZE):
        state = dot(steps[at][0], state, HIGHEST) + steps[at][1]
    size = lax.axis_size("row")
    entering = lax.ppermute(state, "row", [(i, i + size // 2) for i in range(size // 2)])
    result = [entering]
    for at in range(Y_SIZE - 1):
        result.append(dot(steps[at][0], result[-1], HIGHEST) + steps[at][1])
    result = jnp.stack(result)
    back = [lax.dynamic_index_in_dim(result, (y + d) % Y_SIZE, 0, False) for d in range(Y_SIZE)]
    arrived = jnp.stack([back[0]] + [along_y(back[d], d) for d in range(1, Y_SIZE)])
    into_chip = jnp.concatenate([at_chip(arrived, at) for at in range(Y_SIZE)], axis=1)
    into_second = dot(lower_transition, into_chip, HIGHEST) + lower_offset
    kept = jnp.where(core == 0, into_chip, into_second)
    given = jnp.where(core == 0, into_second, into_chip)
    taken = across_core(given)
    incoming = jnp.where(
        core == 0, jnp.concatenate([kept, taken], axis=1), jnp.concatenate([taken, kept], axis=1)
    )
    return correct(swept, response, incoming)


def solution(mesh):
    placed = (
        P("row", "vec"),
        P(None, ("row", "vec"), None, None),
        P(None, ("row", "vec"), None, None),
    )
    return jax.shard_map(
        local, mesh=mesh, in_specs=placed, out_specs=P("row", "vec"), check_vma=False
    )
```

```python
import functools

import jax
import jax.numpy as jnp
from jax import lax
from jax.experimental import pallas as pl
from jax.experimental.pallas import tpu as pltpu
from jax.sharding import PartitionSpec as P

F32 = jnp.float32
BF16 = jnp.bfloat16
Z_SIZE = 4
Y_SIZE = 4
VMEM_BYTES = 56 * 2**20


def dot(a, b, precision=None):
    return jnp.dot(a, b, precision=precision, preferred_element_type=F32)


def dot_transposed(a, b):
    return lax.dot_general(a, b, (((1,), (1,)), ((), ())), preferred_element_type=F32)


def split(value):
    high = value.astype(BF16)
    return high, (value - high.astype(F32)).astype(BF16)


def dot3(a, b):
    high, low = split(a)
    b_high, b_low = split(b)
    count = a.shape[0]
    both = dot(jnp.concatenate([high, low], axis=0), b_high)
    return both[:count] + (both[count:] + dot(high, b_low))


def along_z(value, by):
    pairs = [(v, ((v // 2 + by) % Z_SIZE) * 2 + v % 2) for v in range(2 * Z_SIZE)]
    return lax.ppermute(value, "vec", pairs)


def across_x(value):
    return lax.ppermute(value, "vec", [(v, v ^ 1) for v in range(2 * Z_SIZE)])


def across_core(value):
    return lax.ppermute(value, "row", [(i, i ^ 1) for i in range(lax.axis_size("row"))])


def along_y(value, by):
    def target(i):
        high, y, core = i // (2 * Y_SIZE), (i // 2) % Y_SIZE, i % 2
        return (high * Y_SIZE + (y + by) % Y_SIZE) * 2 + core

    return lax.ppermute(value, "row", [(i, target(i)) for i in range(lax.axis_size("row"))])


def from_next_row(value):
    return lax.ppermute(value, "row", [(i + 1, i) for i in range(lax.axis_size("row") - 1)])


def together(*values):
    return lax.optimization_barrier(values)


def place_of(index):
    vec = lax.axis_index("vec")
    z, x = vec // 2, vec % 2
    dz, dx = index // 2, index % 2
    return lax.rem(z + dz, Z_SIZE) * 2 + lax.rem(x + dx, 2)


def pick_kernel(sources, *refs):
    pieces, out, sems = refs[:-2], refs[-2], refs[-1]
    for (dz, dx), where in sources:

        @pl.when(place_of(2 * dz + dx) == 0)
        def _():
            if len(where) == 1:
                first, second = pieces[where[0]].at[0], pieces[where[0]].at[1, pl.ds(0, 1)]
            else:
                first, second = pieces[where[0]], pieces[where[1]].at[pl.ds(0, 1)]
            copies = [
                pltpu.make_async_copy(first, out.at[pl.ds(0, 2)], sems.at[0]),
                pltpu.make_async_copy(second, out.at[pl.ds(2, 1)], sems.at[1]),
            ]
            for copy in copies:
                copy.start()
            for copy in copies:
                copy.wait()


def pick_first(known):
    arrays, sources = [], []
    for key, held in known.items():
        sources.append((key, tuple(range(len(arrays), len(arrays) + len(held)))))
        arrays += held
    return pl.pallas_call(
        functools.partial(pick_kernel, sources),
        out_shape=jax.ShapeDtypeStruct((3,) + arrays[0].shape[-2:], F32),
        in_specs=[pl.BlockSpec(memory_space=pl.ANY)] * len(arrays),
        out_specs=pl.BlockSpec(memory_space=pltpu.VMEM),
        scratch_shapes=[pltpu.SemaphoreType.DMA((2,))],
        compiler_params=pltpu.CompilerParams(vmem_limit_bytes=VMEM_BYTES),
    )(*arrays)


def build_reflection(packed):
    width = packed.shape[1]
    rows = lax.broadcasted_iota(jnp.int32, (width, width), 0)
    cols = lax.broadcasted_iota(jnp.int32, (width, width), 1)
    top = packed[:width]
    unit = jnp.where(rows == cols, 1.0, jnp.where(rows > cols, top, 0.0))
    factor = jnp.where(rows <= cols, top, 0.0)
    vectors = jnp.concatenate([unit, packed[width:]], axis=0)
    high, low = split(vectors)
    factor_high, factor_low = split(factor)
    both = dot(jnp.concatenate([high, low], axis=0), factor_high)
    weighted_high, weighted_low = split(
        both[: 2 * width] + (both[2 * width :] + dot(high, factor_low))
    )
    both = dot_transposed(jnp.concatenate([weighted_high, weighted_low], axis=0), high)
    update = both[: 2 * width] + (both[2 * width :] + dot_transposed(weighted_high, low))
    rows = lax.broadcasted_iota(jnp.int32, update.shape, 0)
    cols = lax.broadcasted_iota(jnp.int32, update.shape, 1)
    return split(jnp.where(rows == cols, 1.0, 0.0) - update)


def build_kernel(parts, has_input, *refs):
    pieces = refs[: len(refs) - (6 if has_input else 4)]
    outs = refs[-4:-2]
    staged, sems = refs[-2], refs[-1]
    depth = staged.shape[2]
    copies = []
    at = 0
    for index, (source, blocks, group, place) in enumerate(parts):
        size = len(blocks)
        for block in blocks:
            if isinstance(source, tuple):
                usual, late, late_vec = source
                packed = jnp.where(lax.axis_index("vec") == late_vec, pieces[late][block], pieces[usual][block])
            else:
                packed = pieces[source][block]
            high, low = build_reflection(packed)
            staged[at, :depth] = high
            staged[at, depth:] = low
            at += 1
        first = place(lax.axis_index("vec"))
        copy = pltpu.make_async_copy(
            staged.at[pl.ds(at - size, size)], outs[group].at[pl.ds(first, size)], sems.at[index]
        )
        copy.start()
        copies.append(copy)
    for copy in copies:
        copy.wait()


def build(buffers, shapes, pieces, parts):
    depth = pieces[0].shape[-2]
    blocks = sum(len(part[1]) for part in parts)
    has_input = buffers is not None
    any_spec = pl.BlockSpec(memory_space=pl.ANY)
    return pl.pallas_call(
        functools.partial(build_kernel, parts, has_input),
        out_shape=tuple(jax.ShapeDtypeStruct(shape, BF16) for shape in shapes),
        in_specs=[pl.BlockSpec(memory_space=pltpu.VMEM)] * len(pieces) + ([any_spec] * 2 if has_input else []),
        out_specs=(any_spec, any_spec),
        scratch_shapes=[pltpu.VMEM((blocks, 2 * depth, depth), BF16), pltpu.SemaphoreType.DMA((len(parts),))],
        input_output_aliases={len(pieces): 0, len(pieces) + 1: 1} if has_input else {},
        compiler_params=pltpu.CompilerParams(vmem_limit_bytes=VMEM_BYTES),
        cost_estimate=pl.CostEstimate(
            flops=blocks * 300_000_000, bytes_accessed=blocks * depth * depth * 6, transcendentals=0
        ),
    )(*pieces, *(buffers if has_input else ()))


def placed(source, key, groups=(0, 1), whole=True):
    place = lambda vec: 2 * place_of(2 * key[0] + key[1])
    return [(source, [(group, 0), (group, 1)] if whole else [0, 1], group, place) for group in groups]


def apply(reflection, upper, lower):
    depth = reflection.shape[1]
    high, low = split(jnp.concatenate([upper, lower], axis=0))
    both = dot(reflection, high)
    result = both[:depth] + (both[depth:] + dot(reflection[:depth], low))
    return result[: depth // 2], result[depth // 2 :]


def chunks(total, size=256):
    return [(start, min(size, total - start)) for start in range(0, total, size)]


def first_step(reflection, state, lower, between):
    width, total = state.shape
    for start, size in chunks(total):
        cols = slice(start, start + size)
        below = jnp.zeros((width, size), F32) if lower is None else lower[:, cols]
        top, bottom = apply(reflection, state[:, cols], below)
        between[:, cols] = top
        state[:, cols] = bottom


def second_step(reflection, state, between, out):
    for start, size in chunks(state.shape[1]):
        cols = slice(start, start + size)
        top, bottom = apply(reflection, state[:, cols], between[:, cols])
        if out is not None:
            out[:, cols] = top
        state[:, cols] = bottom


def sweep_copies(first_hbm, second_hbm, data_hbm, tail_hbm, first, second, data, sems):
    granules = first.shape[0] // 2
    rows = 0 if data is None else data.shape[1]

    def first_copies(m):
        copies = [pltpu.make_async_copy(first_hbm.at[pl.ds(2 * m, 2)], first.at[pl.ds(2 * m, 2)], sems.at[0, m])]
        if data is not None:
            is_last = isinstance(m, int) and m == granules - 1
            source = tail_hbm if is_last else data_hbm.at[pl.ds(m * rows, rows)]
            copies.append(pltpu.make_async_copy(source, data.at[m], sems.at[1, m]))
        return copies

    def second_copies(m):
        size = 1 if isinstance(m, int) and 2 * m + 1 >= second.shape[0] else 2
        return [pltpu.make_async_copy(second_hbm.at[pl.ds(2 * m, size)], second.at[pl.ds(2 * m, size)], sems.at[2, m])]

    return first_copies, second_copies


def start_all(copies):
    for copy in copies:
        copy.start()


def wait_all(copies):
    for copy in copies:
        copy.wait()


def run_sweep(first, second, data, first_state, second_state, between, result, out, first_copies, second_copies, sems):
    width = first_state.shape[0]
    granules = first.shape[0] // 2
    blocks = second.shape[0] - 1

    def out_copy(block):
        return pltpu.make_async_copy(
            result.at[pl.ds(block * width, width)], out.at[pl.ds(block * width, width)], sems.at[3, block]
        )

    def rows_of(m, odd):
        return None if data is None else data.at[m, pl.ds(odd * width, width)]

    def finished(block):
        start = block * width
        return result.at[pl.ds(start if isinstance(start, int) else pl.multiple_of(start, width), width)]

    def both_steps(m, odd):
        index = 2 * m + odd - 2
        second_step(second[index], second_state, between, finished(index - 1))
        first_step(first[2 * m + odd], first_state, rows_of(m, odd), between)
        out_copy(index - 1).start()

    wait_all(first_copies(1))
    first_step(first[2], first_state, rows_of(1, 0), between)
    both_steps(1, 1)

    @pl.loop(2, granules - 1)
    def _(m):
        wait_all(first_copies(m))
        wait_all(second_copies(m - 1))
        both_steps(m, 0)
        both_steps(m, 1)

    last = granules - 1
    wait_all(first_copies(last))
    wait_all(second_copies(last - 1))
    both_steps(last, 0)
    both_steps(last, 1)
    wait_all(second_copies(last))
    second_step(second[blocks], second_state, between, finished(blocks - 1))
    out_copy(blocks - 1).start()
    for block in range(blocks):
        out_copy(block).wait()


def unit_kernel(
    first_hbm, second_hbm, data_hbm, out, transition, initial,
    first, second, data, first_state, second_state, between, data_between, result, sems,
):
    width = first_state.shape[0]
    first_copies, second_copies = sweep_copies(first_hbm, second_hbm, None, None, first, second, None, sems)
    granules = first.shape[0] // 2
    is_first = lax.axis_index("row") == 0

    @pl.when(is_first)
    def _():
        rows = pltpu.make_async_copy(data_hbm.at[pl.ds(0, 2 * width)], data, sems.at[1, 0])
        copies = first_copies(0) + second_copies(0) + [rows]
        start_all(copies)
        result[...] = jnp.zeros_like(result)
        transition[...] = jnp.zeros_like(transition)
        initial[...] = jnp.zeros_like(initial)
        cleared = pltpu.make_async_copy(result, out, sems.at[3, 0])
        cleared.start()
        wait_all(copies)
        upper, lower = initial.at[pl.ds(0, width)], initial.at[pl.ds(width, width)]
        first_step(first[0], upper, data.at[pl.ds(0, width)], data_between)
        first_step(first[1], upper, data.at[pl.ds(width, width)], data_between)
        second_step(second[0], lower, data_between, None)
        cleared.wait()

    @pl.when(jnp.logical_not(is_first))
    def _():
        for m in range(granules):
            start_all(first_copies(m) + second_copies(m))
        rows = lax.broadcasted_iota(jnp.int32, (width, width), 0)
        cols = lax.broadcasted_iota(jnp.int32, (width, width), 1)
        eye = jnp.where(rows == cols, 1.0, 0.0)
        zeros = jnp.zeros((width, width), F32)
        first_state[...] = eye
        second_state[...] = jnp.concatenate([zeros, eye], axis=1)
        between[...] = jnp.zeros_like(between)
        initial[...] = jnp.zeros_like(initial)
        wait_all(first_copies(0) + second_copies(0))
        run_sweep(
            first, second, None, first_state, second_state, between, result, out, first_copies, second_copies, sems
        )
        transition[:width] = jnp.concatenate([first_state[...], zeros], axis=1)
        transition[width:] = second_state[...]


def data_kernel(
    first_hbm, second_hbm, data_hbm, tail_hbm, initial, out, own_state, sent_state,
    first, second, data, first_state, second_state, between, result, sems,
):
    width = first_state.shape[0]
    first_copies, second_copies = sweep_copies(
        first_hbm, second_hbm, data_hbm, tail_hbm, first, second, data, sems
    )
    for m in range(first.shape[0] // 2):
        start_all(first_copies(m) + second_copies(m))
    first_state[...] = initial[:width]
    second_state[...] = initial[width:]
    wait_all(first_copies(0) + second_copies(0))
    run_sweep(first, second, data, first_state, second_state, between, result, out, first_copies, second_copies, sems)
    half = own_state.shape[1]
    core = lax.rem(lax.axis_index("row"), 2)
    for target, side in ((own_state, core), (sent_state, 1 - core)):
        cols = pl.ds(pl.multiple_of(side * half, half), half)
        target[:width] = first_state[:, cols]
        target[width:] = second_state[:, cols]


ANY = pl.BlockSpec(memory_space=pl.ANY)
VMEM = pl.BlockSpec(memory_space=pltpu.VMEM)
PARAMS = pltpu.CompilerParams(vmem_limit_bytes=VMEM_BYTES)
CORRECT_PARAMS = pltpu.CompilerParams(vmem_limit_bytes=50 * 2**20)
SMALL_PARAMS = pltpu.CompilerParams(vmem_limit_bytes=16 * 2**20)


def estimate(blocks, depth, cols):
    return pl.CostEstimate(
        flops=6 * blocks * depth * depth * cols, bytes_accessed=30 * 2**20, transcendentals=0
    )


def sweep_units(buffers, data):
    first, second = buffers
    depth = first.shape[2]
    width, blocks, cols = depth // 2, second.shape[0] - 1, data.shape[1]
    return pl.pallas_call(
        unit_kernel,
        out_shape=(
            jax.ShapeDtypeStruct((blocks * width, depth), F32),
            jax.ShapeDtypeStruct((depth, depth), F32),
            jax.ShapeDtypeStruct((depth, cols), F32),
        ),
        in_specs=[ANY] * 3,
        out_specs=(ANY, VMEM, VMEM),
        scratch_shapes=[
            pltpu.VMEM(first.shape, BF16),
            pltpu.VMEM(second.shape, BF16),
            pltpu.VMEM((depth, cols), F32),
            pltpu.VMEM((width, width), F32),
            pltpu.VMEM((width, depth), F32),
            pltpu.VMEM((width, depth), F32),
            pltpu.VMEM((width, cols), F32),
            pltpu.VMEM((blocks * width, depth), F32),
            pltpu.SemaphoreType.DMA((4, blocks)),
        ],
        compiler_params=PARAMS,
        cost_estimate=estimate(blocks, depth, 3 * depth),
    )(first, second, data)


def sweep_data(buffers, data, tail, initial):
    first, second = buffers
    depth = first.shape[2]
    width, blocks, cols = depth // 2, second.shape[0] - 1, data.shape[1]
    return pl.pallas_call(
        data_kernel,
        out_shape=(
            jax.ShapeDtypeStruct((blocks * width, cols), F32),
            jax.ShapeDtypeStruct((depth, cols // 2), F32),
            jax.ShapeDtypeStruct((depth, cols // 2), F32),
        ),
        in_specs=[ANY] * 4 + [VMEM],
        out_specs=(ANY, VMEM, VMEM),
        scratch_shapes=[
            pltpu.VMEM(first.shape, BF16),
            pltpu.VMEM(second.shape, BF16),
            pltpu.VMEM((first.shape[0] // 2, depth, cols), F32),
            pltpu.VMEM((width, cols), F32),
            pltpu.VMEM((width, cols), F32),
            pltpu.VMEM((width, cols), F32),
            pltpu.VMEM((blocks * width, cols), F32),
            pltpu.SemaphoreType.DMA((4, blocks)),
        ],
        compiler_params=PARAMS,
        cost_estimate=estimate(blocks, depth, 2 * cols),
    )(first, second, data, tail, initial)


def small(kernel, outs, *args, scratch=()):
    return pl.pallas_call(
        kernel,
        out_shape=tuple(jax.ShapeDtypeStruct(shape, F32) for shape in outs),
        in_specs=[VMEM] * len(args),
        out_specs=tuple(VMEM for _ in outs),
        scratch_shapes=[pltpu.VMEM(shape, F32) for shape in scratch],
        compiler_params=SMALL_PARAMS,
    )(*args)


def position():
    row = lax.axis_index("row")
    return lax.rem(row, 2), lax.rem(row // 2, Y_SIZE)


def chip_at(d):
    return lax.rem(position()[1] + Y_SIZE - d, Y_SIZE)


def lanes(index, size):
    return pl.ds(pl.multiple_of(index * size, size), size)


def by_core(at_first, otherwise):
    return jnp.where(position()[0] == 0, at_first, otherwise)


def chip_transition_kernel(own, received, out):
    out[...] = dot3(by_core(received[...], own[...]), by_core(own[...], received[...]))


def chip_offset_kernel(own_transition, received_transition, own, received, *refs):
    outs, chip = refs[:-1], refs[-1]
    upper = by_core(received_transition[...], own_transition[...])
    chip[...] = dot3(upper, by_core(own[...], received[...])) + by_core(received[...], own[...])
    size = outs[0].shape[1]
    for d, out in enumerate(outs):
        out[...] = chip[:, lanes(chip_at(Y_SIZE - d), size)]


def products_kernel(*refs):
    transitions, ordered, products = refs[:Y_SIZE], refs[Y_SIZE], refs[Y_SIZE + 1]
    for d, transition in enumerate(transitions):
        ordered[chip_at(d)] = transition[...]
    product = ordered[0]
    products[0] = product
    for at in range(1, Y_SIZE - 1):
        product = dot3(ordered[at], product)
        products[at] = product


def chain_kernel(ordered, *refs):
    offsets, partial, total, placed_offsets = refs[:Y_SIZE], refs[-3], refs[-2], refs[-1]
    for d, offset in enumerate(offsets):
        placed_offsets[chip_at(d)] = offset[...]
    state = placed_offsets[0]
    for at in range(1, Y_SIZE):
        partial[at - 1] = state
        state = dot3(ordered[at], state) + placed_offsets[at]
    total[...] = state


def entering_kernel(entering, products, partial, *refs):
    outs, states = refs[:-1], refs[-1]
    states[0] = entering[...]
    for at in range(1, Y_SIZE):
        states[at] = dot3(products[at - 1], entering[...]) + partial[at - 1]
    for d, out in enumerate(outs):
        out[...] = states[chip_at(Y_SIZE - d)]


def core_kernel(own_transition, received_transition, own, received, *refs):
    arrived, kept, given, chip = refs[:Y_SIZE], refs[-3], refs[-2], refs[-1]
    size = arrived[0].shape[1]
    for d, part in enumerate(arrived):
        chip[:, lanes(chip_at(d), size)] = part[...]
    lower = by_core(own_transition[...], received_transition[...])
    into_second = dot3(lower, chip[...]) + by_core(own[...], received[...])
    kept[...] = by_core(chip[...], into_second)
    given[...] = by_core(into_second, chip[...])


def correct_kernel(tile, rows_hbm, response_hbm, kept, taken, out_hbm, rows, response, incoming_high, incoming_low, sems):
    count = rows.shape[0] // tile

    def span(index):
        return pl.ds(index * tile, tile)

    arrivals = [
        (
            pltpu.make_async_copy(response_hbm.at[span(k)], response.at[span(k)], sems.at[0, k]),
            pltpu.make_async_copy(rows_hbm.at[span(k)], rows.at[span(k)], sems.at[1, k]),
        )
        for k in range(count)
    ]
    for pair in arrivals:
        for copy in pair:
            copy.start()
    core = position()[0]
    for part, side in ((kept, core), (taken, 1 - core)):
        high, low = split(part[...])
        incoming_high[:, lanes(side, part.shape[1])] = high
        incoming_low[:, lanes(side, part.shape[1])] = low
    departures = []
    for k in range(count):
        for copy in arrivals[k]:
            copy.wait()
        high, low = split(response[k * tile : (k + 1) * tile])
        both = jnp.concatenate([high, low], axis=0)
        for start, size in chunks(rows.shape[1], 512):
            at = (slice(k * tile, (k + 1) * tile), slice(start, start + size))
            sums = dot(both, incoming_high[:, at[1]])
            rows[at] = rows[at] + (sums[:tile] + (sums[tile:] + dot(high, incoming_low[:, at[1]])))
        copy = pltpu.make_async_copy(rows.at[span(k)], out_hbm.at[span(k)], sems.at[2, k])
        copy.start()
        departures.append(copy)
    for copy in departures:
        copy.wait()


def correct(rows, response, kept, taken, tile=256):
    incoming = (response.shape[1], rows.shape[1])
    return pl.pallas_call(
        functools.partial(correct_kernel, tile),
        out_shape=jax.ShapeDtypeStruct(rows.shape, F32),
        in_specs=[ANY, ANY, VMEM, VMEM],
        out_specs=ANY,
        scratch_shapes=[
            pltpu.VMEM(rows.shape, F32),
            pltpu.VMEM(response.shape, F32),
            pltpu.VMEM(incoming, BF16),
            pltpu.VMEM(incoming, BF16),
            pltpu.SemaphoreType.DMA((3, rows.shape[0] // tile)),
        ],
        compiler_params=CORRECT_PARAMS,
    )(rows, response, kept, taken)


def local(eigvecs, wy_v, wy_t):
    width = wy_t.shape[-1]
    rows_dev, cols_dev = eigvecs.shape
    own_blocks = rows_dev // width
    below = lax.broadcasted_iota(jnp.int32, (width, width), 0) > lax.broadcasted_iota(
        jnp.int32, (width, width), 1
    )
    own = jnp.concatenate([jnp.where(below, wy_v[:, :, :width], wy_t), wy_v[:, :, width:]], axis=2)
    tail = from_next_row(eigvecs[: 2 * width])
    depth = 2 * width
    shapes = ((own_blocks + 2, 2 * depth, depth), (own_blocks + 1, 2 * depth, depth))

    f30, s30 = along_z(own[0], 1), along_z(own[1], 1)
    p01, p10 = across_x(own), along_z(own, -1)
    buffers = build(None, shapes, [own], placed(0, (0, 0)))
    f30, *buffers = together(f30, *buffers)
    f31, f20, p11 = across_x(f30), along_z(f30, 1), along_z(p01, -1)
    s31, s20 = across_x(s30), along_z(s30, 1)
    buffers = build(
        buffers,
        shapes,
        [p01, p10, f30, s30],
        placed(0, (0, 1)) + placed(1, (1, 0)) + placed(2, (3, 0), (0,), False) + placed(3, (3, 0), (1,), False),
    )
    f20, s31, *buffers = together(f20, s31, *buffers)
    f21, s21 = across_x(f20), along_z(s31, 1)
    picked = pick_first(
        {
            (0, 0): [own],
            (0, 1): [p01],
            (1, 0): [p10],
            (1, 1): [p11],
            (3, 0): [f30, s30],
            (3, 1): [f31, s31],
            (2, 0): [f20, s20],
        }
    )
    vecs, rows = lax.axis_size("vec"), lax.axis_size("row")
    late = 5
    extras = [
        lax.ppermute(
            picked,
            ("row", "vec"),
            [((i + 1) * vecs + v, i * vecs + v) for i in range(rows - 1) for v in range(vecs) if v != late],
        ),
        lax.ppermute(
            picked, ("row", "vec"), [((i + 1) * vecs + late - 1, i * vecs + late) for i in range(rows - 1)]
        ),
    ]
    buffers = build(
        buffers,
        shapes,
        [p11, f31, s31, f20, s20],
        placed(0, (1, 1))
        + placed(1, (3, 1), (0,), False)
        + placed(2, (3, 1), (1,), False)
        + placed(3, (2, 0), (0,), False)
        + placed(4, (2, 0), (1,), False),
    )
    buffers = build(
        buffers,
        shapes,
        [f21, s21, *extras],
        placed(0, (2, 1), (0,), False)
        + placed(1, (2, 1), (1,), False)
        + [((2, 3, late), [0, 1], 0, lambda vec: own_blocks), ((2, 3, late), [2], 1, lambda vec: own_blocks)],
    )

    half, quarter = cols_dev // 2, cols_dev // (2 * Y_SIZE)
    response, transition, initial = sweep_units(buffers, eigvecs)
    received_transition = across_core(transition)
    (chip_transition,) = small(chip_transition_kernel, [(depth, depth)], transition, received_transition)
    chip_transition, *buffers = together(chip_transition, *buffers)
    transitions = [chip_transition] + [along_y(chip_transition, d) for d in range(1, Y_SIZE)]
    swept, own_offset, sent_offset = sweep_data(buffers, eigvecs, tail, initial)
    sent_offset, *transitions = together(sent_offset, *transitions)
    received_offset = across_core(sent_offset)
    cores = (transition, received_transition, own_offset, received_offset)
    offsets = small(chip_offset_kernel, [(depth, quarter)] * Y_SIZE, *cores, scratch=[(depth, half)])
    offsets = [offsets[0]] + [along_y(offsets[d], d) for d in range(1, Y_SIZE)]
    ordered, products = small(
        products_kernel, [(Y_SIZE, depth, depth), (Y_SIZE - 1, depth, depth)], *transitions
    )
    partial, total = small(
        chain_kernel,
        [(Y_SIZE - 1, depth, quarter), (depth, quarter)],
        ordered,
        *offsets,
        scratch=[(Y_SIZE, depth, quarter)],
    )
    entering = lax.ppermute(total, "row", [(i, i + rows // 2) for i in range(rows // 2)])
    back = small(
        entering_kernel,
        [(depth, quarter)] * Y_SIZE,
        entering,
        products,
        partial,
        scratch=[(Y_SIZE, depth, quarter)],
    )
    arrived = [back[0]] + [along_y(back[d], d) for d in range(1, Y_SIZE)]
    kept, given = small(core_kernel, [(depth, half)] * 2, *cores, *arrived, scratch=[(depth, half)])
    return correct(swept, response, kept, across_core(given))


def solution(mesh):
    placed_in = (
        P("row", "vec"),
        P(None, ("row", "vec"), None, None),
        P(None, ("row", "vec"), None, None),
    )
    return jax.shard_map(
        local, mesh=mesh, in_specs=placed_in, out_specs=P("row", "vec"), check_vma=False
    )
```

```python
import functools

import jax
import jax.numpy as jnp
from jax import lax
from jax.experimental import pallas as pl
from jax.experimental.pallas import tpu as pltpu
from jax.sharding import PartitionSpec as P

F32 = jnp.float32
BF16 = jnp.bfloat16
Z_SIZE = 4
Y_SIZE = 4
VMEM_BYTES = 56 * 2**20


def dot(a, b, precision=None):
    return jnp.dot(a, b, precision=precision, preferred_element_type=F32)


def dot_transposed(a, b):
    return lax.dot_general(a, b, (((1,), (1,)), ((), ())), preferred_element_type=F32)


def split(value):
    high = value.astype(BF16)
    return high, (value - high.astype(F32)).astype(BF16)


def dot3(a, b):
    high, low = split(a)
    b_high, b_low = split(b)
    count = a.shape[0]
    both = dot(jnp.concatenate([high, low], axis=0), b_high)
    return both[:count] + (both[count:] + dot(high, b_low))


def along_z(value, by):
    pairs = [(v, ((v // 2 + by) % Z_SIZE) * 2 + v % 2) for v in range(2 * Z_SIZE)]
    return lax.ppermute(value, "vec", pairs)


def across_x(value):
    return lax.ppermute(value, "vec", [(v, v ^ 1) for v in range(2 * Z_SIZE)])


def across_core(value):
    return lax.ppermute(value, "row", [(i, i ^ 1) for i in range(lax.axis_size("row"))])


def along_y(value, by):
    def target(i):
        high, y, core = i // (2 * Y_SIZE), (i // 2) % Y_SIZE, i % 2
        return (high * Y_SIZE + (y + by) % Y_SIZE) * 2 + core

    return lax.ppermute(value, "row", [(i, target(i)) for i in range(lax.axis_size("row"))])


def from_next_row(value):
    return lax.ppermute(value, "row", [(i + 1, i) for i in range(lax.axis_size("row") - 1)])


def together(*values):
    return lax.optimization_barrier(values)


def place_of(index):
    vec = lax.axis_index("vec")
    z, x = vec // 2, vec % 2
    dz, dx = index // 2, index % 2
    return lax.rem(z + dz, Z_SIZE) * 2 + lax.rem(x + dx, 2)


def pick_kernel(sources, *refs):
    pieces, out, sems = refs[:-2], refs[-2], refs[-1]
    for (dz, dx), where in sources:

        @pl.when(place_of(2 * dz + dx) == 0)
        def _():
            first, second = pieces[where[0]], pieces[where[1]].at[pl.ds(0, 1)]
            copies = [
                pltpu.make_async_copy(first, out.at[pl.ds(0, 2)], sems.at[0]),
                pltpu.make_async_copy(second, out.at[pl.ds(2, 1)], sems.at[1]),
            ]
            for copy in copies:
                copy.start()
            for copy in copies:
                copy.wait()


def pick_first(known):
    arrays, sources = [], []
    for key, held in known.items():
        sources.append((key, tuple(range(len(arrays), len(arrays) + len(held)))))
        arrays += held
    return pl.pallas_call(
        functools.partial(pick_kernel, sources),
        out_shape=jax.ShapeDtypeStruct((3,) + arrays[0].shape[-2:], F32),
        in_specs=[pl.BlockSpec(memory_space=pl.ANY)] * len(arrays),
        out_specs=pl.BlockSpec(memory_space=pltpu.VMEM),
        scratch_shapes=[pltpu.SemaphoreType.DMA((2,))],
        compiler_params=pltpu.CompilerParams(vmem_limit_bytes=VMEM_BYTES),
    )(*arrays)


def build_reflection(packed):
    width = packed.shape[1]
    rows = lax.broadcasted_iota(jnp.int32, (width, width), 0)
    cols = lax.broadcasted_iota(jnp.int32, (width, width), 1)
    top = packed[:width]
    unit = jnp.where(rows == cols, 1.0, jnp.where(rows > cols, top, 0.0))
    factor = jnp.where(rows <= cols, top, 0.0)
    vectors = jnp.concatenate([unit, packed[width:]], axis=0)
    high, low = split(vectors)
    factor_high, factor_low = split(factor)
    both = dot(jnp.concatenate([high, low], axis=0), factor_high)
    weighted_high, weighted_low = split(
        both[: 2 * width] + (both[2 * width :] + dot(high, factor_low))
    )
    both = dot_transposed(jnp.concatenate([weighted_high, weighted_low], axis=0), high)
    update = both[: 2 * width] + (both[2 * width :] + dot_transposed(weighted_high, low))
    rows = lax.broadcasted_iota(jnp.int32, update.shape, 0)
    cols = lax.broadcasted_iota(jnp.int32, update.shape, 1)
    return split(jnp.where(rows == cols, 1.0, 0.0) - update)


def build_kernel(parts, has_input, *refs):
    pieces = refs[: len(refs) - (6 if has_input else 4)]
    outs = refs[-4:-2]
    staged, sems = refs[-2], refs[-1]
    depth = staged.shape[2]
    copies = []
    at = 0
    for index, (source, blocks, group, place) in enumerate(parts):
        size = len(blocks)
        for block in blocks:
            if isinstance(source, tuple):
                usual, late, late_vec = source
                packed = jnp.where(lax.axis_index("vec") == late_vec, pieces[late][block], pieces[usual][block])
            else:
                packed = pieces[source][block]
            high, low = build_reflection(packed)
            staged[at, :depth] = high
            staged[at, depth:] = low
            at += 1
        first = place(lax.axis_index("vec"))
        copy = pltpu.make_async_copy(
            staged.at[pl.ds(at - size, size)], outs[group].at[pl.ds(first, size)], sems.at[index]
        )
        copy.start()
        copies.append(copy)
    for copy in copies:
        copy.wait()


def build(buffers, shapes, pieces, parts):
    depth = pieces[0].shape[-2]
    blocks = sum(len(part[1]) for part in parts)
    has_input = buffers is not None
    any_spec = pl.BlockSpec(memory_space=pl.ANY)
    return pl.pallas_call(
        functools.partial(build_kernel, parts, has_input),
        out_shape=tuple(jax.ShapeDtypeStruct(shape, BF16) for shape in shapes),
        in_specs=[pl.BlockSpec(memory_space=pltpu.VMEM)] * len(pieces) + ([any_spec] * 2 if has_input else []),
        out_specs=(any_spec, any_spec),
        scratch_shapes=[pltpu.VMEM((blocks, 2 * depth, depth), BF16), pltpu.SemaphoreType.DMA((len(parts),))],
        input_output_aliases={len(pieces): 0, len(pieces) + 1: 1} if has_input else {},
        compiler_params=pltpu.CompilerParams(vmem_limit_bytes=VMEM_BYTES),
        cost_estimate=pl.CostEstimate(
            flops=blocks * 300_000_000, bytes_accessed=blocks * depth * depth * 6, transcendentals=0
        ),
    )(*pieces, *(buffers if has_input else ()))


def placed(source, key, groups=(0, 1), whole=True):
    place = lambda vec: 2 * place_of(2 * key[0] + key[1])
    return [(source, [(group, 0), (group, 1)] if whole else [0, 1], group, place) for group in groups]


def apply(reflection, upper, lower):
    depth = reflection.shape[1]
    high, low = split(jnp.concatenate([upper, lower], axis=0))
    both = dot(reflection, high)
    result = both[:depth] + (both[depth:] + dot(reflection[:depth], low))
    return result[: depth // 2], result[depth // 2 :]


def chunks(total, size=256):
    return [(start, min(size, total - start)) for start in range(0, total, size)]


def first_step(reflection, state, lower, between):
    width, total = state.shape
    for start, size in chunks(total):
        cols = slice(start, start + size)
        below = jnp.zeros((width, size), F32) if lower is None else lower[:, cols]
        top, bottom = apply(reflection, state[:, cols], below)
        between[:, cols] = top
        state[:, cols] = bottom


def second_step(reflection, state, between, out):
    for start, size in chunks(state.shape[1]):
        cols = slice(start, start + size)
        top, bottom = apply(reflection, state[:, cols], between[:, cols])
        if out is not None:
            out[:, cols] = top
        state[:, cols] = bottom


def sweep_copies(first_hbm, second_hbm, data_hbm, tail_hbm, first, second, data, sems):
    granules = first.shape[0] // 2
    rows = 0 if data is None else data.shape[1]

    def first_copies(m):
        copies = [pltpu.make_async_copy(first_hbm.at[pl.ds(2 * m, 2)], first.at[pl.ds(2 * m, 2)], sems.at[0, m])]
        if data is not None:
            is_last = isinstance(m, int) and m == granules - 1
            source = tail_hbm if is_last else data_hbm.at[pl.ds(m * rows, rows)]
            copies.append(pltpu.make_async_copy(source, data.at[m], sems.at[1, m]))
        return copies

    def second_copies(m):
        size = 1 if isinstance(m, int) and 2 * m + 1 >= second.shape[0] else 2
        return [pltpu.make_async_copy(second_hbm.at[pl.ds(2 * m, size)], second.at[pl.ds(2 * m, size)], sems.at[2, m])]

    return first_copies, second_copies


def start_all(copies):
    for copy in copies:
        copy.start()


def wait_all(copies):
    for copy in copies:
        copy.wait()


def run_sweep(first, second, data, first_state, second_state, between, result, out, first_copies, second_copies, sems):
    width = first_state.shape[0]
    granules = first.shape[0] // 2
    blocks = second.shape[0] - 1

    def out_copy(block):
        return pltpu.make_async_copy(
            result.at[pl.ds(block * width, width)], out.at[pl.ds(block * width, width)], sems.at[3, block]
        )

    def rows_of(m, odd):
        return None if data is None else data.at[m, pl.ds(odd * width, width)]

    def finished(block):
        start = block * width
        return result.at[pl.ds(start if isinstance(start, int) else pl.multiple_of(start, width), width)]

    def both_steps(m, odd):
        index = 2 * m + odd - 2
        second_step(second[index], second_state, between, finished(index - 1))
        first_step(first[2 * m + odd], first_state, rows_of(m, odd), between)
        out_copy(index - 1).start()

    wait_all(first_copies(1))
    first_step(first[2], first_state, rows_of(1, 0), between)
    both_steps(1, 1)

    @pl.loop(2, granules - 1)
    def _(m):
        wait_all(first_copies(m))
        wait_all(second_copies(m - 1))
        both_steps(m, 0)
        both_steps(m, 1)

    last = granules - 1
    wait_all(first_copies(last))
    wait_all(second_copies(last - 1))
    both_steps(last, 0)
    both_steps(last, 1)
    wait_all(second_copies(last))
    second_step(second[blocks], second_state, between, finished(blocks - 1))
    out_copy(blocks - 1).start()
    for block in range(blocks):
        out_copy(block).wait()


def unit_kernel(
    first_hbm, second_hbm, data_hbm, out, transition, initial,
    first, second, data, first_state, second_state, between, data_between, result, sems,
):
    width = first_state.shape[0]
    first_copies, second_copies = sweep_copies(first_hbm, second_hbm, None, None, first, second, None, sems)
    granules = first.shape[0] // 2
    is_first = lax.axis_index("row") == 0

    @pl.when(is_first)
    def _():
        rows = pltpu.make_async_copy(data_hbm.at[pl.ds(0, 2 * width)], data, sems.at[1, 0])
        copies = first_copies(0) + second_copies(0) + [rows]
        start_all(copies)
        result[...] = jnp.zeros_like(result)
        transition[...] = jnp.zeros_like(transition)
        initial[...] = jnp.zeros_like(initial)
        cleared = pltpu.make_async_copy(result, out, sems.at[3, 0])
        cleared.start()
        wait_all(copies)
        upper, lower = initial.at[pl.ds(0, width)], initial.at[pl.ds(width, width)]
        first_step(first[0], upper, data.at[pl.ds(0, width)], data_between)
        first_step(first[1], upper, data.at[pl.ds(width, width)], data_between)
        second_step(second[0], lower, data_between, None)
        cleared.wait()

    @pl.when(jnp.logical_not(is_first))
    def _():
        for m in range(granules):
            start_all(first_copies(m) + second_copies(m))
        rows = lax.broadcasted_iota(jnp.int32, (width, width), 0)
        cols = lax.broadcasted_iota(jnp.int32, (width, width), 1)
        eye = jnp.where(rows == cols, 1.0, 0.0)
        zeros = jnp.zeros((width, width), F32)
        first_state[...] = eye
        second_state[...] = jnp.concatenate([zeros, eye], axis=1)
        between[...] = jnp.zeros_like(between)
        initial[...] = jnp.zeros_like(initial)
        wait_all(first_copies(0) + second_copies(0))
        run_sweep(
            first, second, None, first_state, second_state, between, result, out, first_copies, second_copies, sems
        )
        transition[:width] = jnp.concatenate([first_state[...], zeros], axis=1)
        transition[width:] = second_state[...]


def data_kernel(
    first_hbm, second_hbm, data_hbm, tail_hbm, initial, out, own_state, sent_state,
    first, second, data, first_state, second_state, between, result, sems,
):
    width = first_state.shape[0]
    first_copies, second_copies = sweep_copies(
        first_hbm, second_hbm, data_hbm, tail_hbm, first, second, data, sems
    )
    for m in range(first.shape[0] // 2):
        start_all(first_copies(m) + second_copies(m))
    first_state[...] = initial[:width]
    second_state[...] = initial[width:]
    wait_all(first_copies(0) + second_copies(0))
    run_sweep(first, second, data, first_state, second_state, between, result, out, first_copies, second_copies, sems)
    half = own_state.shape[1]
    core = lax.rem(lax.axis_index("row"), 2)
    for target, side in ((own_state, core), (sent_state, 1 - core)):
        cols = pl.ds(pl.multiple_of(side * half, half), half)
        target[:width] = first_state[:, cols]
        target[width:] = second_state[:, cols]


ANY = pl.BlockSpec(memory_space=pl.ANY)
VMEM = pl.BlockSpec(memory_space=pltpu.VMEM)
PARAMS = pltpu.CompilerParams(vmem_limit_bytes=VMEM_BYTES)
CORRECT_PARAMS = pltpu.CompilerParams(vmem_limit_bytes=50 * 2**20)
SMALL_PARAMS = pltpu.CompilerParams(vmem_limit_bytes=16 * 2**20)


def estimate(blocks, depth, cols):
    return pl.CostEstimate(
        flops=6 * blocks * depth * depth * cols, bytes_accessed=30 * 2**20, transcendentals=0
    )


def sweep_units(buffers, data):
    first, second = buffers
    depth = first.shape[2]
    width, blocks, cols = depth // 2, second.shape[0] - 1, data.shape[1]
    return pl.pallas_call(
        unit_kernel,
        out_shape=(
            jax.ShapeDtypeStruct((blocks * width, depth), F32),
            jax.ShapeDtypeStruct((depth, depth), F32),
            jax.ShapeDtypeStruct((depth, cols), F32),
        ),
        in_specs=[ANY] * 3,
        out_specs=(ANY, VMEM, VMEM),
        scratch_shapes=[
            pltpu.VMEM(first.shape, BF16),
            pltpu.VMEM(second.shape, BF16),
            pltpu.VMEM((depth, cols), F32),
            pltpu.VMEM((width, width), F32),
            pltpu.VMEM((width, depth), F32),
            pltpu.VMEM((width, depth), F32),
            pltpu.VMEM((width, cols), F32),
            pltpu.VMEM((blocks * width, depth), F32),
            pltpu.SemaphoreType.DMA((4, blocks)),
        ],
        compiler_params=PARAMS,
        cost_estimate=estimate(blocks, depth, 3 * depth),
    )(first, second, data)


def sweep_data(buffers, data, tail, initial):
    first, second = buffers
    depth = first.shape[2]
    width, blocks, cols = depth // 2, second.shape[0] - 1, data.shape[1]
    return pl.pallas_call(
        data_kernel,
        out_shape=(
            jax.ShapeDtypeStruct((blocks * width, cols), F32),
            jax.ShapeDtypeStruct((depth, cols // 2), F32),
            jax.ShapeDtypeStruct((depth, cols // 2), F32),
        ),
        in_specs=[ANY] * 4 + [VMEM],
        out_specs=(ANY, VMEM, VMEM),
        scratch_shapes=[
            pltpu.VMEM(first.shape, BF16),
            pltpu.VMEM(second.shape, BF16),
            pltpu.VMEM((first.shape[0] // 2, depth, cols), F32),
            pltpu.VMEM((width, cols), F32),
            pltpu.VMEM((width, cols), F32),
            pltpu.VMEM((width, cols), F32),
            pltpu.VMEM((blocks * width, cols), F32),
            pltpu.SemaphoreType.DMA((4, blocks)),
        ],
        compiler_params=PARAMS,
        cost_estimate=estimate(blocks, depth, 2 * cols),
    )(first, second, data, tail, initial)


def small(kernel, outs, *args, scratch=()):
    return pl.pallas_call(
        kernel,
        out_shape=tuple(jax.ShapeDtypeStruct(shape, F32) for shape in outs),
        in_specs=[VMEM] * len(args),
        out_specs=tuple(VMEM for _ in outs),
        scratch_shapes=[pltpu.VMEM(shape, F32) for shape in scratch],
        compiler_params=SMALL_PARAMS,
    )(*args)


def position():
    row = lax.axis_index("row")
    return lax.rem(row, 2), lax.rem(row // 2, Y_SIZE)


def chip_at(d):
    return lax.rem(position()[1] + Y_SIZE - d, Y_SIZE)


def lanes(index, size):
    return pl.ds(pl.multiple_of(index * size, size), size)


def by_core(at_first, otherwise):
    return jnp.where(position()[0] == 0, at_first, otherwise)


def chip_transition_kernel(own, received, out):
    out[...] = dot3(by_core(received[...], own[...]), by_core(own[...], received[...]))


def chip_offset_kernel(own_transition, received_transition, own, received, *refs):
    outs, chip = refs[:-1], refs[-1]
    upper = by_core(received_transition[...], own_transition[...])
    chip[...] = dot3(upper, by_core(own[...], received[...])) + by_core(received[...], own[...])
    size = outs[0].shape[1]
    for d, out in enumerate(outs):
        out[...] = chip[:, lanes(chip_at(Y_SIZE - d), size)]


def products_kernel(*refs):
    transitions, ordered, products = refs[:Y_SIZE], refs[Y_SIZE], refs[Y_SIZE + 1]
    for d, transition in enumerate(transitions):
        ordered[chip_at(d)] = transition[...]
    product = ordered[0]
    products[0] = product
    for at in range(1, Y_SIZE - 1):
        product = dot3(ordered[at], product)
        products[at] = product


def chain_kernel(ordered, *refs):
    offsets, partial, total, placed_offsets = refs[:Y_SIZE], refs[-3], refs[-2], refs[-1]
    for d, offset in enumerate(offsets):
        placed_offsets[chip_at(d)] = offset[...]
    state = placed_offsets[0]
    for at in range(1, Y_SIZE):
        partial[at - 1] = state
        state = dot3(ordered[at], state) + placed_offsets[at]
    total[...] = state


def entering_kernel(entering, products, partial, *refs):
    outs, states = refs[:-1], refs[-1]
    states[0] = entering[...]
    for at in range(1, Y_SIZE):
        states[at] = dot3(products[at - 1], entering[...]) + partial[at - 1]
    for d, out in enumerate(outs):
        out[...] = states[chip_at(Y_SIZE - d)]


def core_kernel(own_transition, received_transition, own, received, *refs):
    arrived, kept, given, chip = refs[:Y_SIZE], refs[-3], refs[-2], refs[-1]
    size = arrived[0].shape[1]
    for d, part in enumerate(arrived):
        chip[:, lanes(chip_at(d), size)] = part[...]
    lower = by_core(own_transition[...], received_transition[...])
    into_second = dot3(lower, chip[...]) + by_core(own[...], received[...])
    kept[...] = by_core(chip[...], into_second)
    given[...] = by_core(into_second, chip[...])


def correct_kernel(tile, rows_hbm, response_hbm, kept, taken, out_hbm, rows, response, incoming_high, incoming_low, sems):
    count = rows.shape[0] // tile

    def span(index):
        return pl.ds(index * tile, tile)

    arrivals = [
        (
            pltpu.make_async_copy(response_hbm.at[span(k)], response.at[span(k)], sems.at[0, k]),
            pltpu.make_async_copy(rows_hbm.at[span(k)], rows.at[span(k)], sems.at[1, k]),
        )
        for k in range(count)
    ]
    for pair in arrivals:
        for copy in pair:
            copy.start()
    core = position()[0]
    for part, side in ((kept, core), (taken, 1 - core)):
        high, low = split(part[...])
        incoming_high[:, lanes(side, part.shape[1])] = high
        incoming_low[:, lanes(side, part.shape[1])] = low
    departures = []
    for k in range(count):
        for copy in arrivals[k]:
            copy.wait()
        high, low = split(response[k * tile : (k + 1) * tile])
        both = jnp.concatenate([high, low], axis=0)
        for start, size in chunks(rows.shape[1], 512):
            at = (slice(k * tile, (k + 1) * tile), slice(start, start + size))
            sums = dot(both, incoming_high[:, at[1]])
            rows[at] = rows[at] + (sums[:tile] + (sums[tile:] + dot(high, incoming_low[:, at[1]])))
        copy = pltpu.make_async_copy(rows.at[span(k)], out_hbm.at[span(k)], sems.at[2, k])
        copy.start()
        departures.append(copy)
    for copy in departures:
        copy.wait()


def correct(rows, response, kept, taken, tile=256):
    incoming = (response.shape[1], rows.shape[1])
    return pl.pallas_call(
        functools.partial(correct_kernel, tile),
        out_shape=jax.ShapeDtypeStruct(rows.shape, F32),
        in_specs=[ANY, ANY, VMEM, VMEM],
        out_specs=ANY,
        scratch_shapes=[
            pltpu.VMEM(rows.shape, F32),
            pltpu.VMEM(response.shape, F32),
            pltpu.VMEM(incoming, BF16),
            pltpu.VMEM(incoming, BF16),
            pltpu.SemaphoreType.DMA((3, rows.shape[0] // tile)),
        ],
        compiler_params=CORRECT_PARAMS,
    )(rows, response, kept, taken)


def local(eigvecs, wy_v, wy_t):
    width = wy_t.shape[-1]
    rows_dev, cols_dev = eigvecs.shape
    own_blocks = rows_dev // width
    below = lax.broadcasted_iota(jnp.int32, (width, width), 0) > lax.broadcasted_iota(
        jnp.int32, (width, width), 1
    )
    own = jnp.concatenate([jnp.where(below, wy_v[:, :, :width], wy_t), wy_v[:, :, width:]], axis=2)
    f00, s00 = own[0], own[1]
    above = eigvecs[: 2 * width]
    depth = 2 * width
    shapes = ((own_blocks + 2, 2 * depth, depth), (own_blocks + 1, 2 * depth, depth))

    def add(buffers, group, pieces, keys):
        parts = []
        for source, key in enumerate(keys):
            parts += placed(source, key, (group,), False)
        return build(buffers, shapes, pieces, parts)

    f01, f30, f10 = across_x(f00), along_z(f00, 1), along_z(f00, -1)
    s01, s30, s10 = across_x(s00), along_z(s00, 1), along_z(s00, -1)
    buffers = build(None, shapes, [f00, s00], placed(0, (0, 0), (0,), False) + placed(1, (0, 0), (1,), False))
    f01, f30, f10, *buffers = together(f01, f30, f10, *buffers)
    f31, f20, f11 = across_x(f30), along_z(f30, 1), along_z(f01, -1)
    buffers = add(buffers, 0, [f01, f30, f10], [(0, 1), (3, 0), (1, 0)])
    s01, s30, s10, *buffers = together(s01, s30, s10, *buffers)
    s31, s20, s11 = across_x(s30), along_z(s30, 1), along_z(s01, -1)
    buffers = add(buffers, 1, [s01, s30, s10], [(0, 1), (3, 0), (1, 0)])
    f31, f20, f11, *buffers = together(f31, f20, f11, *buffers)
    f21 = along_z(f11, -1)
    buffers = add(buffers, 0, [f31, f20, f11], [(3, 1), (2, 0), (1, 1)])
    s31, s20, s11, *buffers = together(s31, s20, s11, *buffers)
    s21 = along_z(s31, 1)
    picked = pick_first(
        {
            (0, 0): [f00, s00],
            (0, 1): [f01, s01],
            (1, 0): [f10, s10],
            (1, 1): [f11, s11],
            (3, 0): [f30, s30],
            (3, 1): [f31, s31],
            (2, 0): [f20, s20],
        }
    )
    vecs, rows = lax.axis_size("vec"), lax.axis_size("row")
    late = 5
    extras = [
        lax.ppermute(
            picked,
            ("row", "vec"),
            [((i + 1) * vecs + v, i * vecs + v) for i in range(rows - 1) for v in range(vecs) if v != late],
        ),
        lax.ppermute(
            picked, ("row", "vec"), [((i + 1) * vecs + late - 1, i * vecs + late) for i in range(rows - 1)]
        ),
    ]
    buffers = add(buffers, 1, [s31, s20, s11], [(3, 1), (2, 0), (1, 1)])
    f21, s21, above, extra, late_extra, *buffers = together(f21, s21, above, *extras, *buffers)
    tail = from_next_row(above)
    buffers = build(
        buffers,
        shapes,
        [f21, s21, extra, late_extra],
        placed(0, (2, 1), (0,), False)
        + placed(1, (2, 1), (1,), False)
        + [((2, 3, late), [0, 1], 0, lambda vec: own_blocks), ((2, 3, late), [2], 1, lambda vec: own_blocks)],
    )

    half, quarter = cols_dev // 2, cols_dev // (2 * Y_SIZE)
    response, transition, initial = sweep_units(buffers, eigvecs)
    received_transition = across_core(transition)
    (chip_transition,) = small(chip_transition_kernel, [(depth, depth)], transition, received_transition)
    chip_transition, *buffers = together(chip_transition, *buffers)
    transitions = [chip_transition] + [along_y(chip_transition, d) for d in range(1, Y_SIZE)]
    swept, own_offset, sent_offset = sweep_data(buffers, eigvecs, tail, initial)
    sent_offset, *transitions = together(sent_offset, *transitions)
    received_offset = across_core(sent_offset)
    cores = (transition, received_transition, own_offset, received_offset)
    offsets = small(chip_offset_kernel, [(depth, quarter)] * Y_SIZE, *cores, scratch=[(depth, half)])
    offsets = [offsets[0]] + [along_y(offsets[d], d) for d in range(1, Y_SIZE)]
    ordered, products = small(
        products_kernel, [(Y_SIZE, depth, depth), (Y_SIZE - 1, depth, depth)], *transitions
    )
    partial, total = small(
        chain_kernel,
        [(Y_SIZE - 1, depth, quarter), (depth, quarter)],
        ordered,
        *offsets,
        scratch=[(Y_SIZE, depth, quarter)],
    )
    entering = lax.ppermute(total, "row", [(i, i + rows // 2) for i in range(rows // 2)])
    back = small(
        entering_kernel,
        [(depth, quarter)] * Y_SIZE,
        entering,
        products,
        partial,
        scratch=[(Y_SIZE, depth, quarter)],
    )
    arrived = [back[0]] + [along_y(back[d], d) for d in range(1, Y_SIZE)]
    kept, given = small(core_kernel, [(depth, half)] * 2, *cores, *arrived, scratch=[(depth, half)])
    return correct(swept, response, kept, across_core(given))


def solution(mesh):
    placed_in = (
        P("row", "vec"),
        P(None, ("row", "vec"), None, None),
        P(None, ("row", "vec"), None, None),
    )
    return jax.shard_map(
        local, mesh=mesh, in_specs=placed_in, out_specs=P("row", "vec"), check_vma=False
    )
```

```python
import functools

import jax
import jax.numpy as jnp
from jax import lax
from jax.experimental import pallas as pl
from jax.experimental.pallas import tpu as pltpu
from jax.sharding import PartitionSpec as P

F32 = jnp.float32
BF16 = jnp.bfloat16
Z_SIZE = 4
Y_SIZE = 4
VMEM_BYTES = 56 * 2**20


def dot(a, b, precision=None):
    return jnp.dot(a, b, precision=precision, preferred_element_type=F32)


def dot_transposed(a, b):
    return lax.dot_general(a, b, (((1,), (1,)), ((), ())), preferred_element_type=F32)


def split(value):
    high = value.astype(BF16)
    return high, (value - high.astype(F32)).astype(BF16)


def dot3(a, b):
    high, low = split(a)
    b_high, b_low = split(b)
    count = a.shape[0]
    both = dot(jnp.concatenate([high, low], axis=0), b_high)
    return both[:count] + (both[count:] + dot(high, b_low))


def along_z(value, by):
    pairs = [(v, ((v // 2 + by) % Z_SIZE) * 2 + v % 2) for v in range(2 * Z_SIZE)]
    return lax.ppermute(value, "vec", pairs)


def across_x(value):
    return lax.ppermute(value, "vec", [(v, v ^ 1) for v in range(2 * Z_SIZE)])


def across_core(value):
    return lax.ppermute(value, "row", [(i, i ^ 1) for i in range(lax.axis_size("row"))])


def along_y(value, by):
    def target(i):
        high, y, core = i // (2 * Y_SIZE), (i // 2) % Y_SIZE, i % 2
        return (high * Y_SIZE + (y + by) % Y_SIZE) * 2 + core

    return lax.ppermute(value, "row", [(i, target(i)) for i in range(lax.axis_size("row"))])


def from_next_row(value):
    return lax.ppermute(value, "row", [(i + 1, i) for i in range(lax.axis_size("row") - 1)])


def together(*values):
    return lax.optimization_barrier(values)


def place_of(index):
    vec = lax.axis_index("vec")
    z, x = vec // 2, vec % 2
    dz, dx = index // 2, index % 2
    return lax.rem(z + dz, Z_SIZE) * 2 + lax.rem(x + dx, 2)


def pick_kernel(keys, cuts, *refs):
    pieces, outs, sems = refs[: len(keys)], refs[len(keys) : -1], refs[-1]
    copies = [
        pltpu.make_async_copy(pieces[keys.index(key)].at[group], out, sems.at[2 + index])
        for index, ((key, group), out) in enumerate(zip(cuts, outs[1:]))
    ]
    for copy in copies:
        copy.start()
    for (dz, dx), piece in zip(keys, pieces):

        @pl.when(place_of(2 * dz + dx) == 0)
        def _():
            chosen = [
                pltpu.make_async_copy(piece.at[0], outs[0].at[pl.ds(0, 2)], sems.at[0]),
                pltpu.make_async_copy(piece.at[1, pl.ds(0, 1)], outs[0].at[pl.ds(2, 1)], sems.at[1]),
            ]
            for copy in chosen:
                copy.start()
            for copy in chosen:
                copy.wait()

    for copy in copies:
        copy.wait()


def pick_first(known, cuts):
    keys = list(known)
    arrays = [known[key] for key in keys]
    tail = arrays[0].shape[-2:]
    return pl.pallas_call(
        functools.partial(pick_kernel, keys, cuts),
        out_shape=tuple(jax.ShapeDtypeStruct((count,) + tail, F32) for count in [3] + [2] * len(cuts)),
        in_specs=[pl.BlockSpec(memory_space=pl.ANY)] * len(arrays),
        out_specs=tuple(pl.BlockSpec(memory_space=pltpu.VMEM) for _ in range(1 + len(cuts))),
        scratch_shapes=[pltpu.SemaphoreType.DMA((2 + len(cuts),))],
        compiler_params=pltpu.CompilerParams(vmem_limit_bytes=16 * 2**20),
    )(*arrays)


def build_reflection(packed):
    width = packed.shape[1]
    rows = lax.broadcasted_iota(jnp.int32, (width, width), 0)
    cols = lax.broadcasted_iota(jnp.int32, (width, width), 1)
    top = packed[:width]
    unit = jnp.where(rows == cols, 1.0, jnp.where(rows > cols, top, 0.0))
    factor = jnp.where(rows <= cols, top, 0.0)
    vectors = jnp.concatenate([unit, packed[width:]], axis=0)
    high, low = split(vectors)
    factor_high, factor_low = split(factor)
    both = dot(jnp.concatenate([high, low], axis=0), factor_high)
    weighted_high, weighted_low = split(
        both[: 2 * width] + (both[2 * width :] + dot(high, factor_low))
    )
    both = dot_transposed(jnp.concatenate([weighted_high, weighted_low], axis=0), high)
    update = both[: 2 * width] + (both[2 * width :] + dot_transposed(weighted_high, low))
    rows = lax.broadcasted_iota(jnp.int32, update.shape, 0)
    cols = lax.broadcasted_iota(jnp.int32, update.shape, 1)
    return split(jnp.where(rows == cols, 1.0, 0.0) - update)


def build_kernel(parts, has_input, *refs):
    pieces = refs[: len(refs) - (6 if has_input else 4)]
    outs = refs[-4:-2]
    staged, sems = refs[-2], refs[-1]
    depth = staged.shape[2]
    copies = []
    at = 0
    for index, (source, blocks, group, place) in enumerate(parts):
        size = len(blocks)
        for block in blocks:
            if isinstance(source, tuple):
                usual, late, late_vec = source
                packed = jnp.where(lax.axis_index("vec") == late_vec, pieces[late][block], pieces[usual][block])
            else:
                packed = pieces[source][block]
            high, low = build_reflection(packed)
            staged[at, :depth] = high
            staged[at, depth:] = low
            at += 1
        first = place(lax.axis_index("vec"))
        copy = pltpu.make_async_copy(
            staged.at[pl.ds(at - size, size)], outs[group].at[pl.ds(first, size)], sems.at[index]
        )
        copy.start()
        copies.append(copy)
    for copy in copies:
        copy.wait()


def build(buffers, shapes, pieces, parts):
    depth = pieces[0].shape[-2]
    blocks = sum(len(part[1]) for part in parts)
    has_input = buffers is not None
    any_spec = pl.BlockSpec(memory_space=pl.ANY)
    return pl.pallas_call(
        functools.partial(build_kernel, parts, has_input),
        out_shape=tuple(jax.ShapeDtypeStruct(shape, BF16) for shape in shapes),
        in_specs=[pl.BlockSpec(memory_space=pltpu.VMEM)] * len(pieces) + ([any_spec] * 2 if has_input else []),
        out_specs=(any_spec, any_spec),
        scratch_shapes=[pltpu.VMEM((blocks, 2 * depth, depth), BF16), pltpu.SemaphoreType.DMA((len(parts),))],
        input_output_aliases={len(pieces): 0, len(pieces) + 1: 1} if has_input else {},
        compiler_params=pltpu.CompilerParams(vmem_limit_bytes=VMEM_BYTES),
        cost_estimate=pl.CostEstimate(
            flops=blocks * 300_000_000, bytes_accessed=blocks * depth * depth * 6, transcendentals=0
        ),
    )(*pieces, *(buffers if has_input else ()))


def placed(source, key, groups=(0, 1), whole=True):
    place = lambda vec: 2 * place_of(2 * key[0] + key[1])
    return [(source, [(group, 0), (group, 1)] if whole else [0, 1], group, place) for group in groups]


def apply(reflection, upper, lower):
    depth = reflection.shape[1]
    high, low = split(jnp.concatenate([upper, lower], axis=0))
    both = dot(reflection, high)
    result = both[:depth] + (both[depth:] + dot(reflection[:depth], low))
    return result[: depth // 2], result[depth // 2 :]


def chunks(total, size=256):
    return [(start, min(size, total - start)) for start in range(0, total, size)]


def first_step(reflection, state, lower, between):
    width, total = state.shape
    for start, size in chunks(total):
        cols = slice(start, start + size)
        below = jnp.zeros((width, size), F32) if lower is None else lower[:, cols]
        top, bottom = apply(reflection, state[:, cols], below)
        between[:, cols] = top
        state[:, cols] = bottom


def second_step(reflection, state, between, out):
    for start, size in chunks(state.shape[1]):
        cols = slice(start, start + size)
        top, bottom = apply(reflection, state[:, cols], between[:, cols])
        if out is not None:
            out[:, cols] = top
        state[:, cols] = bottom


def sweep_copies(first_hbm, second_hbm, data_hbm, tail_hbm, first, second, data, sems):
    granules = first.shape[0] // 2
    rows = 0 if data is None else data.shape[1]

    def first_copies(m):
        copies = [pltpu.make_async_copy(first_hbm.at[pl.ds(2 * m, 2)], first.at[pl.ds(2 * m, 2)], sems.at[0, m])]
        if data is not None:
            is_last = isinstance(m, int) and m == granules - 1
            source = tail_hbm if is_last else data_hbm.at[pl.ds(m * rows, rows)]
            copies.append(pltpu.make_async_copy(source, data.at[m], sems.at[1, m]))
        return copies

    def second_copies(m):
        size = 1 if isinstance(m, int) and 2 * m + 1 >= second.shape[0] else 2
        return [pltpu.make_async_copy(second_hbm.at[pl.ds(2 * m, size)], second.at[pl.ds(2 * m, size)], sems.at[2, m])]

    return first_copies, second_copies


def start_all(copies):
    for copy in copies:
        copy.start()


def wait_all(copies):
    for copy in copies:
        copy.wait()


def run_sweep(first, second, data, first_state, second_state, between, result, out, first_copies, second_copies, sems):
    width = first_state.shape[0]
    granules = first.shape[0] // 2
    blocks = second.shape[0] - 1

    def out_copy(block):
        return pltpu.make_async_copy(
            result.at[pl.ds(block * width, width)], out.at[pl.ds(block * width, width)], sems.at[3, block]
        )

    def rows_of(m, odd):
        return None if data is None else data.at[m, pl.ds(odd * width, width)]

    def finished(block):
        start = block * width
        return result.at[pl.ds(start if isinstance(start, int) else pl.multiple_of(start, width), width)]

    def both_steps(m, odd):
        index = 2 * m + odd - 2
        second_step(second[index], second_state, between, finished(index - 1))
        first_step(first[2 * m + odd], first_state, rows_of(m, odd), between)
        out_copy(index - 1).start()

    wait_all(first_copies(1))
    first_step(first[2], first_state, rows_of(1, 0), between)
    both_steps(1, 1)

    @pl.loop(2, granules - 1)
    def _(m):
        wait_all(first_copies(m))
        wait_all(second_copies(m - 1))
        both_steps(m, 0)
        both_steps(m, 1)

    last = granules - 1
    wait_all(first_copies(last))
    wait_all(second_copies(last - 1))
    both_steps(last, 0)
    both_steps(last, 1)
    wait_all(second_copies(last))
    second_step(second[blocks], second_state, between, finished(blocks - 1))
    out_copy(blocks - 1).start()
    for block in range(blocks):
        out_copy(block).wait()


def unit_kernel(
    first_hbm, second_hbm, data_hbm, out, transition, initial,
    first, second, data, first_state, second_state, between, data_between, result, sems,
):
    width = first_state.shape[0]
    first_copies, second_copies = sweep_copies(first_hbm, second_hbm, None, None, first, second, None, sems)
    granules = first.shape[0] // 2
    is_first = lax.axis_index("row") == 0

    @pl.when(is_first)
    def _():
        rows = pltpu.make_async_copy(data_hbm.at[pl.ds(0, 2 * width)], data, sems.at[1, 0])
        copies = first_copies(0) + second_copies(0) + [rows]
        start_all(copies)
        result[...] = jnp.zeros_like(result)
        transition[...] = jnp.zeros_like(transition)
        initial[...] = jnp.zeros_like(initial)
        cleared = pltpu.make_async_copy(result, out, sems.at[3, 0])
        cleared.start()
        wait_all(copies)
        upper, lower = initial.at[pl.ds(0, width)], initial.at[pl.ds(width, width)]
        first_step(first[0], upper, data.at[pl.ds(0, width)], data_between)
        first_step(first[1], upper, data.at[pl.ds(width, width)], data_between)
        second_step(second[0], lower, data_between, None)
        cleared.wait()

    @pl.when(jnp.logical_not(is_first))
    def _():
        for m in range(granules):
            start_all(first_copies(m) + second_copies(m))
        rows = lax.broadcasted_iota(jnp.int32, (width, width), 0)
        cols = lax.broadcasted_iota(jnp.int32, (width, width), 1)
        eye = jnp.where(rows == cols, 1.0, 0.0)
        zeros = jnp.zeros((width, width), F32)
        first_state[...] = eye
        second_state[...] = jnp.concatenate([zeros, eye], axis=1)
        between[...] = jnp.zeros_like(between)
        initial[...] = jnp.zeros_like(initial)
        wait_all(first_copies(0) + second_copies(0))
        run_sweep(
            first, second, None, first_state, second_state, between, result, out, first_copies, second_copies, sems
        )
        transition[:width] = jnp.concatenate([first_state[...], zeros], axis=1)
        transition[width:] = second_state[...]


def data_kernel(
    first_hbm, second_hbm, data_hbm, tail_hbm, initial, out, own_state, sent_state,
    first, second, data, first_state, second_state, between, result, sems,
):
    width = first_state.shape[0]
    first_copies, second_copies = sweep_copies(
        first_hbm, second_hbm, data_hbm, tail_hbm, first, second, data, sems
    )
    for m in range(first.shape[0] // 2):
        start_all(first_copies(m) + second_copies(m))
    first_state[...] = initial[:width]
    second_state[...] = initial[width:]
    wait_all(first_copies(0) + second_copies(0))
    run_sweep(first, second, data, first_state, second_state, between, result, out, first_copies, second_copies, sems)
    half = own_state.shape[1]
    core = lax.rem(lax.axis_index("row"), 2)
    for target, side in ((own_state, core), (sent_state, 1 - core)):
        cols = pl.ds(pl.multiple_of(side * half, half), half)
        target[:width] = first_state[:, cols]
        target[width:] = second_state[:, cols]


ANY = pl.BlockSpec(memory_space=pl.ANY)
VMEM = pl.BlockSpec(memory_space=pltpu.VMEM)
PARAMS = pltpu.CompilerParams(vmem_limit_bytes=VMEM_BYTES)
CORRECT_PARAMS = pltpu.CompilerParams(vmem_limit_bytes=50 * 2**20)
SMALL_PARAMS = pltpu.CompilerParams(vmem_limit_bytes=16 * 2**20)


def estimate(blocks, depth, cols):
    return pl.CostEstimate(
        flops=6 * blocks * depth * depth * cols, bytes_accessed=30 * 2**20, transcendentals=0
    )


def sweep_units(buffers, data):
    first, second = buffers
    depth = first.shape[2]
    width, blocks, cols = depth // 2, second.shape[0] - 1, data.shape[1]
    return pl.pallas_call(
        unit_kernel,
        out_shape=(
            jax.ShapeDtypeStruct((blocks * width, depth), F32),
            jax.ShapeDtypeStruct((depth, depth), F32),
            jax.ShapeDtypeStruct((depth, cols), F32),
        ),
        in_specs=[ANY] * 3,
        out_specs=(ANY, VMEM, VMEM),
        scratch_shapes=[
            pltpu.VMEM(first.shape, BF16),
            pltpu.VMEM(second.shape, BF16),
            pltpu.VMEM((depth, cols), F32),
            pltpu.VMEM((width, width), F32),
            pltpu.VMEM((width, depth), F32),
            pltpu.VMEM((width, depth), F32),
            pltpu.VMEM((width, cols), F32),
            pltpu.VMEM((blocks * width, depth), F32),
            pltpu.SemaphoreType.DMA((4, blocks)),
        ],
        compiler_params=PARAMS,
        cost_estimate=estimate(blocks, depth, 3 * depth),
    )(first, second, data)


def sweep_data(buffers, data, tail, initial):
    first, second = buffers
    depth = first.shape[2]
    width, blocks, cols = depth // 2, second.shape[0] - 1, data.shape[1]
    return pl.pallas_call(
        data_kernel,
        out_shape=(
            jax.ShapeDtypeStruct((blocks * width, cols), F32),
            jax.ShapeDtypeStruct((depth, cols // 2), F32),
            jax.ShapeDtypeStruct((depth, cols // 2), F32),
        ),
        in_specs=[ANY] * 4 + [VMEM],
        out_specs=(ANY, VMEM, VMEM),
        scratch_shapes=[
            pltpu.VMEM(first.shape, BF16),
            pltpu.VMEM(second.shape, BF16),
            pltpu.VMEM((first.shape[0] // 2, depth, cols), F32),
            pltpu.VMEM((width, cols), F32),
            pltpu.VMEM((width, cols), F32),
            pltpu.VMEM((width, cols), F32),
            pltpu.VMEM((blocks * width, cols), F32),
            pltpu.SemaphoreType.DMA((4, blocks)),
        ],
        compiler_params=PARAMS,
        cost_estimate=estimate(blocks, depth, 2 * cols),
    )(first, second, data, tail, initial)


def small(kernel, outs, *args, scratch=()):
    return pl.pallas_call(
        kernel,
        out_shape=tuple(jax.ShapeDtypeStruct(shape, F32) for shape in outs),
        in_specs=[VMEM] * len(args),
        out_specs=tuple(VMEM for _ in outs),
        scratch_shapes=[pltpu.VMEM(shape, F32) for shape in scratch],
        compiler_params=SMALL_PARAMS,
    )(*args)


def position():
    row = lax.axis_index("row")
    return lax.rem(row, 2), lax.rem(row // 2, Y_SIZE)


def chip_at(d):
    return lax.rem(position()[1] + Y_SIZE - d, Y_SIZE)


def lanes(index, size):
    return pl.ds(pl.multiple_of(index * size, size), size)


def by_core(at_first, otherwise):
    return jnp.where(position()[0] == 0, at_first, otherwise)


def chip_transition_kernel(own, received, out):
    out[...] = dot3(by_core(received[...], own[...]), by_core(own[...], received[...]))


def chip_offset_kernel(own_transition, received_transition, own, received, *refs):
    outs, chip = refs[:-1], refs[-1]
    upper = by_core(received_transition[...], own_transition[...])
    chip[...] = dot3(upper, by_core(own[...], received[...])) + by_core(received[...], own[...])
    size = outs[0].shape[1]
    for d, out in enumerate(outs):
        out[...] = chip[:, lanes(chip_at(Y_SIZE - d), size)]


def products_kernel(*refs):
    transitions, ordered, products = refs[:Y_SIZE], refs[Y_SIZE], refs[Y_SIZE + 1]
    for d, transition in enumerate(transitions):
        ordered[chip_at(d)] = transition[...]
    product = ordered[0]
    products[0] = product
    for at in range(1, Y_SIZE - 1):
        product = dot3(ordered[at], product)
        products[at] = product


def chain_kernel(ordered, *refs):
    offsets, partial, total, placed_offsets = refs[:Y_SIZE], refs[-3], refs[-2], refs[-1]
    for d, offset in enumerate(offsets):
        placed_offsets[chip_at(d)] = offset[...]
    state = placed_offsets[0]
    for at in range(1, Y_SIZE):
        partial[at - 1] = state
        state = dot3(ordered[at], state) + placed_offsets[at]
    total[...] = state


def entering_kernel(entering, products, partial, *refs):
    outs, states = refs[:-1], refs[-1]
    states[0] = entering[...]
    for at in range(1, Y_SIZE):
        states[at] = dot3(products[at - 1], entering[...]) + partial[at - 1]
    for d, out in enumerate(outs):
        out[...] = states[chip_at(Y_SIZE - d)]


def core_kernel(own_transition, received_transition, own, received, *refs):
    arrived, kept, given, chip = refs[:Y_SIZE], refs[-3], refs[-2], refs[-1]
    size = arrived[0].shape[1]
    for d, part in enumerate(arrived):
        chip[:, lanes(chip_at(d), size)] = part[...]
    lower = by_core(own_transition[...], received_transition[...])
    into_second = dot3(lower, chip[...]) + by_core(own[...], received[...])
    kept[...] = by_core(chip[...], into_second)
    given[...] = by_core(into_second, chip[...])


def correct_kernel(tile, rows_hbm, response_hbm, kept, taken, out_hbm, rows, response, incoming_high, incoming_low, sems):
    count = rows.shape[0] // tile

    def span(index):
        return pl.ds(index * tile, tile)

    arrivals = [
        (
            pltpu.make_async_copy(response_hbm.at[span(k)], response.at[span(k)], sems.at[0, k]),
            pltpu.make_async_copy(rows_hbm.at[span(k)], rows.at[span(k)], sems.at[1, k]),
        )
        for k in range(count)
    ]
    for pair in arrivals:
        for copy in pair:
            copy.start()
    core = position()[0]
    for part, side in ((kept, core), (taken, 1 - core)):
        high, low = split(part[...])
        incoming_high[:, lanes(side, part.shape[1])] = high
        incoming_low[:, lanes(side, part.shape[1])] = low
    departures = []
    for k in range(count):
        for copy in arrivals[k]:
            copy.wait()
        high, low = split(response[k * tile : (k + 1) * tile])
        both = jnp.concatenate([high, low], axis=0)
        for start, size in chunks(rows.shape[1], 512):
            at = (slice(k * tile, (k + 1) * tile), slice(start, start + size))
            sums = dot(both, incoming_high[:, at[1]])
            rows[at] = rows[at] + (sums[:tile] + (sums[tile:] + dot(high, incoming_low[:, at[1]])))
        copy = pltpu.make_async_copy(rows.at[span(k)], out_hbm.at[span(k)], sems.at[2, k])
        copy.start()
        departures.append(copy)
    for copy in departures:
        copy.wait()


def correct(rows, response, kept, taken, tile=256):
    incoming = (response.shape[1], rows.shape[1])
    return pl.pallas_call(
        functools.partial(correct_kernel, tile),
        out_shape=jax.ShapeDtypeStruct(rows.shape, F32),
        in_specs=[ANY, ANY, VMEM, VMEM],
        out_specs=ANY,
        scratch_shapes=[
            pltpu.VMEM(rows.shape, F32),
            pltpu.VMEM(response.shape, F32),
            pltpu.VMEM(incoming, BF16),
            pltpu.VMEM(incoming, BF16),
            pltpu.SemaphoreType.DMA((3, rows.shape[0] // tile)),
        ],
        compiler_params=CORRECT_PARAMS,
    )(rows, response, kept, taken)


def local(eigvecs, wy_v, wy_t):
    width = wy_t.shape[-1]
    rows_dev, cols_dev = eigvecs.shape
    own_blocks = rows_dev // width
    below = lax.broadcasted_iota(jnp.int32, (width, width), 0) > lax.broadcasted_iota(
        jnp.int32, (width, width), 1
    )
    own = jnp.concatenate([jnp.where(below, wy_v[:, :, :width], wy_t), wy_v[:, :, width:]], axis=2)
    above = eigvecs[: 2 * width]
    depth = 2 * width
    shapes = ((own_blocks + 2, 2 * depth, depth), (own_blocks + 1, 2 * depth, depth))

    def add(buffers, pieces, keys):
        parts = []
        for source, key in enumerate(keys):
            parts += placed(source, key)
        return build(buffers, shapes, pieces, parts)

    p01, p30, p10 = across_x(own), along_z(own, 1), along_z(own, -1)
    buffers = add(None, [own], [(0, 0)])
    p01, p30, p10, *buffers = together(p01, p30, p10, *buffers)
    p31, p20, p11 = across_x(p30), along_z(p30, 1), along_z(p01, -1)
    buffers = add(buffers, [p01, p30, p10], [(0, 1), (3, 0), (1, 0)])
    p31, p20, p11, *buffers = together(p31, p20, p11, *buffers)
    known = {(0, 0): own, (0, 1): p01, (3, 0): p30, (1, 0): p10, (3, 1): p31, (2, 0): p20, (1, 1): p11}
    picked, f11, s31 = pick_first(known, [((1, 1), 0), ((3, 1), 1)])
    f21, s21 = along_z(f11, -1), along_z(s31, 1)
    vecs, rows = lax.axis_size("vec"), lax.axis_size("row")
    late = 5
    extra = lax.ppermute(
        picked,
        ("row", "vec"),
        [((i + 1) * vecs + v, i * vecs + v) for i in range(rows - 1) for v in range(vecs) if v != late],
    )
    late_extra = lax.ppermute(
        picked, ("row", "vec"), [((i + 1) * vecs + late - 1, i * vecs + late) for i in range(rows - 1)]
    )
    buffers = add(buffers, [p31, p20, p11], [(3, 1), (2, 0), (1, 1)])
    f21, s21, above, extra, late_extra, *buffers = together(f21, s21, above, extra, late_extra, *buffers)
    tail = from_next_row(above)
    buffers = build(
        buffers,
        shapes,
        [f21, s21, extra, late_extra],
        placed(0, (2, 1), (0,), False)
        + placed(1, (2, 1), (1,), False)
        + [((2, 3, late), [0, 1], 0, lambda vec: own_blocks), ((2, 3, late), [2], 1, lambda vec: own_blocks)],
    )

    half, quarter = cols_dev // 2, cols_dev // (2 * Y_SIZE)
    response, transition, initial = sweep_units(buffers, eigvecs)
    received_transition = across_core(transition)
    (chip_transition,) = small(chip_transition_kernel, [(depth, depth)], transition, received_transition)
    chip_transition, *buffers = together(chip_transition, *buffers)
    transitions = [chip_transition] + [along_y(chip_transition, d) for d in range(1, Y_SIZE)]
    swept, own_offset, sent_offset = sweep_data(buffers, eigvecs, tail, initial)
    sent_offset, *transitions = together(sent_offset, *transitions)
    received_offset = across_core(sent_offset)
    cores = (transition, received_transition, own_offset, received_offset)
    offsets = small(chip_offset_kernel, [(depth, quarter)] * Y_SIZE, *cores, scratch=[(depth, half)])
    offsets = [offsets[0]] + [along_y(offsets[d], d) for d in range(1, Y_SIZE)]
    ordered, products = small(
        products_kernel, [(Y_SIZE, depth, depth), (Y_SIZE - 1, depth, depth)], *transitions
    )
    partial, total = small(
        chain_kernel,
        [(Y_SIZE - 1, depth, quarter), (depth, quarter)],
        ordered,
        *offsets,
        scratch=[(Y_SIZE, depth, quarter)],
    )
    entering = lax.ppermute(total, "row", [(i, i + rows // 2) for i in range(rows // 2)])
    back = small(
        entering_kernel,
        [(depth, quarter)] * Y_SIZE,
        entering,
        products,
        partial,
        scratch=[(Y_SIZE, depth, quarter)],
    )
    arrived = [back[0]] + [along_y(back[d], d) for d in range(1, Y_SIZE)]
    kept, given = small(core_kernel, [(depth, half)] * 2, *cores, *arrived, scratch=[(depth, half)])
    return correct(swept, response, kept, across_core(given))


def solution(mesh):
    placed_in = (
        P("row", "vec"),
        P(None, ("row", "vec"), None, None),
        P(None, ("row", "vec"), None, None),
    )
    return jax.shard_map(
        local, mesh=mesh, in_specs=placed_in, out_specs=P("row", "vec"), check_vma=False
    )
```

```python
import functools

import jax
import jax.numpy as jnp
from jax import lax
from jax.experimental import pallas as pl
from jax.experimental.pallas import tpu as pltpu
from jax.sharding import PartitionSpec as P

F32 = jnp.float32
BF16 = jnp.bfloat16
Z_SIZE = 4
Y_SIZE = 4
VMEM_BYTES = 56 * 2**20


def dot(a, b, precision=None):
    return jnp.dot(a, b, precision=precision, preferred_element_type=F32)


def dot_transposed(a, b):
    return lax.dot_general(a, b, (((1,), (1,)), ((), ())), preferred_element_type=F32)


def split(value):
    high = value.astype(BF16)
    return high, (value - high.astype(F32)).astype(BF16)


def dot3(a, b):
    high, low = split(a)
    b_high, b_low = split(b)
    count = a.shape[0]
    both = dot(jnp.concatenate([high, low], axis=0), b_high)
    return both[:count] + (both[count:] + dot(high, b_low))


def along_z(value, by):
    pairs = [(v, ((v // 2 + by) % Z_SIZE) * 2 + v % 2) for v in range(2 * Z_SIZE)]
    return lax.ppermute(value, "vec", pairs)


def across_x(value):
    return lax.ppermute(value, "vec", [(v, v ^ 1) for v in range(2 * Z_SIZE)])


def across_core(value):
    return lax.ppermute(value, "row", [(i, i ^ 1) for i in range(lax.axis_size("row"))])


def along_y(value, by):
    def target(i):
        high, y, core = i // (2 * Y_SIZE), (i // 2) % Y_SIZE, i % 2
        return (high * Y_SIZE + (y + by) % Y_SIZE) * 2 + core

    return lax.ppermute(value, "row", [(i, target(i)) for i in range(lax.axis_size("row"))])


def from_next_row(value):
    return lax.ppermute(value, "row", [(i + 1, i) for i in range(lax.axis_size("row") - 1)])


def together(*values):
    return lax.optimization_barrier(values)


def place_of(index):
    vec = lax.axis_index("vec")
    z, x = vec // 2, vec % 2
    dz, dx = index // 2, index % 2
    return lax.rem(z + dz, Z_SIZE) * 2 + lax.rem(x + dx, 2)


def pick_kernel(sources, rows, *refs):
    pieces, out, above, sems = refs[:-3], refs[-3], refs[-2], refs[-1]
    head = pltpu.make_async_copy(rows.at[pl.ds(0, above.shape[0])], above, sems.at[2])
    head.start()
    for (dz, dx), (first, second) in sources:

        @pl.when(place_of(2 * dz + dx) == 0)
        def _():
            copies = [
                pltpu.make_async_copy(pieces[first], out.at[pl.ds(0, 2)], sems.at[0]),
                pltpu.make_async_copy(pieces[second].at[pl.ds(0, 1)], out.at[pl.ds(2, 1)], sems.at[1]),
            ]
            for copy in copies:
                copy.start()
            for copy in copies:
                copy.wait()

    head.wait()


def pick_first(rows, known):
    arrays, sources = [], []
    for key, held in known.items():
        sources.append((key, (len(arrays), len(arrays) + 1)))
        arrays += held
    depth, width = arrays[0].shape[-2:]
    return pl.pallas_call(
        functools.partial(pick_kernel, sources),
        out_shape=(
            jax.ShapeDtypeStruct((3, depth, width), F32),
            jax.ShapeDtypeStruct((depth, rows.shape[1]), F32),
        ),
        in_specs=[pl.BlockSpec(memory_space=pl.ANY)] * (1 + len(arrays)),
        out_specs=(pl.BlockSpec(memory_space=pltpu.VMEM),) * 2,
        scratch_shapes=[pltpu.SemaphoreType.DMA((3,))],
        compiler_params=pltpu.CompilerParams(vmem_limit_bytes=VMEM_BYTES),
    )(rows, *arrays)


def build_reflection(packed):
    width = packed.shape[1]
    rows = lax.broadcasted_iota(jnp.int32, (width, width), 0)
    cols = lax.broadcasted_iota(jnp.int32, (width, width), 1)
    top = packed[:width]
    unit = jnp.where(rows == cols, 1.0, jnp.where(rows > cols, top, 0.0))
    factor = jnp.where(rows <= cols, top, 0.0)
    vectors = jnp.concatenate([unit, packed[width:]], axis=0)
    high, low = split(vectors)
    factor_high, factor_low = split(factor)
    both = dot(jnp.concatenate([high, low], axis=0), factor_high)
    weighted_high, weighted_low = split(
        both[: 2 * width] + (both[2 * width :] + dot(high, factor_low))
    )
    both = dot_transposed(jnp.concatenate([weighted_high, weighted_low], axis=0), high)
    update = both[: 2 * width] + (both[2 * width :] + dot_transposed(weighted_high, low))
    rows = lax.broadcasted_iota(jnp.int32, update.shape, 0)
    cols = lax.broadcasted_iota(jnp.int32, update.shape, 1)
    return split(jnp.where(rows == cols, 1.0, 0.0) - update)


def build_kernel(parts, has_input, *refs):
    pieces = refs[: len(refs) - (6 if has_input else 4)]
    outs = refs[-4:-2]
    staged, sems = refs[-2], refs[-1]
    depth = staged.shape[2]
    copies = []
    at = 0
    for index, (source, blocks, group, place) in enumerate(parts):
        size = len(blocks)
        for block in blocks:
            if isinstance(source, tuple):
                usual, late, late_vec = source
                packed = jnp.where(lax.axis_index("vec") == late_vec, pieces[late][block], pieces[usual][block])
            else:
                packed = pieces[source][block]
            high, low = build_reflection(packed)
            staged[at, :depth] = high
            staged[at, depth:] = low
            at += 1
        first = place(lax.axis_index("vec"))
        copy = pltpu.make_async_copy(
            staged.at[pl.ds(at - size, size)], outs[group].at[pl.ds(first, size)], sems.at[index]
        )
        copy.start()
        copies.append(copy)
    for copy in copies:
        copy.wait()


def build(buffers, shapes, pieces, parts):
    depth = pieces[0].shape[-2]
    blocks = sum(len(part[1]) for part in parts)
    has_input = buffers is not None
    any_spec = pl.BlockSpec(memory_space=pl.ANY)
    return pl.pallas_call(
        functools.partial(build_kernel, parts, has_input),
        out_shape=tuple(jax.ShapeDtypeStruct(shape, BF16) for shape in shapes),
        in_specs=[pl.BlockSpec(memory_space=pltpu.VMEM)] * len(pieces) + ([any_spec] * 2 if has_input else []),
        out_specs=(any_spec, any_spec),
        scratch_shapes=[pltpu.VMEM((blocks, 2 * depth, depth), BF16), pltpu.SemaphoreType.DMA((len(parts),))],
        input_output_aliases={len(pieces): 0, len(pieces) + 1: 1} if has_input else {},
        compiler_params=pltpu.CompilerParams(vmem_limit_bytes=VMEM_BYTES),
        cost_estimate=pl.CostEstimate(
            flops=blocks * 300_000_000, bytes_accessed=blocks * depth * depth * 6, transcendentals=0
        ),
    )(*pieces, *(buffers if has_input else ()))


def placed(source, key, groups=(0, 1), whole=True):
    place = lambda vec: 2 * place_of(2 * key[0] + key[1])
    return [(source, [(group, 0), (group, 1)] if whole else [0, 1], group, place) for group in groups]


def apply(reflection, upper, lower):
    depth = reflection.shape[1]
    high, low = split(jnp.concatenate([upper, lower], axis=0))
    both = dot(reflection, high)
    result = both[:depth] + (both[depth:] + dot(reflection[:depth], low))
    return result[: depth // 2], result[depth // 2 :]


def chunks(total, size=256):
    return [(start, min(size, total - start)) for start in range(0, total, size)]


def first_step(reflection, state, lower, between):
    width, total = state.shape
    for start, size in chunks(total):
        cols = slice(start, start + size)
        below = jnp.zeros((width, size), F32) if lower is None else lower[:, cols]
        top, bottom = apply(reflection, state[:, cols], below)
        between[:, cols] = top
        state[:, cols] = bottom


def second_step(reflection, state, between, out):
    for start, size in chunks(state.shape[1]):
        cols = slice(start, start + size)
        top, bottom = apply(reflection, state[:, cols], between[:, cols])
        if out is not None:
            out[:, cols] = top
        state[:, cols] = bottom


def sweep_copies(first_hbm, second_hbm, data_hbm, tail_hbm, first, second, data, sems):
    granules = first.shape[0] // 2
    rows = 0 if data is None else data.shape[1]

    def first_copies(m):
        copies = [pltpu.make_async_copy(first_hbm.at[pl.ds(2 * m, 2)], first.at[pl.ds(2 * m, 2)], sems.at[0, m])]
        if data is not None:
            is_last = isinstance(m, int) and m == granules - 1
            source = tail_hbm if is_last else data_hbm.at[pl.ds(m * rows, rows)]
            copies.append(pltpu.make_async_copy(source, data.at[m], sems.at[1, m]))
        return copies

    def second_copies(m):
        size = 1 if isinstance(m, int) and 2 * m + 1 >= second.shape[0] else 2
        return [pltpu.make_async_copy(second_hbm.at[pl.ds(2 * m, size)], second.at[pl.ds(2 * m, size)], sems.at[2, m])]

    return first_copies, second_copies


def start_all(copies):
    for copy in copies:
        copy.start()


def wait_all(copies):
    for copy in copies:
        copy.wait()


def run_sweep(first, second, data, first_state, second_state, between, result, out, first_copies, second_copies, sems):
    width = first_state.shape[0]
    granules = first.shape[0] // 2
    blocks = second.shape[0] - 1

    def out_copy(block):
        return pltpu.make_async_copy(
            result.at[pl.ds(block * width, width)], out.at[pl.ds(block * width, width)], sems.at[3, block]
        )

    def rows_of(m, odd):
        return None if data is None else data.at[m, pl.ds(odd * width, width)]

    def finished(block):
        start = block * width
        return result.at[pl.ds(start if isinstance(start, int) else pl.multiple_of(start, width), width)]

    def both_steps(m, odd):
        index = 2 * m + odd - 2
        second_step(second[index], second_state, between, finished(index - 1))
        first_step(first[2 * m + odd], first_state, rows_of(m, odd), between)
        out_copy(index - 1).start()

    wait_all(first_copies(1))
    first_step(first[2], first_state, rows_of(1, 0), between)
    both_steps(1, 1)

    @pl.loop(2, granules - 1)
    def _(m):
        wait_all(first_copies(m))
        wait_all(second_copies(m - 1))
        both_steps(m, 0)
        both_steps(m, 1)

    last = granules - 1
    wait_all(first_copies(last))
    wait_all(second_copies(last - 1))
    both_steps(last, 0)
    both_steps(last, 1)
    wait_all(second_copies(last))
    second_step(second[blocks], second_state, between, finished(blocks - 1))
    out_copy(blocks - 1).start()
    for block in range(blocks):
        out_copy(block).wait()


def unit_kernel(
    first_hbm, second_hbm, data_hbm, out, transition, initial,
    first, second, data, first_state, second_state, between, data_between, result, sems,
):
    width = first_state.shape[0]
    first_copies, second_copies = sweep_copies(first_hbm, second_hbm, None, None, first, second, None, sems)
    granules = first.shape[0] // 2
    is_first = lax.axis_index("row") == 0

    @pl.when(is_first)
    def _():
        rows = pltpu.make_async_copy(data_hbm.at[pl.ds(0, 2 * width)], data, sems.at[1, 0])
        copies = first_copies(0) + second_copies(0) + [rows]
        start_all(copies)
        result[...] = jnp.zeros_like(result)
        transition[...] = jnp.zeros_like(transition)
        initial[...] = jnp.zeros_like(initial)
        cleared = pltpu.make_async_copy(result, out, sems.at[3, 0])
        cleared.start()
        wait_all(copies)
        upper, lower = initial.at[pl.ds(0, width)], initial.at[pl.ds(width, width)]
        first_step(first[0], upper, data.at[pl.ds(0, width)], data_between)
        first_step(first[1], upper, data.at[pl.ds(width, width)], data_between)
        second_step(second[0], lower, data_between, None)
        cleared.wait()

    @pl.when(jnp.logical_not(is_first))
    def _():
        for m in range(1, granules):
            start_all(first_copies(m) + second_copies(m - 1))
        start_all(second_copies(granules - 1))
        rows = lax.broadcasted_iota(jnp.int32, (width, width), 0)
        cols = lax.broadcasted_iota(jnp.int32, (width, width), 1)
        eye = jnp.where(rows == cols, 1.0, 0.0)
        zeros = jnp.zeros((width, width), F32)
        first_state[...] = eye
        second_state[...] = jnp.concatenate([zeros, eye], axis=1)
        between[...] = jnp.zeros_like(between)
        initial[...] = jnp.zeros_like(initial)
        wait_all(second_copies(0))
        run_sweep(
            first, second, None, first_state, second_state, between, result, out, first_copies, second_copies, sems
        )
        transition[:width] = jnp.concatenate([first_state[...], zeros], axis=1)
        transition[width:] = second_state[...]


def data_kernel(
    first_hbm, second_hbm, data_hbm, tail_hbm, initial, out, own_state, sent_state,
    first, second, data, first_state, second_state, between, result, sems,
):
    width = first_state.shape[0]
    first_copies, second_copies = sweep_copies(
        first_hbm, second_hbm, data_hbm, tail_hbm, first, second, data, sems
    )
    granules = first.shape[0] // 2
    for m in range(1, granules):
        start_all(first_copies(m) + second_copies(m - 1))
    start_all(second_copies(granules - 1))
    first_state[...] = initial[:width]
    second_state[...] = initial[width:]
    wait_all(second_copies(0))
    run_sweep(first, second, data, first_state, second_state, between, result, out, first_copies, second_copies, sems)
    half = own_state.shape[1]
    core = lax.rem(lax.axis_index("row"), 2)
    for target, side in ((own_state, core), (sent_state, 1 - core)):
        cols = pl.ds(pl.multiple_of(side * half, half), half)
        target[:width] = first_state[:, cols]
        target[width:] = second_state[:, cols]


ANY = pl.BlockSpec(memory_space=pl.ANY)
VMEM = pl.BlockSpec(memory_space=pltpu.VMEM)
PARAMS = pltpu.CompilerParams(vmem_limit_bytes=VMEM_BYTES)
CORRECT_PARAMS = pltpu.CompilerParams(vmem_limit_bytes=50 * 2**20)
SMALL_PARAMS = pltpu.CompilerParams(vmem_limit_bytes=16 * 2**20)


def estimate(blocks, depth, cols):
    return pl.CostEstimate(
        flops=6 * blocks * depth * depth * cols, bytes_accessed=30 * 2**20, transcendentals=0
    )


def sweep_units(buffers, data):
    first, second = buffers
    depth = first.shape[2]
    width, blocks, cols = depth // 2, second.shape[0] - 1, data.shape[1]
    return pl.pallas_call(
        unit_kernel,
        out_shape=(
            jax.ShapeDtypeStruct((blocks * width, depth), F32),
            jax.ShapeDtypeStruct((depth, depth), F32),
            jax.ShapeDtypeStruct((depth, cols), F32),
        ),
        in_specs=[ANY] * 3,
        out_specs=(ANY, VMEM, VMEM),
        scratch_shapes=[
            pltpu.VMEM(first.shape, BF16),
            pltpu.VMEM(second.shape, BF16),
            pltpu.VMEM((depth, cols), F32),
            pltpu.VMEM((width, width), F32),
            pltpu.VMEM((width, depth), F32),
            pltpu.VMEM((width, depth), F32),
            pltpu.VMEM((width, cols), F32),
            pltpu.VMEM((blocks * width, depth), F32),
            pltpu.SemaphoreType.DMA((4, blocks)),
        ],
        compiler_params=pltpu.CompilerParams(vmem_limit_bytes=50 * 2**20),
        cost_estimate=estimate(blocks, depth, 3 * depth),
    )(first, second, data)


def sweep_data(buffers, data, tail, initial):
    first, second = buffers
    depth = first.shape[2]
    width, blocks, cols = depth // 2, second.shape[0] - 1, data.shape[1]
    return pl.pallas_call(
        data_kernel,
        out_shape=(
            jax.ShapeDtypeStruct((blocks * width, cols), F32),
            jax.ShapeDtypeStruct((depth, cols // 2), F32),
            jax.ShapeDtypeStruct((depth, cols // 2), F32),
        ),
        in_specs=[ANY] * 4 + [VMEM],
        out_specs=(ANY, VMEM, VMEM),
        scratch_shapes=[
            pltpu.VMEM(first.shape, BF16),
            pltpu.VMEM(second.shape, BF16),
            pltpu.VMEM((first.shape[0] // 2, depth, cols), F32),
            pltpu.VMEM((width, cols), F32),
            pltpu.VMEM((width, cols), F32),
            pltpu.VMEM((width, cols), F32),
            pltpu.VMEM((blocks * width, cols), F32),
            pltpu.SemaphoreType.DMA((4, blocks)),
        ],
        compiler_params=pltpu.CompilerParams(vmem_limit_bytes=50 * 2**20),
        cost_estimate=estimate(blocks, depth, 2 * cols),
    )(first, second, data, tail, initial)


def small(kernel, outs, *args, scratch=()):
    return pl.pallas_call(
        kernel,
        out_shape=tuple(jax.ShapeDtypeStruct(shape, F32) for shape in outs),
        in_specs=[VMEM] * len(args),
        out_specs=tuple(VMEM for _ in outs),
        scratch_shapes=[pltpu.VMEM(shape, F32) for shape in scratch],
        compiler_params=SMALL_PARAMS,
    )(*args)


def position():
    row = lax.axis_index("row")
    return lax.rem(row, 2), lax.rem(row // 2, Y_SIZE)


def chip_at(d):
    return lax.rem(position()[1] + Y_SIZE - d, Y_SIZE)


def lanes(index, size):
    return pl.ds(pl.multiple_of(index * size, size), size)


def by_core(at_first, otherwise):
    return jnp.where(position()[0] == 0, at_first, otherwise)


def chip_transition_kernel(own, received, out):
    out[...] = dot3(by_core(received[...], own[...]), by_core(own[...], received[...]))


def chip_offset_kernel(own_transition, received_transition, own, received, *refs):
    outs, chip = refs[:-1], refs[-1]
    upper = by_core(received_transition[...], own_transition[...])
    chip[...] = dot3(upper, by_core(own[...], received[...])) + by_core(received[...], own[...])
    size = outs[0].shape[1]
    for d, out in enumerate(outs):
        out[...] = chip[:, lanes(chip_at(Y_SIZE - d), size)]


def products_kernel(*refs):
    transitions, ordered, products = refs[:Y_SIZE], refs[Y_SIZE], refs[Y_SIZE + 1]
    for d, transition in enumerate(transitions):
        ordered[chip_at(d)] = transition[...]
    product = ordered[0]
    products[0] = product
    for at in range(1, Y_SIZE - 1):
        product = dot3(ordered[at], product)
        products[at] = product


def chain_kernel(ordered, *refs):
    offsets, partial, total, placed_offsets = refs[:Y_SIZE], refs[-3], refs[-2], refs[-1]
    for d, offset in enumerate(offsets):
        placed_offsets[chip_at(d)] = offset[...]
    state = placed_offsets[0]
    for at in range(1, Y_SIZE):
        partial[at - 1] = state
        state = dot3(ordered[at], state) + placed_offsets[at]
    total[...] = state


def entering_kernel(entering, products, partial, *refs):
    outs, states = refs[:-1], refs[-1]
    states[0] = entering[...]
    for at in range(1, Y_SIZE):
        states[at] = dot3(products[at - 1], entering[...]) + partial[at - 1]
    for d, out in enumerate(outs):
        out[...] = states[chip_at(Y_SIZE - d)]


def core_kernel(own_transition, received_transition, own, received, *refs):
    arrived, kept, given, chip = refs[:Y_SIZE], refs[-3], refs[-2], refs[-1]
    size = arrived[0].shape[1]
    for d, part in enumerate(arrived):
        chip[:, lanes(chip_at(d), size)] = part[...]
    lower = by_core(own_transition[...], received_transition[...])
    into_second = dot3(lower, chip[...]) + by_core(own[...], received[...])
    kept[...] = by_core(chip[...], into_second)
    given[...] = by_core(into_second, chip[...])


def correct_kernel(tile, rows_hbm, response_hbm, kept, taken, out_hbm, rows, response, incoming_high, incoming_low, sems):
    count = rows.shape[0] // tile

    def span(index):
        return pl.ds(index * tile, tile)

    arrivals = [
        (
            pltpu.make_async_copy(response_hbm.at[span(k)], response.at[span(k)], sems.at[0, k]),
            pltpu.make_async_copy(rows_hbm.at[span(k)], rows.at[span(k)], sems.at[1, k]),
        )
        for k in range(count)
    ]
    for pair in arrivals:
        for copy in pair:
            copy.start()
    core = position()[0]
    for part, side in ((kept, core), (taken, 1 - core)):
        high, low = split(part[...])
        incoming_high[:, lanes(side, part.shape[1])] = high
        incoming_low[:, lanes(side, part.shape[1])] = low
    departures = []
    for k in range(count):
        for copy in arrivals[k]:
            copy.wait()
        high, low = split(response[k * tile : (k + 1) * tile])
        both = jnp.concatenate([high, low], axis=0)
        for start, size in chunks(rows.shape[1], 512):
            at = (slice(k * tile, (k + 1) * tile), slice(start, start + size))
            sums = dot(both, incoming_high[:, at[1]])
            rows[at] = rows[at] + (sums[:tile] + (sums[tile:] + dot(high, incoming_low[:, at[1]])))
        copy = pltpu.make_async_copy(rows.at[span(k)], out_hbm.at[span(k)], sems.at[2, k])
        copy.start()
        departures.append(copy)
    for copy in departures:
        copy.wait()


def correct(rows, response, kept, taken, tile=256):
    incoming = (response.shape[1], rows.shape[1])
    return pl.pallas_call(
        functools.partial(correct_kernel, tile),
        out_shape=jax.ShapeDtypeStruct(rows.shape, F32),
        in_specs=[ANY, ANY, VMEM, VMEM],
        out_specs=ANY,
        scratch_shapes=[
            pltpu.VMEM(rows.shape, F32),
            pltpu.VMEM(response.shape, F32),
            pltpu.VMEM(incoming, BF16),
            pltpu.VMEM(incoming, BF16),
            pltpu.SemaphoreType.DMA((3, rows.shape[0] // tile)),
        ],
        compiler_params=CORRECT_PARAMS,
    )(rows, response, kept, taken)


def local(eigvecs, wy_v, wy_t):
    width = wy_t.shape[-1]
    rows_dev, cols_dev = eigvecs.shape
    own_blocks = rows_dev // width
    below = lax.broadcasted_iota(jnp.int32, (width, width), 0) > lax.broadcasted_iota(
        jnp.int32, (width, width), 1
    )
    own = jnp.concatenate([jnp.where(below, wy_v[:, :, :width], wy_t), wy_v[:, :, width:]], axis=2)
    f00, s00 = own[0], own[1]
    depth = 2 * width
    shapes = ((own_blocks + 2, 2 * depth, depth), (own_blocks + 1, 2 * depth, depth))

    def add(buffers, first_pieces, second_pieces, keys):
        parts = []
        for group, pieces in enumerate((first_pieces, second_pieces)):
            for source, key in enumerate(keys):
                parts += placed(group * len(keys) + source, key, (group,), False)
        return build(buffers, shapes, first_pieces + second_pieces, parts)

    f01, f30, f10 = across_x(f00), along_z(f00, 1), along_z(f00, -1)
    s01, s30, s10 = across_x(s00), along_z(s00, 1), along_z(s00, -1)
    buffers = add(None, [f00], [s00], [(0, 0)])
    f01, f30, f10, *buffers = together(f01, f30, f10, *buffers)
    f31, f20, f11 = across_x(f30), along_z(f30, 1), along_z(f01, -1)
    s31, s20, s11 = across_x(s30), along_z(s30, 1), along_z(s01, -1)
    buffers = add(buffers, [f01, f30, f10], [s01, s30, s10], [(0, 1), (3, 0), (1, 0)])
    f31, f20, f11, s31, s20, s11, *buffers = together(f31, f20, f11, s31, s20, s11, *buffers)
    f21, s21 = along_z(f11, -1), along_z(s31, 1)
    picked, above = pick_first(
        eigvecs,
        {
            (0, 0): [f00, s00],
            (0, 1): [f01, s01],
            (1, 0): [f10, s10],
            (1, 1): [f11, s11],
            (3, 0): [f30, s30],
            (3, 1): [f31, s31],
            (2, 0): [f20, s20],
        }
    )
    vecs, rows = lax.axis_size("vec"), lax.axis_size("row")
    late = 5
    extras = [
        lax.ppermute(
            picked,
            ("row", "vec"),
            [((i + 1) * vecs + v, i * vecs + v) for i in range(rows - 1) for v in range(vecs) if v != late],
        ),
        lax.ppermute(
            picked, ("row", "vec"), [((i + 1) * vecs + late - 1, i * vecs + late) for i in range(rows - 1)]
        ),
    ]
    buffers = add(buffers, [f31, f20, f11], [s31, s20, s11], [(3, 1), (2, 0), (1, 1)])
    f21, s21, above, extra, late_extra, *buffers = together(f21, s21, above, *extras, *buffers)
    tail = from_next_row(above)
    buffers = build(
        buffers,
        shapes,
        [f21, s21, extra, late_extra],
        placed(0, (2, 1), (0,), False)
        + placed(1, (2, 1), (1,), False)
        + [((2, 3, late), [0, 1], 0, lambda vec: own_blocks), ((2, 3, late), [2], 1, lambda vec: own_blocks)],
    )

    half, quarter = cols_dev // 2, cols_dev // (2 * Y_SIZE)
    response, transition, initial = sweep_units(buffers, eigvecs)
    received_transition = across_core(transition)
    (chip_transition,) = small(chip_transition_kernel, [(depth, depth)], transition, received_transition)
    chip_transition, *buffers = together(chip_transition, *buffers)
    transitions = [chip_transition] + [along_y(chip_transition, d) for d in range(1, Y_SIZE)]
    swept, own_offset, sent_offset = sweep_data(buffers, eigvecs, tail, initial)
    sent_offset, *transitions = together(sent_offset, *transitions)
    received_offset = across_core(sent_offset)
    cores = (transition, received_transition, own_offset, received_offset)
    offsets = small(chip_offset_kernel, [(depth, quarter)] * Y_SIZE, *cores, scratch=[(depth, half)])
    offsets = [offsets[0]] + [along_y(offsets[d], d) for d in range(1, Y_SIZE)]
    ordered, products = small(
        products_kernel, [(Y_SIZE, depth, depth), (Y_SIZE - 1, depth, depth)], *transitions
    )
    partial, total = small(
        chain_kernel,
        [(Y_SIZE - 1, depth, quarter), (depth, quarter)],
        ordered,
        *offsets,
        scratch=[(Y_SIZE, depth, quarter)],
    )
    entering = lax.ppermute(total, "row", [(i, i + rows // 2) for i in range(rows // 2)])
    back = small(
        entering_kernel,
        [(depth, quarter)] * Y_SIZE,
        entering,
        products,
        partial,
        scratch=[(Y_SIZE, depth, quarter)],
    )
    arrived = [back[0]] + [along_y(back[d], d) for d in range(1, Y_SIZE)]
    kept, given = small(core_kernel, [(depth, half)] * 2, *cores, *arrived, scratch=[(depth, half)])
    return correct(swept, response, kept, across_core(given))


def solution(mesh):
    placed_in = (
        P("row", "vec"),
        P(None, ("row", "vec"), None, None),
        P(None, ("row", "vec"), None, None),
    )
    return jax.shard_map(
        local, mesh=mesh, in_specs=placed_in, out_specs=P("row", "vec"), check_vma=False
    )
```

```python
import functools

import jax
import jax.numpy as jnp
from jax import lax
from jax.experimental import pallas as pl
from jax.experimental.pallas import tpu as pltpu
from jax.sharding import PartitionSpec as P

F32 = jnp.float32
BF16 = jnp.bfloat16
Z_SIZE = 4
Y_SIZE = 4
VMEM_BYTES = 56 * 2**20


def dot(a, b, precision=None):
    return jnp.dot(a, b, precision=precision, preferred_element_type=F32)


def dot_transposed(a, b):
    return lax.dot_general(a, b, (((1,), (1,)), ((), ())), preferred_element_type=F32)


def split(value):
    high = value.astype(BF16)
    return high, (value - high.astype(F32)).astype(BF16)


def dot3(a, b):
    high, low = split(a)
    b_high, b_low = split(b)
    count = a.shape[0]
    both = dot(jnp.concatenate([high, low], axis=0), b_high)
    return both[:count] + (both[count:] + dot(high, b_low))


def along_z(value, by):
    pairs = [(v, ((v // 2 + by) % Z_SIZE) * 2 + v % 2) for v in range(2 * Z_SIZE)]
    return lax.ppermute(value, "vec", pairs)


def across_x(value):
    return lax.ppermute(value, "vec", [(v, v ^ 1) for v in range(2 * Z_SIZE)])


def across_core(value):
    return lax.ppermute(value, "row", [(i, i ^ 1) for i in range(lax.axis_size("row"))])


def along_y(value, by):
    def target(i):
        high, y, core = i // (2 * Y_SIZE), (i // 2) % Y_SIZE, i % 2
        return (high * Y_SIZE + (y + by) % Y_SIZE) * 2 + core

    return lax.ppermute(value, "row", [(i, target(i)) for i in range(lax.axis_size("row"))])


def from_next_row(value):
    return lax.ppermute(value, "row", [(i + 1, i) for i in range(lax.axis_size("row") - 1)])


def together(*values):
    return lax.optimization_barrier(values)


def place_of(index):
    vec = lax.axis_index("vec")
    z, x = vec // 2, vec % 2
    dz, dx = index // 2, index % 2
    return lax.rem(z + dz, Z_SIZE) * 2 + lax.rem(x + dx, 2)


def pick_kernel(sources, rows, *refs):
    pieces, out, above, sems = refs[:-3], refs[-3], refs[-2], refs[-1]
    head = pltpu.make_async_copy(rows.at[pl.ds(0, above.shape[0])], above, sems.at[2])
    head.start()
    for (dz, dx), (first, second) in sources:

        @pl.when(place_of(2 * dz + dx) == 0)
        def _():
            copies = [
                pltpu.make_async_copy(pieces[first], out.at[pl.ds(0, 2)], sems.at[0]),
                pltpu.make_async_copy(pieces[second].at[pl.ds(0, 1)], out.at[pl.ds(2, 1)], sems.at[1]),
            ]
            for copy in copies:
                copy.start()
            for copy in copies:
                copy.wait()

    head.wait()


def pick_first(rows, known):
    arrays, sources = [], []
    for key, held in known.items():
        sources.append((key, (len(arrays), len(arrays) + 1)))
        arrays += held
    depth, width = arrays[0].shape[-2:]
    return pl.pallas_call(
        functools.partial(pick_kernel, sources),
        out_shape=(
            jax.ShapeDtypeStruct((3, depth, width), F32),
            jax.ShapeDtypeStruct((depth, rows.shape[1]), F32),
        ),
        in_specs=[pl.BlockSpec(memory_space=pl.ANY)] * (1 + len(arrays)),
        out_specs=(pl.BlockSpec(memory_space=pltpu.VMEM),) * 2,
        scratch_shapes=[pltpu.SemaphoreType.DMA((3,))],
        compiler_params=pltpu.CompilerParams(vmem_limit_bytes=VMEM_BYTES),
    )(rows, *arrays)


def build_reflection(packed):
    width = packed.shape[1]
    rows = lax.broadcasted_iota(jnp.int32, (width, width), 0)
    cols = lax.broadcasted_iota(jnp.int32, (width, width), 1)
    top = packed[:width]
    unit = jnp.where(rows == cols, 1.0, jnp.where(rows > cols, top, 0.0))
    factor = jnp.where(rows <= cols, top, 0.0)
    vectors = jnp.concatenate([unit, packed[width:]], axis=0)
    high, low = split(vectors)
    factor_high, factor_low = split(factor)
    both = dot(jnp.concatenate([high, low], axis=0), factor_high)
    weighted_high, weighted_low = split(
        both[: 2 * width] + (both[2 * width :] + dot(high, factor_low))
    )
    both = dot_transposed(jnp.concatenate([weighted_high, weighted_low], axis=0), high)
    update = both[: 2 * width] + (both[2 * width :] + dot_transposed(weighted_high, low))
    rows = lax.broadcasted_iota(jnp.int32, update.shape, 0)
    cols = lax.broadcasted_iota(jnp.int32, update.shape, 1)
    return split(jnp.where(rows == cols, 1.0, 0.0) - update)


def build_kernel(parts, has_input, *refs):
    pieces = refs[: len(refs) - (6 if has_input else 4)]
    outs = refs[-4:-2]
    staged, sems = refs[-2], refs[-1]
    depth = staged.shape[2]
    copies = []
    at = 0
    for index, (source, blocks, group, place) in enumerate(parts):
        size = len(blocks)
        for block in blocks:
            if isinstance(source, tuple):
                usual, late, late_vec = source
                packed = jnp.where(lax.axis_index("vec") == late_vec, pieces[late][block], pieces[usual][block])
            else:
                packed = pieces[source][block]
            high, low = build_reflection(packed)
            staged[at, :depth] = high
            staged[at, depth:] = low
            at += 1
        first = place(lax.axis_index("vec"))
        copy = pltpu.make_async_copy(
            staged.at[pl.ds(at - size, size)], outs[group].at[pl.ds(first, size)], sems.at[index]
        )
        copy.start()
        copies.append(copy)
    for copy in copies:
        copy.wait()


def build(buffers, shapes, pieces, parts):
    depth = pieces[0].shape[-2]
    blocks = sum(len(part[1]) for part in parts)
    has_input = buffers is not None
    any_spec = pl.BlockSpec(memory_space=pl.ANY)
    return pl.pallas_call(
        functools.partial(build_kernel, parts, has_input),
        out_shape=tuple(jax.ShapeDtypeStruct(shape, BF16) for shape in shapes),
        in_specs=[pl.BlockSpec(memory_space=pltpu.VMEM)] * len(pieces) + ([any_spec] * 2 if has_input else []),
        out_specs=(any_spec, any_spec),
        scratch_shapes=[pltpu.VMEM((blocks, 2 * depth, depth), BF16), pltpu.SemaphoreType.DMA((len(parts),))],
        input_output_aliases={len(pieces): 0, len(pieces) + 1: 1} if has_input else {},
        compiler_params=pltpu.CompilerParams(vmem_limit_bytes=VMEM_BYTES),
        cost_estimate=pl.CostEstimate(
            flops=blocks * 300_000_000, bytes_accessed=blocks * depth * depth * 6, transcendentals=0
        ),
    )(*pieces, *(buffers if has_input else ()))


def placed(source, key, groups=(0, 1), whole=True):
    place = lambda vec: 2 * place_of(2 * key[0] + key[1])
    return [(source, [(group, 0), (group, 1)] if whole else [0, 1], group, place) for group in groups]


def apply(reflection, upper, lower):
    depth = reflection.shape[1]
    high, low = split(jnp.concatenate([upper, lower], axis=0))
    both = dot(reflection, high)
    result = both[:depth] + (both[depth:] + dot(reflection[:depth], low))
    return result[: depth // 2], result[depth // 2 :]


def chunks(total, size=256):
    return [(start, min(size, total - start)) for start in range(0, total, size)]


def first_step(reflection, state, lower, between):
    width, total = state.shape
    for start, size in chunks(total):
        cols = slice(start, start + size)
        below = jnp.zeros((width, size), F32) if lower is None else lower[:, cols]
        top, bottom = apply(reflection, state[:, cols], below)
        between[:, cols] = top
        state[:, cols] = bottom


def second_step(reflection, state, between, out):
    for start, size in chunks(state.shape[1]):
        cols = slice(start, start + size)
        top, bottom = apply(reflection, state[:, cols], between[:, cols])
        if out is not None:
            out[:, cols] = top
        state[:, cols] = bottom


def sweep_copies(first_hbm, second_hbm, data_hbm, tail_hbm, first, second, data, sems):
    granules = first.shape[0] // 2
    rows = 0 if data is None else data.shape[1]

    def first_copies(m):
        copies = [pltpu.make_async_copy(first_hbm.at[pl.ds(2 * m, 2)], first.at[pl.ds(2 * m, 2)], sems.at[0, m])]
        if data is not None:
            is_last = isinstance(m, int) and m == granules - 1
            source = tail_hbm if is_last else data_hbm.at[pl.ds(m * rows, rows)]
            copies.append(pltpu.make_async_copy(source, data.at[m], sems.at[1, m]))
        return copies

    def second_copies(m):
        size = 1 if isinstance(m, int) and 2 * m + 1 >= second.shape[0] else 2
        return [pltpu.make_async_copy(second_hbm.at[pl.ds(2 * m, size)], second.at[pl.ds(2 * m, size)], sems.at[2, m])]

    return first_copies, second_copies


def start_all(copies):
    for copy in copies:
        copy.start()


def wait_all(copies):
    for copy in copies:
        copy.wait()


def run_sweep(first, second, data, first_state, second_state, between, result, out, first_copies, second_copies, sems):
    width = first_state.shape[0]
    granules = first.shape[0] // 2
    blocks = second.shape[0] - 1

    def out_copy(block):
        return pltpu.make_async_copy(
            result.at[pl.ds(block * width, width)], out.at[pl.ds(block * width, width)], sems.at[3, block]
        )

    def rows_of(m, odd):
        return None if data is None else data.at[m, pl.ds(odd * width, width)]

    def finished(block):
        start = block * width
        return result.at[pl.ds(start if isinstance(start, int) else pl.multiple_of(start, width), width)]

    def both_steps(m, odd):
        index = 2 * m + odd - 2
        second_step(second[index], second_state, between, finished(index - 1))
        first_step(first[2 * m + odd], first_state, rows_of(m, odd), between)
        out_copy(index - 1).start()

    wait_all(first_copies(1))
    first_step(first[2], first_state, rows_of(1, 0), between)
    both_steps(1, 1)

    @pl.loop(2, granules - 1)
    def _(m):
        wait_all(first_copies(m))
        wait_all(second_copies(m - 1))
        both_steps(m, 0)
        both_steps(m, 1)

    last = granules - 1
    wait_all(first_copies(last))
    wait_all(second_copies(last - 1))
    both_steps(last, 0)
    both_steps(last, 1)
    wait_all(second_copies(last))
    second_step(second[blocks], second_state, between, finished(blocks - 1))
    out_copy(blocks - 1).start()
    for block in range(blocks):
        out_copy(block).wait()


def unit_kernel(
    first_hbm, second_hbm, data_hbm, out, transition, initial,
    first, second, data, first_state, second_state, between, data_between, result, sems,
):
    width = first_state.shape[0]
    first_copies, second_copies = sweep_copies(first_hbm, second_hbm, None, None, first, second, None, sems)
    granules = first.shape[0] // 2
    is_first = lax.axis_index("row") == 0

    @pl.when(is_first)
    def _():
        rows = pltpu.make_async_copy(data_hbm.at[pl.ds(0, 2 * width)], data, sems.at[1, 0])
        copies = first_copies(0) + second_copies(0) + [rows]
        start_all(copies)
        result[...] = jnp.zeros_like(result)
        transition[...] = jnp.zeros_like(transition)
        initial[...] = jnp.zeros_like(initial)
        cleared = pltpu.make_async_copy(result, out, sems.at[3, 0])
        cleared.start()
        wait_all(copies)
        upper, lower = initial.at[pl.ds(0, width)], initial.at[pl.ds(width, width)]
        first_step(first[0], upper, data.at[pl.ds(0, width)], data_between)
        first_step(first[1], upper, data.at[pl.ds(width, width)], data_between)
        second_step(second[0], lower, data_between, None)
        cleared.wait()

    @pl.when(jnp.logical_not(is_first))
    def _():
        for m in range(1, granules):
            start_all(first_copies(m) + second_copies(m - 1))
        start_all(second_copies(granules - 1))
        rows = lax.broadcasted_iota(jnp.int32, (width, width), 0)
        cols = lax.broadcasted_iota(jnp.int32, (width, width), 1)
        eye = jnp.where(rows == cols, 1.0, 0.0)
        zeros = jnp.zeros((width, width), F32)
        first_state[...] = eye
        second_state[...] = jnp.concatenate([zeros, eye], axis=1)
        between[...] = jnp.zeros_like(between)
        initial[...] = jnp.zeros_like(initial)
        wait_all(second_copies(0))
        run_sweep(
            first, second, None, first_state, second_state, between, result, out, first_copies, second_copies, sems
        )
        transition[:width] = jnp.concatenate([first_state[...], zeros], axis=1)
        transition[width:] = second_state[...]


def data_kernel(
    first_hbm, second_hbm, data_hbm, tail_hbm, initial, out, own_state, sent_state,
    first, second, data, first_state, second_state, between, result, sems,
):
    width = first_state.shape[0]
    first_copies, second_copies = sweep_copies(
        first_hbm, second_hbm, data_hbm, tail_hbm, first, second, data, sems
    )
    granules = first.shape[0] // 2
    for m in range(1, granules):
        start_all(first_copies(m) + second_copies(m - 1))
    start_all(second_copies(granules - 1))
    first_state[...] = initial[:width]
    second_state[...] = initial[width:]
    wait_all(second_copies(0))
    run_sweep(first, second, data, first_state, second_state, between, result, out, first_copies, second_copies, sems)
    half = own_state.shape[1]
    core = lax.rem(lax.axis_index("row"), 2)
    for target, side in ((own_state, core), (sent_state, 1 - core)):
        cols = pl.ds(pl.multiple_of(side * half, half), half)
        target[:width] = first_state[:, cols]
        target[width:] = second_state[:, cols]


ANY = pl.BlockSpec(memory_space=pl.ANY)
VMEM = pl.BlockSpec(memory_space=pltpu.VMEM)
PARAMS = pltpu.CompilerParams(vmem_limit_bytes=VMEM_BYTES)
CORRECT_PARAMS = pltpu.CompilerParams(vmem_limit_bytes=50 * 2**20)
SMALL_PARAMS = pltpu.CompilerParams(vmem_limit_bytes=16 * 2**20)


def estimate(blocks, depth, cols):
    return pl.CostEstimate(
        flops=6 * blocks * depth * depth * cols, bytes_accessed=30 * 2**20, transcendentals=0
    )


def sweep_units(buffers, data):
    first, second = buffers
    depth = first.shape[2]
    width, blocks, cols = depth // 2, second.shape[0] - 1, data.shape[1]
    return pl.pallas_call(
        unit_kernel,
        out_shape=(
            jax.ShapeDtypeStruct((blocks * width, depth), F32),
            jax.ShapeDtypeStruct((depth, depth), F32),
            jax.ShapeDtypeStruct((depth, cols), F32),
        ),
        in_specs=[ANY] * 3,
        out_specs=(ANY, VMEM, VMEM),
        scratch_shapes=[
            pltpu.VMEM(first.shape, BF16),
            pltpu.VMEM(second.shape, BF16),
            pltpu.VMEM((depth, cols), F32),
            pltpu.VMEM((width, width), F32),
            pltpu.VMEM((width, depth), F32),
            pltpu.VMEM((width, depth), F32),
            pltpu.VMEM((width, cols), F32),
            pltpu.VMEM((blocks * width, depth), F32),
            pltpu.SemaphoreType.DMA((4, blocks)),
        ],
        compiler_params=pltpu.CompilerParams(vmem_limit_bytes=50 * 2**20),
        cost_estimate=estimate(blocks, depth, 3 * depth),
    )(first, second, data)


def sweep_data(buffers, data, tail, initial):
    first, second = buffers
    depth = first.shape[2]
    width, blocks, cols = depth // 2, second.shape[0] - 1, data.shape[1]
    return pl.pallas_call(
        data_kernel,
        out_shape=(
            jax.ShapeDtypeStruct((blocks * width, cols), F32),
            jax.ShapeDtypeStruct((depth, cols // 2), F32),
            jax.ShapeDtypeStruct((depth, cols // 2), F32),
        ),
        in_specs=[ANY] * 4 + [VMEM],
        out_specs=(ANY, VMEM, VMEM),
        scratch_shapes=[
            pltpu.VMEM(first.shape, BF16),
            pltpu.VMEM(second.shape, BF16),
            pltpu.VMEM((first.shape[0] // 2, depth, cols), F32),
            pltpu.VMEM((width, cols), F32),
            pltpu.VMEM((width, cols), F32),
            pltpu.VMEM((width, cols), F32),
            pltpu.VMEM((blocks * width, cols), F32),
            pltpu.SemaphoreType.DMA((4, blocks)),
        ],
        compiler_params=pltpu.CompilerParams(vmem_limit_bytes=46 * 2**20),
        cost_estimate=estimate(blocks, depth, 2 * cols),
    )(first, second, data, tail, initial)


def small(kernel, outs, *args, scratch=()):
    return pl.pallas_call(
        kernel,
        out_shape=tuple(jax.ShapeDtypeStruct(shape, F32) for shape in outs),
        in_specs=[VMEM] * len(args),
        out_specs=tuple(VMEM for _ in outs),
        scratch_shapes=[pltpu.VMEM(shape, F32) for shape in scratch],
        compiler_params=SMALL_PARAMS,
    )(*args)


def position():
    row = lax.axis_index("row")
    return lax.rem(row, 2), lax.rem(row // 2, Y_SIZE)


def chip_at(d):
    return lax.rem(position()[1] + Y_SIZE - d, Y_SIZE)


def lanes(index, size):
    return pl.ds(pl.multiple_of(index * size, size), size)


def by_core(at_first, otherwise):
    return jnp.where(position()[0] == 0, at_first, otherwise)


def chip_transition_kernel(own, received, out):
    out[...] = dot3(by_core(received[...], own[...]), by_core(own[...], received[...]))


def chip_offset_kernel(own_transition, received_transition, own, received, *refs):
    outs, chip = refs[:-1], refs[-1]
    upper = by_core(received_transition[...], own_transition[...])
    chip[...] = dot3(upper, by_core(own[...], received[...])) + by_core(received[...], own[...])
    size = outs[0].shape[1]
    for d, out in enumerate(outs):
        out[...] = chip[:, lanes(chip_at(Y_SIZE - d), size)]


def products_kernel(*refs):
    transitions, ordered, products = refs[:Y_SIZE], refs[Y_SIZE], refs[Y_SIZE + 1]
    for d, transition in enumerate(transitions):
        ordered[chip_at(d)] = transition[...]
    product = ordered[0]
    products[0] = product
    for at in range(1, Y_SIZE - 1):
        product = dot3(ordered[at], product)
        products[at] = product


def chain_kernel(ordered, *refs):
    offsets, partial, total, placed_offsets = refs[:Y_SIZE], refs[-3], refs[-2], refs[-1]
    for d, offset in enumerate(offsets):
        placed_offsets[chip_at(d)] = offset[...]
    state = placed_offsets[0]
    for at in range(1, Y_SIZE):
        partial[at - 1] = state
        state = dot3(ordered[at], state) + placed_offsets[at]
    total[...] = state


def entering_kernel(entering, products, partial, *refs):
    outs, states = refs[:-1], refs[-1]
    states[0] = entering[...]
    for at in range(1, Y_SIZE):
        states[at] = dot3(products[at - 1], entering[...]) + partial[at - 1]
    for d, out in enumerate(outs):
        out[...] = states[chip_at(Y_SIZE - d)]


def core_kernel(own_transition, received_transition, own, received, *refs):
    arrived, kept, given, chip = refs[:Y_SIZE], refs[-3], refs[-2], refs[-1]
    size = arrived[0].shape[1]
    for d, part in enumerate(arrived):
        chip[:, lanes(chip_at(d), size)] = part[...]
    lower = by_core(own_transition[...], received_transition[...])
    into_second = dot3(lower, chip[...]) + by_core(own[...], received[...])
    kept[...] = by_core(chip[...], into_second)
    given[...] = by_core(into_second, chip[...])


def correct_kernel(tile, rows_hbm, response_hbm, kept, taken, out_hbm, rows, response, incoming_high, incoming_low, sems):
    count = rows.shape[0] // tile

    def span(index):
        return pl.ds(index * tile, tile)

    arrivals = [
        (
            pltpu.make_async_copy(response_hbm.at[span(k)], response.at[span(k)], sems.at[0, k]),
            pltpu.make_async_copy(rows_hbm.at[span(k)], rows.at[span(k)], sems.at[1, k]),
        )
        for k in range(count)
    ]
    for pair in arrivals:
        for copy in pair:
            copy.start()
    core = position()[0]
    for part, side in ((kept, core), (taken, 1 - core)):
        high, low = split(part[...])
        incoming_high[:, lanes(side, part.shape[1])] = high
        incoming_low[:, lanes(side, part.shape[1])] = low
    departures = []
    for k in range(count):
        for copy in arrivals[k]:
            copy.wait()
        high, low = split(response[k * tile : (k + 1) * tile])
        both = jnp.concatenate([high, low], axis=0)
        for start, size in chunks(rows.shape[1], 512):
            at = (slice(k * tile, (k + 1) * tile), slice(start, start + size))
            sums = dot(both, incoming_high[:, at[1]])
            rows[at] = rows[at] + (sums[:tile] + (sums[tile:] + dot(high, incoming_low[:, at[1]])))
        copy = pltpu.make_async_copy(rows.at[span(k)], out_hbm.at[span(k)], sems.at[2, k])
        copy.start()
        departures.append(copy)
    for copy in departures:
        copy.wait()


def correct(rows, response, kept, taken, tile=256):
    incoming = (response.shape[1], rows.shape[1])
    return pl.pallas_call(
        functools.partial(correct_kernel, tile),
        out_shape=jax.ShapeDtypeStruct(rows.shape, F32),
        in_specs=[ANY, ANY, VMEM, VMEM],
        out_specs=ANY,
        scratch_shapes=[
            pltpu.VMEM(rows.shape, F32),
            pltpu.VMEM(response.shape, F32),
            pltpu.VMEM(incoming, BF16),
            pltpu.VMEM(incoming, BF16),
            pltpu.SemaphoreType.DMA((3, rows.shape[0] // tile)),
        ],
        compiler_params=CORRECT_PARAMS,
    )(rows, response, kept, taken)


def local(eigvecs, wy_v, wy_t):
    width = wy_t.shape[-1]
    rows_dev, cols_dev = eigvecs.shape
    own_blocks = rows_dev // width
    below = lax.broadcasted_iota(jnp.int32, (width, width), 0) > lax.broadcasted_iota(
        jnp.int32, (width, width), 1
    )
    own = jnp.concatenate([jnp.where(below, wy_v[:, :, :width], wy_t), wy_v[:, :, width:]], axis=2)
    f00, s00 = own[0], own[1]
    depth = 2 * width
    shapes = ((own_blocks + 2, 2 * depth, depth), (own_blocks + 1, 2 * depth, depth))

    def add(buffers, first_pieces, second_pieces, keys):
        parts = []
        for group, pieces in enumerate((first_pieces, second_pieces)):
            for source, key in enumerate(keys):
                parts += placed(group * len(keys) + source, key, (group,), False)
        return build(buffers, shapes, first_pieces + second_pieces, parts)

    f01, f30, f10 = across_x(f00), along_z(f00, 1), along_z(f00, -1)
    s01, s30, s10 = across_x(s00), along_z(s00, 1), along_z(s00, -1)
    buffers = add(None, [f00], [s00], [(0, 0)])
    f01, f30, f10, *buffers = together(f01, f30, f10, *buffers)
    f31, f20, f11 = across_x(f30), along_z(f30, 1), along_z(f01, -1)
    s31, s20, s11 = across_x(s30), along_z(s30, 1), along_z(s01, -1)
    buffers = add(buffers, [f01, f30, f10], [s01, s30, s10], [(0, 1), (3, 0), (1, 0)])
    f21 = along_z(f11, -1)
    f31, f20, f11, f21, s31, s20, s11, *buffers = together(f31, f20, f11, f21, s31, s20, s11, *buffers)
    s21 = along_z(s31, 1)
    picked, above = pick_first(
        eigvecs,
        {
            (0, 0): [f00, s00],
            (0, 1): [f01, s01],
            (1, 0): [f10, s10],
            (1, 1): [f11, s11],
            (3, 0): [f30, s30],
            (3, 1): [f31, s31],
            (2, 0): [f20, s20],
        }
    )
    vecs, rows = lax.axis_size("vec"), lax.axis_size("row")
    late = 5
    extras = [
        lax.ppermute(
            picked,
            ("row", "vec"),
            [((i + 1) * vecs + v, i * vecs + v) for i in range(rows - 1) for v in range(vecs) if v != late],
        ),
        lax.ppermute(
            picked, ("row", "vec"), [((i + 1) * vecs + late - 1, i * vecs + late) for i in range(rows - 1)]
        ),
    ]
    buffers = add(buffers, [f31, f20, f11], [s31, s20, s11], [(3, 1), (2, 0), (1, 1)])
    f21, s21, extra, late_extra, *buffers = together(f21, s21, *extras, *buffers)
    tail = from_next_row(above)
    buffers = build(
        buffers,
        shapes,
        [f21, s21, extra, late_extra],
        placed(0, (2, 1), (0,), False)
        + placed(1, (2, 1), (1,), False)
        + [((2, 3, late), [0, 1], 0, lambda vec: own_blocks), ((2, 3, late), [2], 1, lambda vec: own_blocks)],
    )

    half, quarter = cols_dev // 2, cols_dev // (2 * Y_SIZE)
    response, transition, initial = sweep_units(buffers, eigvecs)
    received_transition = across_core(transition)
    (chip_transition,) = small(chip_transition_kernel, [(depth, depth)], transition, received_transition)
    chip_transition, *buffers = together(chip_transition, *buffers)
    transitions = [chip_transition] + [along_y(chip_transition, d) for d in range(1, Y_SIZE)]
    swept, own_offset, sent_offset = sweep_data(buffers, eigvecs, tail, initial)
    sent_offset, *transitions = together(sent_offset, *transitions)
    received_offset = across_core(sent_offset)
    cores = (transition, received_transition, own_offset, received_offset)
    offsets = small(chip_offset_kernel, [(depth, quarter)] * Y_SIZE, *cores, scratch=[(depth, half)])
    offsets = [offsets[0]] + [along_y(offsets[d], d) for d in range(1, Y_SIZE)]
    ordered, products = small(
        products_kernel, [(Y_SIZE, depth, depth), (Y_SIZE - 1, depth, depth)], *transitions
    )
    partial, total = small(
        chain_kernel,
        [(Y_SIZE - 1, depth, quarter), (depth, quarter)],
        ordered,
        *offsets,
        scratch=[(Y_SIZE, depth, quarter)],
    )
    entering = lax.ppermute(total, "row", [(i, i + rows // 2) for i in range(rows // 2)])
    back = small(
        entering_kernel,
        [(depth, quarter)] * Y_SIZE,
        entering,
        products,
        partial,
        scratch=[(Y_SIZE, depth, quarter)],
    )
    arrived = [back[0]] + [along_y(back[d], d) for d in range(1, Y_SIZE)]
    kept, given = small(core_kernel, [(depth, half)] * 2, *cores, *arrived, scratch=[(depth, half)])
    return correct(swept, response, kept, across_core(given))


def solution(mesh):
    placed_in = (
        P("row", "vec"),
        P(None, ("row", "vec"), None, None),
        P(None, ("row", "vec"), None, None),
    )
    return jax.shard_map(
        local, mesh=mesh, in_specs=placed_in, out_specs=P("row", "vec"), check_vma=False
    )
```

```python
import functools

import jax
import jax.numpy as jnp
from jax import lax
from jax.experimental import pallas as pl
from jax.experimental.pallas import tpu as pltpu
from jax.sharding import PartitionSpec as P

F32 = jnp.float32
BF16 = jnp.bfloat16
Z_SIZE = 4
Y_SIZE = 4
VMEM_BYTES = 56 * 2**20


def dot(a, b, precision=None):
    return jnp.dot(a, b, precision=precision, preferred_element_type=F32)


def dot_transposed(a, b):
    return lax.dot_general(a, b, (((1,), (1,)), ((), ())), preferred_element_type=F32)


def split(value):
    high = value.astype(BF16)
    return high, (value - high.astype(F32)).astype(BF16)


def dot3(a, b):
    high, low = split(a)
    b_high, b_low = split(b)
    count = a.shape[0]
    both = dot(jnp.concatenate([high, low], axis=0), b_high)
    return both[:count] + (both[count:] + dot(high, b_low))


def along_z(value, by):
    pairs = [(v, ((v // 2 + by) % Z_SIZE) * 2 + v % 2) for v in range(2 * Z_SIZE)]
    return lax.ppermute(value, "vec", pairs)


def across_x(value):
    return lax.ppermute(value, "vec", [(v, v ^ 1) for v in range(2 * Z_SIZE)])


def across_core(value):
    return lax.ppermute(value, "row", [(i, i ^ 1) for i in range(lax.axis_size("row"))])


def along_y(value, by):
    def target(i):
        high, y, core = i // (2 * Y_SIZE), (i // 2) % Y_SIZE, i % 2
        return (high * Y_SIZE + (y + by) % Y_SIZE) * 2 + core

    return lax.ppermute(value, "row", [(i, target(i)) for i in range(lax.axis_size("row"))])


def from_next_row(value):
    return lax.ppermute(value, "row", [(i + 1, i) for i in range(lax.axis_size("row") - 1)])


def together(*values):
    return lax.optimization_barrier(values)


def place_of(index):
    vec = lax.axis_index("vec")
    z, x = vec // 2, vec % 2
    dz, dx = index // 2, index % 2
    return lax.rem(z + dz, Z_SIZE) * 2 + lax.rem(x + dx, 2)


def pick_kernel(sources, rows, *refs):
    pieces, out, above, sems = refs[:-3], refs[-3], refs[-2], refs[-1]
    head = pltpu.make_async_copy(rows.at[pl.ds(0, above.shape[0])], above, sems.at[2])
    head.start()
    for (dz, dx), (first, second) in sources:

        @pl.when(place_of(2 * dz + dx) == 0)
        def _():
            copies = [
                pltpu.make_async_copy(pieces[first], out.at[pl.ds(0, 2)], sems.at[0]),
                pltpu.make_async_copy(pieces[second].at[pl.ds(0, 1)], out.at[pl.ds(2, 1)], sems.at[1]),
            ]
            for copy in copies:
                copy.start()
            for copy in copies:
                copy.wait()

    head.wait()


def pick_first(rows, known):
    arrays, sources = [], []
    for key, held in known.items():
        sources.append((key, (len(arrays), len(arrays) + 1)))
        arrays += held
    depth, width = arrays[0].shape[-2:]
    return pl.pallas_call(
        functools.partial(pick_kernel, sources),
        out_shape=(
            jax.ShapeDtypeStruct((3, depth, width), F32),
            jax.ShapeDtypeStruct((depth, rows.shape[1]), F32),
        ),
        in_specs=[pl.BlockSpec(memory_space=pl.ANY)] * (1 + len(arrays)),
        out_specs=(pl.BlockSpec(memory_space=pltpu.VMEM),) * 2,
        scratch_shapes=[pltpu.SemaphoreType.DMA((3,))],
        compiler_params=pltpu.CompilerParams(vmem_limit_bytes=VMEM_BYTES),
    )(rows, *arrays)


def build_reflection(packed):
    width = packed.shape[1]
    rows = lax.broadcasted_iota(jnp.int32, (width, width), 0)
    cols = lax.broadcasted_iota(jnp.int32, (width, width), 1)
    top = packed[:width]
    unit = jnp.where(rows == cols, 1.0, jnp.where(rows > cols, top, 0.0))
    factor = jnp.where(rows <= cols, top, 0.0)
    vectors = jnp.concatenate([unit, packed[width:]], axis=0)
    high, low = split(vectors)
    factor_high, factor_low = split(factor)
    both = dot(jnp.concatenate([high, low], axis=0), factor_high)
    weighted_high, weighted_low = split(
        both[: 2 * width] + (both[2 * width :] + dot(high, factor_low))
    )
    both = dot_transposed(jnp.concatenate([weighted_high, weighted_low], axis=0), high)
    update = both[: 2 * width] + (both[2 * width :] + dot_transposed(weighted_high, low))
    rows = lax.broadcasted_iota(jnp.int32, update.shape, 0)
    cols = lax.broadcasted_iota(jnp.int32, update.shape, 1)
    return split(jnp.where(rows == cols, 1.0, 0.0) - update)


def build_kernel(parts, has_input, *refs):
    pieces = refs[: len(refs) - (6 if has_input else 4)]
    outs = refs[-4:-2]
    staged, sems = refs[-2], refs[-1]
    depth = staged.shape[2]
    copies = []
    at = 0
    for index, (source, blocks, group, place) in enumerate(parts):
        size = len(blocks)
        for block in blocks:
            if isinstance(source, tuple):
                usual, late, late_vec = source
                packed = jnp.where(lax.axis_index("vec") == late_vec, pieces[late][block], pieces[usual][block])
            else:
                packed = pieces[source][block]
            high, low = build_reflection(packed)
            staged[at, :depth] = high
            staged[at, depth:] = low
            at += 1
        first = place(lax.axis_index("vec"))
        copy = pltpu.make_async_copy(
            staged.at[pl.ds(at - size, size)], outs[group].at[pl.ds(first, size)], sems.at[index]
        )
        copy.start()
        copies.append(copy)
    for copy in copies:
        copy.wait()


def build(buffers, shapes, pieces, parts):
    depth = pieces[0].shape[-2]
    blocks = sum(len(part[1]) for part in parts)
    has_input = buffers is not None
    any_spec = pl.BlockSpec(memory_space=pl.ANY)
    return pl.pallas_call(
        functools.partial(build_kernel, parts, has_input),
        out_shape=tuple(jax.ShapeDtypeStruct(shape, BF16) for shape in shapes),
        in_specs=[pl.BlockSpec(memory_space=pltpu.VMEM)] * len(pieces) + ([any_spec] * 2 if has_input else []),
        out_specs=(any_spec, any_spec),
        scratch_shapes=[pltpu.VMEM((blocks, 2 * depth, depth), BF16), pltpu.SemaphoreType.DMA((len(parts),))],
        input_output_aliases={len(pieces): 0, len(pieces) + 1: 1} if has_input else {},
        compiler_params=pltpu.CompilerParams(vmem_limit_bytes=VMEM_BYTES),
        cost_estimate=pl.CostEstimate(
            flops=blocks * 300_000_000, bytes_accessed=blocks * depth * depth * 6, transcendentals=0
        ),
    )(*pieces, *(buffers if has_input else ()))


def placed(source, key, groups=(0, 1), whole=True):
    place = lambda vec: 2 * place_of(2 * key[0] + key[1])
    return [(source, [(group, 0), (group, 1)] if whole else [0, 1], group, place) for group in groups]


def apply(reflection, upper, lower):
    depth = reflection.shape[1]
    high, low = split(jnp.concatenate([upper, lower], axis=0))
    both = dot(reflection, high)
    result = both[:depth] + (both[depth:] + dot(reflection[:depth], low))
    return result[: depth // 2], result[depth // 2 :]


def chunks(total, size=256):
    return [(start, min(size, total - start)) for start in range(0, total, size)]


def first_step(reflection, state, lower, between):
    width, total = state.shape
    for start, size in chunks(total):
        cols = slice(start, start + size)
        below = jnp.zeros((width, size), F32) if lower is None else lower[:, cols]
        top, bottom = apply(reflection, state[:, cols], below)
        between[:, cols] = top
        state[:, cols] = bottom


def second_step(reflection, state, between, out):
    for start, size in chunks(state.shape[1]):
        cols = slice(start, start + size)
        top, bottom = apply(reflection, state[:, cols], between[:, cols])
        if out is not None:
            out[:, cols] = top
        state[:, cols] = bottom


def sweep_copies(first_hbm, second_hbm, data_hbm, tail_hbm, first, second, data, sems):
    granules = first.shape[0] // 2
    rows = 0 if data is None else data.shape[1]

    def first_copies(m):
        copies = [pltpu.make_async_copy(first_hbm.at[pl.ds(2 * m, 2)], first.at[pl.ds(2 * m, 2)], sems.at[0, m])]
        if data is not None:
            is_last = isinstance(m, int) and m == granules - 1
            source = tail_hbm if is_last else data_hbm.at[pl.ds(m * rows, rows)]
            copies.append(pltpu.make_async_copy(source, data.at[m], sems.at[1, m]))
        return copies

    def second_copies(m):
        size = 1 if isinstance(m, int) and 2 * m + 1 >= second.shape[0] else 2
        return [pltpu.make_async_copy(second_hbm.at[pl.ds(2 * m, size)], second.at[pl.ds(2 * m, size)], sems.at[2, m])]

    return first_copies, second_copies


def start_all(copies):
    for copy in copies:
        copy.start()


def wait_all(copies):
    for copy in copies:
        copy.wait()


def run_sweep(first, second, data, first_state, second_state, between, result, out, first_copies, second_copies, sems):
    width = first_state.shape[0]
    granules = first.shape[0] // 2
    blocks = second.shape[0] - 1

    def out_copy(block):
        return pltpu.make_async_copy(
            result.at[pl.ds(block * width, width)], out.at[pl.ds(block * width, width)], sems.at[3, block]
        )

    def rows_of(m, odd):
        return None if data is None else data.at[m, pl.ds(odd * width, width)]

    def finished(block):
        start = block * width
        return result.at[pl.ds(start if isinstance(start, int) else pl.multiple_of(start, width), width)]

    def both_steps(m, odd):
        index = 2 * m + odd - 2
        second_step(second[index], second_state, between, finished(index - 1))
        first_step(first[2 * m + odd], first_state, rows_of(m, odd), between)
        out_copy(index - 1).start()

    wait_all(first_copies(1))
    first_step(first[2], first_state, rows_of(1, 0), between)
    both_steps(1, 1)

    @pl.loop(2, granules - 1)
    def _(m):
        wait_all(first_copies(m))
        wait_all(second_copies(m - 1))
        both_steps(m, 0)
        both_steps(m, 1)

    last = granules - 1
    wait_all(first_copies(last))
    wait_all(second_copies(last - 1))
    both_steps(last, 0)
    both_steps(last, 1)
    wait_all(second_copies(last))
    second_step(second[blocks], second_state, between, finished(blocks - 1))
    out_copy(blocks - 1).start()
    for block in range(blocks):
        out_copy(block).wait()


def unit_kernel(
    first_hbm, second_hbm, data_hbm, out, transition, initial,
    first, second, data, first_state, second_state, between, data_between, result, sems,
):
    width = first_state.shape[0]
    first_copies, second_copies = sweep_copies(first_hbm, second_hbm, None, None, first, second, None, sems)
    granules = first.shape[0] // 2
    is_first = lax.axis_index("row") == 0

    @pl.when(is_first)
    def _():
        rows = pltpu.make_async_copy(data_hbm.at[pl.ds(0, 2 * width)], data, sems.at[1, 0])
        copies = first_copies(0) + second_copies(0) + [rows]
        start_all(copies)
        result[...] = jnp.zeros_like(result)
        transition[...] = jnp.zeros_like(transition)
        initial[...] = jnp.zeros_like(initial)
        cleared = pltpu.make_async_copy(result, out, sems.at[3, 0])
        cleared.start()
        wait_all(copies)
        upper, lower = initial.at[pl.ds(0, width)], initial.at[pl.ds(width, width)]
        first_step(first[0], upper, data.at[pl.ds(0, width)], data_between)
        first_step(first[1], upper, data.at[pl.ds(width, width)], data_between)
        second_step(second[0], lower, data_between, None)
        cleared.wait()

    @pl.when(jnp.logical_not(is_first))
    def _():
        for m in range(1, granules):
            start_all(first_copies(m) + second_copies(m - 1))
        start_all(second_copies(granules - 1))
        rows = lax.broadcasted_iota(jnp.int32, (width, width), 0)
        cols = lax.broadcasted_iota(jnp.int32, (width, width), 1)
        eye = jnp.where(rows == cols, 1.0, 0.0)
        zeros = jnp.zeros((width, width), F32)
        first_state[...] = eye
        second_state[...] = jnp.concatenate([zeros, eye], axis=1)
        between[...] = jnp.zeros_like(between)
        initial[...] = jnp.zeros_like(initial)
        wait_all(second_copies(0))
        run_sweep(
            first, second, None, first_state, second_state, between, result, out, first_copies, second_copies, sems
        )
        transition[:width] = jnp.concatenate([first_state[...], zeros], axis=1)
        transition[width:] = second_state[...]


def data_kernel(
    first_hbm, second_hbm, data_hbm, tail_hbm, initial, out, own_state, sent_state,
    first, second, data, first_state, second_state, between, result, sems,
):
    width = first_state.shape[0]
    first_copies, second_copies = sweep_copies(
        first_hbm, second_hbm, data_hbm, tail_hbm, first, second, data, sems
    )
    granules = first.shape[0] // 2
    for m in range(1, granules):
        start_all(first_copies(m) + second_copies(m - 1))
    start_all(second_copies(granules - 1))
    first_state[...] = initial[:width]
    second_state[...] = initial[width:]
    wait_all(second_copies(0))
    run_sweep(first, second, data, first_state, second_state, between, result, out, first_copies, second_copies, sems)
    half = own_state.shape[1]
    core = lax.rem(lax.axis_index("row"), 2)
    for target, side in ((own_state, core), (sent_state, 1 - core)):
        cols = pl.ds(pl.multiple_of(side * half, half), half)
        target[:width] = first_state[:, cols]
        target[width:] = second_state[:, cols]


ANY = pl.BlockSpec(memory_space=pl.ANY)
VMEM = pl.BlockSpec(memory_space=pltpu.VMEM)
PARAMS = pltpu.CompilerParams(vmem_limit_bytes=VMEM_BYTES)
CORRECT_PARAMS = pltpu.CompilerParams(vmem_limit_bytes=50 * 2**20)
SMALL_PARAMS = pltpu.CompilerParams(vmem_limit_bytes=16 * 2**20)


def estimate(blocks, depth, cols):
    return pl.CostEstimate(
        flops=6 * blocks * depth * depth * cols, bytes_accessed=30 * 2**20, transcendentals=0
    )


def sweep_units(buffers, data):
    first, second = buffers
    depth = first.shape[2]
    width, blocks, cols = depth // 2, second.shape[0] - 1, data.shape[1]
    return pl.pallas_call(
        unit_kernel,
        out_shape=(
            jax.ShapeDtypeStruct((blocks * width, depth), F32),
            jax.ShapeDtypeStruct((depth, depth), F32),
            jax.ShapeDtypeStruct((depth, cols), F32),
        ),
        in_specs=[ANY] * 3,
        out_specs=(ANY, VMEM, VMEM),
        scratch_shapes=[
            pltpu.VMEM(first.shape, BF16),
            pltpu.VMEM(second.shape, BF16),
            pltpu.VMEM((depth, cols), F32),
            pltpu.VMEM((width, width), F32),
            pltpu.VMEM((width, depth), F32),
            pltpu.VMEM((width, depth), F32),
            pltpu.VMEM((width, cols), F32),
            pltpu.VMEM((blocks * width, depth), F32),
            pltpu.SemaphoreType.DMA((4, blocks)),
        ],
        compiler_params=pltpu.CompilerParams(vmem_limit_bytes=50 * 2**20),
        cost_estimate=estimate(blocks, depth, 3 * depth),
    )(first, second, data)


def sweep_data(buffers, data, tail, initial):
    first, second = buffers
    depth = first.shape[2]
    width, blocks, cols = depth // 2, second.shape[0] - 1, data.shape[1]
    return pl.pallas_call(
        data_kernel,
        out_shape=(
            jax.ShapeDtypeStruct((blocks * width, cols), F32),
            jax.ShapeDtypeStruct((depth, cols // 2), F32),
            jax.ShapeDtypeStruct((depth, cols // 2), F32),
        ),
        in_specs=[ANY] * 4 + [VMEM],
        out_specs=(ANY, VMEM, VMEM),
        scratch_shapes=[
            pltpu.VMEM(first.shape, BF16),
            pltpu.VMEM(second.shape, BF16),
            pltpu.VMEM((first.shape[0] // 2, depth, cols), F32),
            pltpu.VMEM((width, cols), F32),
            pltpu.VMEM((width, cols), F32),
            pltpu.VMEM((width, cols), F32),
            pltpu.VMEM((blocks * width, cols), F32),
            pltpu.SemaphoreType.DMA((4, blocks)),
        ],
        compiler_params=pltpu.CompilerParams(vmem_limit_bytes=46 * 2**20),
        cost_estimate=estimate(blocks, depth, 2 * cols),
    )(first, second, data, tail, initial)


def small(kernel, outs, *args, scratch=()):
    return pl.pallas_call(
        kernel,
        out_shape=tuple(jax.ShapeDtypeStruct(shape, F32) for shape in outs),
        in_specs=[VMEM] * len(args),
        out_specs=tuple(VMEM for _ in outs),
        scratch_shapes=[pltpu.VMEM(shape, F32) for shape in scratch],
        compiler_params=SMALL_PARAMS,
    )(*args)


def position():
    row = lax.axis_index("row")
    return lax.rem(row, 2), lax.rem(row // 2, Y_SIZE)


def chip_at(d):
    return lax.rem(position()[1] + Y_SIZE - d, Y_SIZE)


def lanes(index, size):
    return pl.ds(pl.multiple_of(index * size, size), size)


def by_core(at_first, otherwise):
    return jnp.where(position()[0] == 0, at_first, otherwise)


def chip_transition_kernel(own, received, out):
    out[...] = dot3(by_core(received[...], own[...]), by_core(own[...], received[...]))


def chip_offset_kernel(own_transition, received_transition, own, received, *refs):
    outs, chip = refs[:-1], refs[-1]
    upper = by_core(received_transition[...], own_transition[...])
    chip[...] = dot3(upper, by_core(own[...], received[...])) + by_core(received[...], own[...])
    size = outs[0].shape[1]
    for d, out in enumerate(outs):
        out[...] = chip[:, lanes(chip_at(Y_SIZE - d), size)]


def products_kernel(*refs):
    transitions, ordered, products = refs[:Y_SIZE], refs[Y_SIZE], refs[Y_SIZE + 1]
    for d, transition in enumerate(transitions):
        ordered[chip_at(d)] = transition[...]
    product = ordered[0]
    products[0] = product
    for at in range(1, Y_SIZE - 1):
        product = dot3(ordered[at], product)
        products[at] = product


def chain_kernel(ordered, *refs):
    offsets, partial, total, placed_offsets = refs[:Y_SIZE], refs[-3], refs[-2], refs[-1]
    for d, offset in enumerate(offsets):
        placed_offsets[chip_at(d)] = offset[...]
    state = placed_offsets[0]
    for at in range(1, Y_SIZE):
        partial[at - 1] = state
        state = dot3(ordered[at], state) + placed_offsets[at]
    total[...] = state


def entering_kernel(entering, products, partial, *refs):
    outs, states = refs[:-1], refs[-1]
    states[0] = entering[...]
    for at in range(1, Y_SIZE):
        states[at] = dot3(products[at - 1], entering[...]) + partial[at - 1]
    for d, out in enumerate(outs):
        out[...] = states[chip_at(Y_SIZE - d)]


def core_kernel(own_transition, received_transition, own, received, *refs):
    arrived, kept, given, chip = refs[:Y_SIZE], refs[-3], refs[-2], refs[-1]
    size = arrived[0].shape[1]
    for d, part in enumerate(arrived):
        chip[:, lanes(chip_at(d), size)] = part[...]
    lower = by_core(own_transition[...], received_transition[...])
    into_second = dot3(lower, chip[...]) + by_core(own[...], received[...])
    kept[...] = by_core(chip[...], into_second)
    given[...] = by_core(into_second, chip[...])


def correct_kernel(tile, rows_hbm, response_hbm, kept, taken, out_hbm, rows, response, incoming_high, incoming_low, sems):
    count = rows.shape[0] // tile

    def span(index):
        return pl.ds(index * tile, tile)

    arrivals = [
        (
            pltpu.make_async_copy(response_hbm.at[span(k)], response.at[span(k)], sems.at[0, k]),
            pltpu.make_async_copy(rows_hbm.at[span(k)], rows.at[span(k)], sems.at[1, k]),
        )
        for k in range(count)
    ]
    for pair in arrivals:
        for copy in pair:
            copy.start()
    core = position()[0]
    for part, side in ((kept, core), (taken, 1 - core)):
        high, low = split(part[...])
        incoming_high[:, lanes(side, part.shape[1])] = high
        incoming_low[:, lanes(side, part.shape[1])] = low
    departures = []
    for k in range(count):
        for copy in arrivals[k]:
            copy.wait()
        high, low = split(response[k * tile : (k + 1) * tile])
        both = jnp.concatenate([high, low], axis=0)
        for start, size in chunks(rows.shape[1], 512):
            at = (slice(k * tile, (k + 1) * tile), slice(start, start + size))
            sums = dot(both, incoming_high[:, at[1]])
            rows[at] = rows[at] + (sums[:tile] + (sums[tile:] + dot(high, incoming_low[:, at[1]])))
        copy = pltpu.make_async_copy(rows.at[span(k)], out_hbm.at[span(k)], sems.at[2, k])
        copy.start()
        departures.append(copy)
    for copy in departures:
        copy.wait()


def correct(rows, response, kept, taken, tile=256):
    incoming = (response.shape[1], rows.shape[1])
    return pl.pallas_call(
        functools.partial(correct_kernel, tile),
        out_shape=jax.ShapeDtypeStruct(rows.shape, F32),
        in_specs=[ANY, ANY, VMEM, VMEM],
        out_specs=ANY,
        scratch_shapes=[
            pltpu.VMEM(rows.shape, F32),
            pltpu.VMEM(response.shape, F32),
            pltpu.VMEM(incoming, BF16),
            pltpu.VMEM(incoming, BF16),
            pltpu.SemaphoreType.DMA((3, rows.shape[0] // tile)),
        ],
        compiler_params=CORRECT_PARAMS,
    )(rows, response, kept, taken)


def local(eigvecs, wy_v, wy_t):
    width = wy_t.shape[-1]
    rows_dev, cols_dev = eigvecs.shape
    own_blocks = rows_dev // width
    below = lax.broadcasted_iota(jnp.int32, (width, width), 0) > lax.broadcasted_iota(
        jnp.int32, (width, width), 1
    )
    own = jnp.concatenate([jnp.where(below, wy_v[:, :, :width], wy_t), wy_v[:, :, width:]], axis=2)
    f00, s00 = own[0], own[1]
    depth = 2 * width
    shapes = ((own_blocks + 2, 2 * depth, depth), (own_blocks + 1, 2 * depth, depth))

    def add(buffers, first_pieces, second_pieces, keys):
        parts = []
        for group, pieces in enumerate((first_pieces, second_pieces)):
            for source, key in enumerate(keys):
                parts += placed(group * len(keys) + source, key, (group,), False)
        return build(buffers, shapes, first_pieces + second_pieces, parts)

    f01, f30, f10 = across_x(f00), along_z(f00, 1), along_z(f00, -1)
    s01, s30, s10 = across_x(s00), along_z(s00, 1), along_z(s00, -1)
    buffers = add(None, [f00], [s00], [(0, 0)])
    f01, f30, f10, *buffers = together(f01, f30, f10, *buffers)
    f31, f20, f11 = across_x(f30), along_z(f30, 1), along_z(f01, -1)
    s31, s20, s11 = across_x(s30), along_z(s30, 1), along_z(s01, -1)
    buffers = add(buffers, [f01, f30, f10], [s01, s30, s10], [(0, 1), (3, 0), (1, 0)])
    f31, f20, f11, s31, s20, s11, *buffers = together(f31, f20, f11, s31, s20, s11, *buffers)
    f21, s21 = along_z(f11, -1), along_z(s31, 1)
    picked, above = pick_first(
        eigvecs,
        {
            (0, 0): [f00, s00],
            (0, 1): [f01, s01],
            (1, 0): [f10, s10],
            (1, 1): [f11, s11],
            (3, 0): [f30, s30],
            (3, 1): [f31, s31],
            (2, 0): [f20, s20],
        }
    )
    vecs, rows = lax.axis_size("vec"), lax.axis_size("row")
    late = 5
    extras = [
        lax.ppermute(
            picked,
            ("row", "vec"),
            [((i + 1) * vecs + v, i * vecs + v) for i in range(rows - 1) for v in range(vecs) if v != late],
        ),
        lax.ppermute(
            picked, ("row", "vec"), [((i + 1) * vecs + late - 1, i * vecs + late) for i in range(rows - 1)]
        ),
    ]
    buffers = add(buffers, [f31, f20, f11], [s31, s20, s11], [(3, 1), (2, 0), (1, 1)])
    f21, s21, extra, late_extra, *buffers = together(f21, s21, *extras, *buffers)
    tail = from_next_row(above)
    buffers = build(
        buffers,
        shapes,
        [f21, s21, extra, late_extra],
        placed(0, (2, 1), (0,), False)
        + placed(1, (2, 1), (1,), False)
        + [((2, 3, late), [0, 1], 0, lambda vec: own_blocks), ((2, 3, late), [2], 1, lambda vec: own_blocks)],
    )

    half, quarter = cols_dev // 2, cols_dev // (2 * Y_SIZE)
    response, transition, initial = sweep_units(buffers, eigvecs)
    received_transition = across_core(transition)
    (chip_transition,) = small(chip_transition_kernel, [(depth, depth)], transition, received_transition)
    chip_transition, *buffers = together(chip_transition, *buffers)
    transitions = [chip_transition] + [along_y(chip_transition, d) for d in range(1, Y_SIZE)]
    swept, own_offset, sent_offset = sweep_data(buffers, eigvecs, tail, initial)
    sent_offset, *transitions = together(sent_offset, *transitions)
    received_offset = across_core(sent_offset)
    cores = (transition, received_transition, own_offset, received_offset)
    offsets = small(chip_offset_kernel, [(depth, quarter)] * Y_SIZE, *cores, scratch=[(depth, half)])
    offsets = [offsets[0]] + [along_y(offsets[d], d) for d in range(1, Y_SIZE)]
    ordered, products = small(
        products_kernel, [(Y_SIZE, depth, depth), (Y_SIZE - 1, depth, depth)], *transitions
    )
    partial, total = small(
        chain_kernel,
        [(Y_SIZE - 1, depth, quarter), (depth, quarter)],
        ordered,
        *offsets,
        scratch=[(Y_SIZE, depth, quarter)],
    )
    entering = lax.ppermute(total, "row", [(i, i + rows // 2) for i in range(rows // 2)])
    back = small(
        entering_kernel,
        [(depth, quarter)] * Y_SIZE,
        entering,
        products,
        partial,
        scratch=[(Y_SIZE, depth, quarter)],
    )
    arrived = [back[0]] + [along_y(back[d], d) for d in range(1, Y_SIZE)]
    kept, given = small(core_kernel, [(depth, half)] * 2, *cores, *arrived, scratch=[(depth, half)])
    return correct(swept, response, kept, across_core(given))


def solution(mesh):
    placed_in = (
        P("row", "vec"),
        P(None, ("row", "vec"), None, None),
        P(None, ("row", "vec"), None, None),
    )
    return jax.shard_map(
        local, mesh=mesh, in_specs=placed_in, out_specs=P("row", "vec"), check_vma=False
    )
```
